32 devices in a mesh: pipe: 2 (over core), ctx: 4 (over y, x), fsdp: 4 (over z).
Axes of the slice: x: 2, y: 2, z: 4, core: 2. Of those that a mesh axis runs over, the one named last changes fastest.
Arguments:
- tokens: bfloat16 [2, 4, 1024, 960], P(None, 'fsdp', 'ctx'), may hold values from -6 to 6
- cotangent: bfloat16 [2, 4, 1024, 960], P(None, 'fsdp', 'ctx'), may hold values from -6 to 6
- doc_ids: int32 [2, 4, 1024], P(None, 'fsdp'), may hold values from 0 to 8, as said below
- w_query: bfloat16 [2, 960, 960], P('pipe', 'fsdp'), may hold values from -0.1875 to 0.1875
- w_keyval: bfloat16 [2, 960, 640], P('pipe', 'fsdp'), may hold values from -0.1875 to 0.1875
- w_out: bfloat16 [2, 960, 960], P('pipe', 'fsdp'), may hold values from -0.75 to 0.75
- w_gateup: bfloat16 [2, 960, 5120], P('pipe', 'fsdp'), may hold values from -0.1875 to 0.1875
- w_down: bfloat16 [2, 2560, 960], P('pipe', 'fsdp'), may hold values from -0.25 to 0.25
- gain_attn: float32 [2, 960], P('pipe'), may hold values from 0.5 to 1.5
- gain_ffn: float32 [2, 960], P('pipe'), may hold values from 0.5 to 1.5
Outputs:
- section_out: bfloat16 [2, 2, 4, 1024, 960], P('pipe', None, 'fsdp', 'ctx')
- section_in_grad: bfloat16 [2, 2, 4, 1024, 960], P('pipe', None, 'fsdp', 'ctx')
- grad_query: float32 [2, 960, 960], P('pipe', ('ctx', 'fsdp'))
- grad_keyval: float32 [2, 960, 640], P('pipe', ('ctx', 'fsdp'))
- grad_out: float32 [2, 960, 960], P('pipe', ('ctx', 'fsdp'))
- grad_gateup: float32 [2, 960, 5120], P('pipe', ('ctx', 'fsdp'))
- grad_down: float32 [2, 2560, 960], P('pipe', ('ctx', 'fsdp'))
- grad_gain_attn: float32 [2, 960], P('pipe')
- grad_gain_ffn: float32 [2, 960], P('pipe')
The draws below stay inside these ranges and needn't reach their ends.
Inputs may be any that keep to these rules, and one draw needn't show every extreme that they name: doc_ids never falls along a row and is 0 at the first position and 8 at the last; documents have any length from 1 position to most of a row, and their number may differ from row to row. For each of the 4 rows, in one micro-batch drawn from the seed, some document begins within the first 128 positions and ends within the last 128 positions of the row.
All inputs are finite; a program needn't handle non-finite values.
Results may differ from the reference program's by a relative error of at most 0.023.
Values may be sent and summed in bfloat16 or wider, within the bound.
No kernel may reach another device: no remote copies, remote signals or barrier semaphores. Data moves between devices by JAX's collectives and lax.ppermute only.
A program may use at most 256 MiB of HBM per device.

```python
import math
import jax
import jax.numpy as jnp
from jax import lax

D = 960
HEADS = 15
KV_HEADS = 5
HEAD = 64
FF = 2560
TOK_MB = 256
MICRO = 2
ROWS = 4
SEQ = 1024
KVD = 320
N_PIPE = 2


def draw_doc_ids(key, part):
    key = jax.random.fold_in(key, 7)
    keys = jax.random.split(key, 5)
    cut_count = 8
    cuts = jax.random.randint(keys[0], (MICRO, ROWS, cut_count), 1, SEQ)
    active = jax.random.randint(keys[1], (MICRO, ROWS, cut_count), 0, 2)
    cuts = jnp.where(active == 1, cuts, SEQ - 1)
    begin = jax.random.randint(keys[2], (1, ROWS, 1), 1, TOK_MB // 2 + 1)
    finish = jax.random.randint(keys[3], (1, ROWS, 1), SEQ - TOK_MB // 2, SEQ)
    span_micro = jax.random.randint(keys[4], (1, ROWS, 1), 0, MICRO)
    squeezed = jnp.where(cuts < SEQ // 2, jnp.minimum(cuts, begin), jnp.maximum(cuts, finish))
    slot = jnp.arange(cut_count, dtype=jnp.int32)[None, None, :]
    squeezed = jnp.where(slot == 0, begin, jnp.where(slot == 1, finish, squeezed))
    is_span = jnp.arange(MICRO, dtype=jnp.int32)[:, None, None] == span_micro
    cuts = jnp.where(is_span, squeezed, cuts)
    index = jnp.arange(SEQ, dtype=jnp.int32)[None, None, :, None]
    return jnp.sum((index >= cuts[:, :, None, :]).astype(jnp.int32), axis=-1)


def levels(stream_key, shape, shards, smallest, high):
    def one(position, parts):
        heights = jax.random.uniform(jax.random.fold_in(jax.random.fold_in(stream_key, 6), position), (parts,), jnp.float32, smallest / len(shards), high / len(shards))
        return jnp.repeat(jnp.exp(heights), shape[position] // parts).reshape((-1,) + (1,) * (len(shape) - position - 1))

    level = one(*shards[0])
    for cut in shards[1:]:
        level = level * one(*cut)
    return level


def noise(rng, shape, scale, bound, cuts=(), kind=jnp.bfloat16):
    factor_of = levels(rng, shape, cuts, -0.22, 0.18) if cuts else 1.0
    values = jax.random.normal(rng, shape, jnp.float32) * scale * factor_of
    return jnp.minimum(jnp.maximum(values, -bound), bound).astype(kind)


def setup_inputs(seed: int = 0) -> dict:
    arg_keys = jax.random.split(jax.random.key(seed), 11)
    tokens = noise(arg_keys[0], (MICRO, ROWS, SEQ, D), 1.0, 6.0, ((1, 4), (2, 4)))
    cotangent = noise(arg_keys[1], (MICRO, ROWS, SEQ, D), 1.0, 6.0, ((1, 4), (2, 4)))
    doc_ids = draw_doc_ids(jax.random.fold_in(arg_keys[10], 71), 0)
    w_query = noise(arg_keys[3], (N_PIPE, D, D), D ** -0.5, 0.1875, ((0, 2), (1, 4)))
    w_keyval = noise(arg_keys[4], (N_PIPE, D, 2 * KVD), D ** -0.5, 0.1875, ((0, 2), (1, 4)))
    w_out = noise(arg_keys[5], (N_PIPE, D, D), (D // 16) ** -0.5, 0.75, ((0, 2), (1, 4)))
    w_gateup = noise(arg_keys[6], (N_PIPE, D, 2 * FF), D ** -0.5, 0.1875, ((0, 2), (1, 4)))
    w_down = noise(arg_keys[7], (N_PIPE, FF, D), (FF // 4) ** -0.5, 0.25, ((0, 2), (1, 4)))
    gain_attn = jnp.clip(1.0 + 0.1 * jax.random.normal(arg_keys[8], (N_PIPE, D), jnp.float32), 0.5, 1.5)
    gain_ffn = jnp.clip(1.0 + 0.1 * jax.random.normal(arg_keys[9], (N_PIPE, D), jnp.float32), 0.5, 1.5)
    return dict(tokens=tokens, cotangent=cotangent, doc_ids=doc_ids, w_query=w_query, w_keyval=w_keyval, w_out=w_out, w_gateup=w_gateup, w_down=w_down, gain_attn=gain_attn, gain_ffn=gain_ffn)


EPSILON = 1e-05
NEGATIVE = -1e+30
HIGHEST = lax.Precision.HIGHEST

@jax.custom_vjp
def low(v):
    return lax.optimization_barrier(v.astype(jnp.bfloat16)).astype(jnp.float32)

@jax.custom_vjp
def low_back(v):
    return v

def low_keep(v):
    return (low(v), None)

def low_pass(kept, grad):
    return (grad,)

def back_keep(v):
    return (v, None)

def back_low(kept, grad):
    return (low(grad),)
low.defvjp(low_keep, low_pass)
low_back.defvjp(back_keep, back_low)

def normalize(values, gain):
    return values * lax.rsqrt(lax.optimization_barrier(jnp.mean(values * values, axis=-1, keepdims=True)) + EPSILON) * gain

def angle_tables(token_pos, head_size):
    half_size = head_size // 2
    freqs = jnp.exp(jnp.arange(half_size, dtype=jnp.float32) * (-2.0 * math.log(100000.0) / head_size))
    angles = token_pos[:, None] * freqs[None, :]
    cosine = jnp.concatenate([jnp.cos(angles), jnp.cos(angles)], axis=-1)[:, None, :]
    sine_table = jnp.concatenate([jnp.sin(angles), jnp.sin(angles)], axis=-1)[:, None, :]
    return (cosine, sine_table)

def half_turn(values):
    half_size = values.shape[-1] // 2
    return jnp.concatenate([-values[..., half_size:], values[..., :half_size]], axis=-1)

def rotate_pairs(values, cosine, sine_table):
    return values * cosine + half_turn(values) * sine_table

def segment_positions(doc_row):
    length = doc_row.shape[0]
    earlier = lax.optimization_barrier(jnp.sum((doc_row[None, :] < doc_row[:, None]).astype(jnp.int32), axis=1))
    return jnp.arange(length, dtype=jnp.int32) - earlier

def layer_row(params, inputs, doc_row):
    w_query, w_keyval, w_out, w_gateup, w_down, gain_attn, gain_ffn = params
    length = inputs.shape[0]
    width = inputs.shape[1]
    kv_width = w_keyval.shape[1] // 2
    scale_factor = 1.0 / math.sqrt(HEAD)
    normed = low(normalize(inputs, gain_attn))
    projected = low_back(jnp.dot(normed, jnp.concatenate([w_query, w_keyval], axis=1), precision=HIGHEST))
    token_pos = segment_positions(doc_row)
    cosine, sine_table = angle_tables(token_pos.astype(jnp.float32), HEAD)
    queries = low(rotate_pairs(projected[:, :width].reshape(length, HEADS, HEAD), cosine, sine_table))
    keys_all = low(rotate_pairs(projected[:, width:width + kv_width].reshape(length, KV_HEADS, HEAD), cosine, sine_table))
    values_all = low(projected[:, width + kv_width:].reshape(length, KV_HEADS, HEAD))
    grouped = queries.reshape(length, KV_HEADS, HEADS // KV_HEADS, HEAD)
    scores = low_back(jnp.einsum('rhgd,shd->hgrs', grouped, keys_all, precision=HIGHEST) * scale_factor)
    index = jnp.arange(length, dtype=jnp.int32)
    key_mask = (doc_row[:, None] == doc_row[None, :]) & (index[None, :] <= index[:, None])
    scores = jnp.where(key_mask, scores, NEGATIVE)
    probs = low(jax.nn.softmax(scores, axis=-1))
    attended = jnp.einsum('hgrs,shd->rhgd', probs, values_all, precision=HIGHEST).reshape(length, width)
    attended = low(low_back(attended))
    resid = inputs + low_back(jnp.dot(attended, w_out, precision=HIGHEST))
    normed_ffn = low(normalize(resid, gain_ffn))
    gated = low_back(jnp.dot(normed_ffn, w_gateup, precision=HIGHEST))
    hidden = low(jax.nn.silu(gated[:, :FF]) * gated[:, FF:])
    return resid + low_back(jnp.dot(hidden, w_down, precision=HIGHEST))

def layer_all(params, inputs, doc_rows):

    def one_row(pair):
        return layer_row(params, pair[0], pair[1])
    return lax.map(jax.checkpoint(one_row), (inputs, doc_rows))

def reference(tokens, cotangent, doc_ids, w_query, w_keyval, w_out, w_gateup, w_down, gain_attn, gain_ffn):
    row_total = MICRO * ROWS
    doc_rows = doc_ids.reshape(row_total, SEQ)
    weights_all = (w_query, w_keyval, w_out, w_gateup, w_down, gain_attn, gain_ffn)

    def layer_params(layer):
        return tuple((weight[layer].astype(jnp.float32) for weight in weights_all))

    def run_layer(params, inputs):
        return layer_all(params, inputs, doc_rows)
    first_in = tokens.astype(jnp.float32).reshape(row_total, SEQ, D)
    first_out, first_pull = jax.vjp(run_layer, layer_params(0), first_in)
    middle = first_out.astype(jnp.bfloat16)
    second_out, second_pull = jax.vjp(run_layer, layer_params(1), middle.astype(jnp.float32))
    second_grads, middle_grad = second_pull(cotangent.astype(jnp.float32).reshape(row_total, SEQ, D))
    middle_low = middle_grad.astype(jnp.bfloat16)
    first_grads, input_grad = first_pull(middle_low.astype(jnp.float32))
    out_shape = (MICRO, ROWS, SEQ, D)
    section_out = jnp.stack([middle.reshape(out_shape), second_out.astype(jnp.bfloat16).reshape(out_shape)])
    section_in_grad = jnp.stack([input_grad.astype(jnp.bfloat16).reshape(out_shape), middle_low.reshape(out_shape)])
    stacked = [jnp.stack([first_grads[index], second_grads[index]]) for index in range(7)]
    return (section_out, section_in_grad, stacked[0], stacked[1], stacked[2], stacked[3], stacked[4], stacked[5], stacked[6])
```

```python
import functools
import math

import jax
import jax.numpy as jnp
from jax import lax
from jax.experimental import pallas as pl
from jax.experimental.pallas import tpu as pltpu
from jax.sharding import PartitionSpec as P

HEADS = 15
KV_HEADS = 5
HEAD = 64
GROUPS = HEADS // KV_HEADS
EPSILON = 1e-05
NEGATIVE = -1e30
SCALE = 1.0 / math.sqrt(HEAD)
F32 = jnp.float32
BF16 = jnp.bfloat16


def swap_cores(array):
    return lax.ppermute(array, "pipe", [(0, 1), (1, 0)])


def one_way(array, source, target):
    return lax.ppermute(array, "pipe", [(source, target)])


def across(array, axis, mask):
    count = lax.axis_size(axis)
    return lax.ppermute(array, axis, [(i, i ^ mask) for i in range(count)])


def pick(flag, first, second):
    return jnp.where(flag, first, second)


def tie(array, other):
    return lax.optimization_barrier((array, other))[0]


class Order:
    def __init__(self):
        self.last = None

    def hold(self, *arrays):
        if self.last is not None:
            *arrays, _ = lax.optimization_barrier((*arrays, self.last))
        return arrays[0] if len(arrays) == 1 else tuple(arrays)

    def wait(self, array):
        array = self.hold(array)
        self.last = array
        return array


def first_way(array):
    pairs = [(c, c ^ 1) for c in range(4)] + [(4 + c, 4 + (c ^ 2)) for c in range(4)]
    return lax.ppermute(array, ("pipe", "ctx"), pairs)


def second_way(array):
    pairs = [(c, c ^ 2) for c in range(4)] + [(4 + c, 4 + (c ^ 1)) for c in range(4)]
    return lax.ppermute(array, ("pipe", "ctx"), pairs)


def dot(left, right):
    return jnp.dot(left, right, preferred_element_type=F32)


def dot_back(left, right):
    return lax.dot_general(left, right, (((1,), (1,)), ((), ())), preferred_element_type=F32)


def dot_rows(left, right):
    return lax.dot_general(left, right, (((0,), (0,)), ((), ())), preferred_element_type=F32)


def normalize(values, gain):
    return values * lax.rsqrt(jnp.mean(values * values, axis=-1, keepdims=True) + EPSILON) * gain


def normalize_back(values, gain, grad):
    inverse = lax.rsqrt(jnp.mean(values * values, axis=-1, keepdims=True) + EPSILON)
    unit = values * inverse
    gain_grad = jnp.sum(grad * unit, axis=0)
    scaled = grad * gain
    return inverse * (scaled - unit * jnp.mean(scaled * unit, axis=-1, keepdims=True)), gain_grad


def angle_tables(token_pos):
    half_size = HEAD // 2
    freqs = jnp.exp(jnp.arange(half_size, dtype=F32) * (-2.0 * math.log(100000.0) / HEAD))
    angles = freqs[:, None] * token_pos[None, :]
    cosine, sine = jnp.cos(angles), jnp.sin(angles)
    return jnp.concatenate([cosine, cosine], axis=0), jnp.concatenate([sine, sine], axis=0)


def rotate(values, tables):
    rows, cols = values.shape
    heads = values.reshape(rows // HEAD, HEAD, cols)
    half = HEAD // 2
    turned = jnp.concatenate([-heads[:, half:], heads[:, :half]], axis=1)
    return (heads * tables[0] + turned * tables[1]).reshape(rows, cols)


def rotate_back(values, tables):
    rows, cols = values.shape
    heads = values.reshape(rows // HEAD, HEAD, cols)
    half = HEAD // 2
    scaled = heads * tables[1]
    turned = jnp.concatenate([scaled[:, half:], -scaled[:, :half]], axis=1)
    return (heads * tables[0] + turned).reshape(rows, cols)


def z_masks():
    count = lax.axis_size("fsdp")
    masks = []
    while count > 1:
        count //= 2
        masks.append(count)
    return masks


class Spread:
    def __init__(self, order, own):
        self.order = order
        self.held = own[None]
        self.rank = [0]
        self.step = 0
        masks = z_masks()
        for mask in masks[:-2]:
            self.join(across(self.held, "fsdp", mask), mask)
        self.masks = masks[-2:]
        self.start()

    def join(self, got, mask):
        self.held = jnp.concatenate([self.held, got], axis=0)
        self.rank = self.rank + [place ^ mask for place in self.rank]

    def start(self):
        held = self.order.hold(self.held)
        if self.step < 2:
            self.flight = across(held, "fsdp", self.masks[self.step])
        elif self.step == 2:
            self.flight = first_way(held)
            self.side = second_way(held)
            self.parts = [(held, swap_cores(held))]
        else:
            self.flight = second_way(held)

    def arrive(self):
        got = self.order.wait(self.flight)
        self.step += 1
        if self.step < 3:
            self.join(got, self.masks[self.step - 1])
            return
        self.parts.append((got, swap_cores(got)))
        if self.step == 3:
            self.held = got
        else:
            side = self.order.wait(self.side)
            self.parts.insert(2, (side, swap_cores(side)))

    def advance(self):
        self.arrive()
        if self.step < 4:
            self.start()

    def split(self, count):
        parts = []
        for held in (self.held[:, :count], self.held[:, count:]):
            part = Spread.__new__(Spread)
            part.order, part.held, part.rank = self.order, held, self.rank
            part.step, part.masks = 2, self.masks
            parts.append(part)
        return parts


    def copies(self, refs, out):
        depth, groups, _, cols = self.parts[0][0].shape
        core, ctx = lax.axis_index("pipe"), lax.axis_index("ctx")
        zed, ccount = lax.axis_index("fsdp"), lax.axis_size("ctx")
        for number in range(8):
            half = core if number < 4 else 1 - core
            mask = 0
            if number % 2 == 1:
                mask = mask ^ (1 + half)
            if number % 4 >= 2:
                mask = mask ^ (2 - half)
            for slot in range(depth):
                for group in range(groups):
                    col = pl.multiple_of((group * ccount + (ctx ^ mask)) * cols, cols)
                    yield (
                        refs[number].at[slot, group],
                        out.at[zed ^ self.rank[slot], half, :, pl.ds(col, cols)],
                    )

    def arrays(self):
        return [part[side] for side in range(2) for part in self.parts]

    def shape(self):
        _, groups, rows, cols = self.parts[0][0].shape
        return (lax.axis_size("fsdp"), 2, rows, groups * lax.axis_size("ctx") * cols)


class Along(Spread):
    def advance(self):
        got = self.order.wait(self.flight)
        self.step += 1
        if self.step == 1:
            self.join(got, self.masks[0])
            self.start()
            self.parts = [(self.held, swap_cores(self.held))]
        else:
            self.parts.append((got, swap_cores(got)))
            self.rank = self.rank + [place ^ self.masks[1] for place in self.rank]

    def copies(self, refs, out):
        core, zed = lax.axis_index("pipe"), lax.axis_index("fsdp")
        depth = self.parts[0][0].shape[0]
        for number in range(4):
            half = core if number < 2 else 1 - core
            for slot in range(depth):
                rank = self.rank[(number % 2) * depth + slot]
                yield refs[number].at[slot], out.at[zed ^ rank, half]

    def shape(self):
        return (lax.axis_size("fsdp"), 2, *self.parts[0][0].shape[1:])


def place(*groups):
    arrays = [group.arrays() for group in groups]
    starts = [sum(len(a) for a in arrays[:n]) for n in range(len(groups) + 1)]
    shapes = [group.shape() for group in groups]
    count = sum(
        len(a) * a[0].shape[0] * (a[0].shape[1] if a[0].ndim == 4 else 1) for a in arrays
    )

    def body(*refs):
        sems = refs[-1]
        copies = []
        for number, group in enumerate(groups):
            ins = refs[starts[number] : starts[number + 1]]
            for source, target in group.copies(ins, refs[starts[-1] + number]):
                copies.append(pltpu.make_async_copy(source, target, sems.at[len(copies)]))
        for copy in copies:
            copy.start()
        for copy in copies:
            copy.wait()

    outs = pl.pallas_call(
        body,
        out_shape=[jax.ShapeDtypeStruct(shape, BF16) for shape in shapes],
        in_specs=[pl.BlockSpec(memory_space=pl.ANY)] * starts[-1],
        out_specs=[pl.BlockSpec(memory_space=pltpu.VMEM)] * len(groups),
        scratch_shapes=[pltpu.SemaphoreType.DMA((count,))],
        compiler_params=pltpu.CompilerParams(vmem_limit_bytes=40 * 1024 * 1024),
        cost_estimate=pl.CostEstimate(
            flops=0, bytes_accessed=sum(4 * math.prod(s) for s in shapes), transcendentals=0
        ),
    )(*[array for group in arrays for array in group])
    return [out.reshape(-1, out.shape[-1]) for out in outs]


def own_pieces(w_query, w_keyval, w_out, w_gateup, w_down, core, ctx):
    attn = jnp.concatenate([w_keyval, w_query, w_out], axis=1)
    rows = attn.shape[0] // 2
    cols = attn.shape[1] // 4
    ffn = w_gateup.shape[1] // 2
    depth = w_down.shape[0] // 2

    def parts(half):
        attn_piece = lax.dynamic_slice(attn, (half * rows, ctx * cols), (rows, cols))[None]
        gate = lax.dynamic_slice(w_gateup, (half * rows, ctx * cols), (rows, cols))
        up = lax.dynamic_slice(w_gateup, (half * rows, ffn + ctx * cols), (rows, cols))
        down = lax.dynamic_slice_in_dim(w_down, half * depth, depth, 0)
        return (attn_piece, jnp.stack([gate, up]), down)

    kept = parts(core)
    received = [swap_cores(piece) for piece in parts(1 - core)]
    first = [pick(core == 0, a, b) for a, b in zip(kept, received)]
    second = [pick(core == 0, b, a) for a, b in zip(kept, received)]
    return first, second


def add_low(kept, received):
    return (kept.astype(F32) + received.astype(F32)).astype(BF16)


class Reduce:
    def __init__(self, order, term, offload=False):
        self.order = order
        self.offload = offload
        zcount = lax.axis_size("fsdp")
        core, ctx, self.zed = lax.axis_index("pipe"), lax.axis_index("ctx"), lax.axis_index("fsdp")
        rows, cols = term.shape
        self.deep = rows // 4
        y, x = ctx // 2, ctx % 2
        view = term.reshape(4, self.deep, cols)
        index = lax.dynamic_index_in_dim

        def blocks(bit):
            first = pick(core == 0, bit(x), 2 * bit(y))
            stride = pick(core == 0, 2, 1)
            return jnp.stack(
                [index(view, first, 0, False), index(view, first + stride, 0, False)]
            )

        self.kept = blocks(lambda own: own)
        self.side = pick(core == 0, y, x)
        self.step = 0
        self.result = None
        self.flights = [first_way(order.hold(blocks(lambda own: 1 - own)))]

    def land(self):
        total = self.kept.astype(F32)
        for flight in self.flights:
            total = total + self.order.wait(flight).astype(F32)
        return total

    def advance(self):
        if self.result is not None:
            return
        total = self.land()
        self.step += 1
        if self.step == 3:
            self.result = total
            return
        low = total.astype(BF16)
        index = lax.dynamic_index_in_dim
        if self.step == 1:
            self.kept = index(low, self.side, 0, False)
            self.flights = [second_way(self.order.hold(index(low, 1 - self.side, 0, False)))]
            return
        if self.offload:
            count = lax.axis_size("fsdp")
            parts = self.order.hold(low).reshape(count, low.shape[0] // count, low.shape[1])
            self.result = lax.psum_scatter(parts, "fsdp", scatter_dimension=0, tiled=False)
            return
        for mask in z_masks()[:-2]:
            half = low.shape[0] // 2
            high = (self.zed & mask) != 0
            self.kept = pick(high, low[half:], low[:half])
            self.flights = [across(pick(high, low[:half], low[half:]), "fsdp", mask)]
            low = self.land().astype(BF16)
        parts = low.reshape(4, low.shape[0] // 4, low.shape[1])
        here = self.zed % 4
        self.kept = index(parts, here, 0, False)
        sent = [index(parts, here ^ mask, 0, False) for mask in (3, 2, 1)]
        sent = self.order.hold(*sent)
        self.flights = [
            across(block, "fsdp", mask) for block, mask in zip(sent, (3, 2, 1))
        ]

    def settle(self):
        self.result = self.order.wait(self.result)


def send_keys(keyval):
    flows = []
    for mask in (3, 1, 2):
        pairs = [(i, i ^ mask) for i in range(4) if i < i ^ mask]
        flows.append(lax.ppermute(keyval, "ctx", pairs))
    return flows[1], flows[2], flows[0]


def return_keys(parts):
    flows = []
    for mask in (3, 1, 2):
        pairs = [(i, i ^ mask) for i in range(4) if i > i ^ mask]
        flows.append(lax.ppermute(parts[mask].astype(BF16), "ctx", pairs))
    return flows


def project(inputs_low, w_attn, gain_attn, tables):
    width = inputs_low.shape[1]
    kv_width = (w_attn.shape[1] - 2 * width) // 2
    inputs = inputs_low.astype(F32)
    normed = normalize(inputs, gain_attn).astype(BF16)
    projected = lax.dot_general(
        w_attn[:, : 2 * kv_width + width],
        normed,
        (((0,), (1,)), ((), ())),
        preferred_element_type=F32,
    )
    keyval = jnp.concatenate(
        [rotate(projected[:kv_width], tables), projected[kv_width : 2 * kv_width]], axis=0
    ).astype(BF16)
    queries = (rotate(projected[2 * kv_width :], tables).astype(BF16) * SCALE).astype(BF16)
    return inputs, normed, queries, keyval


def head_rows(ref, head, offset=0):
    return ref[pl.ds(pl.multiple_of(head * HEAD + offset, HEAD), HEAD), :]


def attend_kernel(q_ref, p0, p1, p2, p3, bias_ref, o_ref, lse_ref):
    pieces = (p0, p1, p2, p3)
    count = q_ref.shape[1]
    kv_width = p0.shape[0] // 2
    ones = jnp.ones((16, count), BF16)

    def group(kv_head, carry):
        keys = [head_rows(p, kv_head).T for p in pieces]
        values = [
            jnp.concatenate([head_rows(p, kv_head, kv_width), ones], axis=0) for p in pieces
        ]
        for member in range(GROUPS):
            head = kv_head * GROUPS + member
            query = head_rows(q_ref, head)
            scores = [
                dot(keys[r], query) + bias_ref[r * count : (r + 1) * count, :] for r in range(4)
            ]
            top = jnp.maximum(
                jnp.maximum(scores[0], scores[1]), jnp.maximum(scores[2], scores[3])
            )
            top = jnp.max(top, axis=0, keepdims=True)
            total = jnp.zeros((HEAD + 16, count), F32)
            for r in range(4):
                total = total + dot(values[r], jnp.exp(scores[r] - top).astype(BF16))
            summed = total[HEAD : HEAD + 1]
            o_ref[pl.ds(pl.multiple_of(head * HEAD, HEAD), HEAD), :] = (
                total[:HEAD] / summed
            ).astype(BF16)
            lse_ref[head] = top + jnp.log(summed)
        return carry

    lax.fori_loop(0, KV_HEADS, group, 0)


def scores_back_kernel(
    q_ref, p0, p1, p2, p3, bias_ref, lse_ref, do_ref, o_ref, dq_ref, dkv_ref
):
    pieces = (p0, p1, p2, p3)
    count = q_ref.shape[1]
    kv_width = p0.shape[0] // 2

    def group(kv_head, carry):
        keys_turned = [head_rows(p, kv_head) for p in pieces]
        keys = [k.T for k in keys_turned]
        values = [head_rows(p, kv_head, kv_width).T for p in pieces]
        key_grads = [jnp.zeros((HEAD, count), F32) for _ in range(4)]
        value_grads = [jnp.zeros((HEAD, count), F32) for _ in range(4)]
        for member in range(GROUPS):
            head = kv_head * GROUPS + member
            query = head_rows(q_ref, head)
            grad = head_rows(do_ref, head)
            delta = jnp.sum(
                grad.astype(F32) * head_rows(o_ref, head).astype(F32), axis=0, keepdims=True
            )
            log_total = lse_ref[head]
            query_grad = jnp.zeros((HEAD, count), F32)
            for r in range(4):
                scores = dot(keys[r], query) + bias_ref[r * count : (r + 1) * count, :]
                probs = jnp.exp(scores - log_total)
                prob_grad = dot(values[r], grad)
                score_low = (probs * (prob_grad - delta)).astype(BF16)
                value_grads[r] = value_grads[r] + dot_back(grad, probs.astype(BF16))
                key_grads[r] = key_grads[r] + dot_back(query, score_low)
                query_grad = query_grad + dot(keys_turned[r], score_low)
            dq_ref[pl.ds(pl.multiple_of(head * HEAD, HEAD), HEAD), :] = query_grad * SCALE
        for r in range(4):
            start = pl.multiple_of(kv_head * HEAD, HEAD)
            dkv_ref[r, pl.ds(start, HEAD), :] = key_grads[r]
            dkv_ref[r, pl.ds(pl.multiple_of(start + kv_width, HEAD), HEAD), :] = value_grads[r]
        return carry

    lax.fori_loop(0, KV_HEADS, group, 0)


def local_call(kernel, outs, flops, *args):
    moved = sum(x.size * x.dtype.itemsize for x in (*args, *outs))
    return pl.pallas_call(
        kernel,
        out_shape=outs,
        in_specs=[pl.BlockSpec(memory_space=pltpu.VMEM)] * len(args),
        out_specs=[pl.BlockSpec(memory_space=pltpu.VMEM)] * len(outs),
        compiler_params=pltpu.CompilerParams(vmem_limit_bytes=48 * 1024 * 1024),
        cost_estimate=pl.CostEstimate(flops=flops, bytes_accessed=moved, transcendentals=0),
    )(*args)


def attend(projected, pieces, w_attn, bias):
    inputs, normed, queries, _ = projected
    width, rows = queries.shape
    kv_width = (w_attn.shape[1] - 2 * width) // 2
    attended, log_total = local_call(
        attend_kernel,
        [
            jax.ShapeDtypeStruct((width, rows), BF16),
            jax.ShapeDtypeStruct((HEADS, 1, rows), F32),
        ],
        10**10,
        queries,
        *pieces,
        bias,
    )
    resid = inputs + dot_rows(attended, w_attn[:, 2 * kv_width + width :])
    return resid, (inputs, normed, queries, pieces, log_total, attended)


def forward_ffn(resid, w_gateup, w_down, gain_ffn):
    normed = normalize(resid, gain_ffn).astype(BF16)
    gated = dot(normed, w_gateup)
    ffn = gated.shape[1] // 2
    hidden = (jax.nn.silu(gated[:, :ffn]) * gated[:, ffn:]).astype(BF16)
    outputs = resid + dot(hidden, w_down)
    return outputs, (resid, normed, gated, hidden)


def backward_ffn(grad, grad_low, saved, w_gateup, w_down, gain_ffn):
    resid, normed, gated, hidden = saved
    ffn = gated.shape[1] // 2
    hidden_grad = dot_back(grad_low, w_down)
    gate, up = gated[:, :ffn], gated[:, ffn:]
    sig = 1.0 / (1.0 + jnp.exp(-gate))
    gate_grad = (hidden_grad * up * (sig * (1.0 + gate * (1.0 - sig)))).astype(BF16)
    up_grad = (hidden_grad * (gate * sig)).astype(BF16)
    normed_grad = dot_back(gate_grad, w_gateup[:, :ffn]) + dot_back(up_grad, w_gateup[:, ffn:])
    resid_part, gain_grad = normalize_back(resid, gain_ffn, normed_grad)
    return grad + resid_part, gain_grad, gate_grad, up_grad


def backward_scores(resid_low, saved, w_attn, bias):
    _, _, queries, pieces, log_total, attended = saved
    width, rows = queries.shape
    kv_width = (w_attn.shape[1] - 2 * width) // 2
    attended_low = dot_back(w_attn[:, 2 * kv_width + width :], resid_low).astype(BF16)
    return local_call(
        scores_back_kernel,
        [
            jax.ShapeDtypeStruct((width, rows), F32),
            jax.ShapeDtypeStruct((4, 2 * kv_width, rows), F32),
        ],
        2 * 10**10,
        queries,
        *pieces,
        bias,
        log_total,
        attended_low,
        attended,
    )


def backward_project(resid_grad, query_grad, kv_grad, saved, w_attn, gain_attn, tables):
    inputs = saved[0]
    width = inputs.shape[1]
    kv_width = (w_attn.shape[1] - 2 * width) // 2
    query_low = rotate_back(query_grad, tables).astype(BF16)
    key_low = rotate_back(kv_grad[:kv_width], tables).astype(BF16)
    value_low = kv_grad[kv_width:].astype(BF16)
    projected_low = jnp.concatenate([key_low, value_low, query_low], axis=0)
    normed_grad = lax.dot_general(
        projected_low,
        w_attn[:, : 2 * kv_width + width],
        (((0,), (1,)), ((), ())),
        preferred_element_type=F32,
    )
    input_part, gain_grad = normalize_back(inputs, gain_attn, normed_grad)
    return resid_grad + input_part, gain_grad, query_low, key_low, value_low


def both(own, other):
    return jnp.concatenate([own, other], axis=0)


def shards(
    tokens, cotangent, doc_ids, w_query, w_keyval, w_out, w_gateup, w_down, gain_attn, gain_ffn
):
    core = lax.axis_index("pipe")
    ctx = lax.axis_index("ctx")
    zed = lax.axis_index("fsdp")
    on_first = core == 0
    rows = tokens.shape[2]
    width = tokens.shape[3]
    length = doc_ids.shape[2]
    kv_width = w_keyval.shape[2] // 2

    pieces = own_pieces(
        w_query[0], w_keyval[0], w_out[0], w_gateup[0], w_down[0], core, ctx
    )
    gains = jnp.concatenate([gain_attn, gain_ffn], axis=0)
    gains_other = swap_cores(gains)
    layer_gains = (pick(on_first, gains, gains_other), pick(on_first, gains_other, gains))

    doc_row = lax.dynamic_index_in_dim(doc_ids[:, 0], core, 0, keepdims=False)
    inputs_low = lax.dynamic_index_in_dim(tokens[:, 0], core, 0, keepdims=False)
    cotangent_own = lax.dynamic_index_in_dim(cotangent[:, 0], core, 0, keepdims=False)
    earlier = jnp.sum((doc_row[None, :] < doc_row[:, None]).astype(jnp.int32), axis=1)
    positions = jnp.arange(length, dtype=jnp.int32) - earlier
    token_pos = lax.dynamic_slice_in_dim(positions, ctx * rows, rows, 0)
    tables = angle_tables(token_pos.astype(F32))
    own_docs = lax.dynamic_slice_in_dim(doc_row, ctx * rows, rows, 0)
    query_index = ctx * rows + jnp.arange(rows, dtype=jnp.int32)
    key_docs = []
    key_index = []
    for mask in range(4):
        key_docs.append(lax.dynamic_slice_in_dim(doc_row, (ctx ^ mask) * rows, rows, 0))
        key_index.append((ctx ^ mask) * rows + jnp.arange(rows, dtype=jnp.int32))
    key_docs = jnp.concatenate(key_docs)
    key_index = jnp.concatenate(key_index)
    seen = (own_docs[None, :] == key_docs[:, None]) & (
        key_index[:, None] <= query_index[None, :]
    )
    bias = jnp.where(seen, 0.0, NEGATIVE).astype(F32)

    order = Order()
    (attn_first, gu_first, down_first), (attn_second, gu_second, down_second) = pieces
    attn0 = Spread(order, attn_first)
    gu0 = Spread(order, gu_first)
    attn0.advance()
    attn0.advance()
    gu0.advance()
    down0 = Along(order, down_first)
    attn0.advance()
    gu0.advance()
    both1 = Spread(order, jnp.concatenate([attn_second, gu_second], axis=0))
    attn0.advance()
    (w_attn0,) = place(attn0)
    w_attn0 = order.wait(w_attn0)
    own0 = project(inputs_low, w_attn0, layer_gains[0][0], tables)
    keys0 = send_keys(own0[3])
    down0.advance()
    keyval0 = (own0[3], *[order.wait(flow) for flow in keys0])
    gu0.advance()
    resid0, attn_saved0 = attend(own0, keyval0, w_attn0, bias)
    resid0 = order.wait(resid0)
    both1.advance()
    down1 = Along(order, down_second)
    down0.advance()
    gu0.advance()
    both1.arrive()
    attn1, gu1 = both1.split(1)
    attn1.start()
    gu1.start()
    w_gu0, w_down0 = place(gu0, down0)
    w_gu0 = order.wait(w_gu0)
    down1.advance()
    outputs0, ffn_saved0 = forward_ffn(resid0, w_gu0, w_down0, layer_gains[0][1])
    middle = order.wait(outputs0.astype(BF16))
    attn1.advance()
    attn1.advance()
    (w_attn1,) = place(attn1)
    w_attn1 = order.wait(w_attn1)
    own1 = project(middle, w_attn1, layer_gains[1][0], tables)
    keys1 = send_keys(own1[3])
    gu1.advance()
    keyval1 = (own1[3], *[order.wait(flow) for flow in keys1])
    resid1, attn_saved1 = attend(own1, keyval1, w_attn1, bias)
    resid1 = order.wait(resid1)
    down1.advance()
    gu1.advance()
    w_gu1, w_down1 = place(gu1, down1)
    w_gu1 = order.wait(w_gu1)
    outputs1, ffn_saved1 = forward_ffn(resid1, w_gu1, w_down1, layer_gains[1][1])
    section_outs = [middle, outputs1.astype(BF16)]

    weights = [(w_attn0, w_gu0, w_down0), (w_attn1, w_gu1, w_down1)]
    saved = [(attn_saved0, ffn_saved0), (attn_saved1, ffn_saved1)]
    half = -(-width // 256) * 128

    def down_term(grad_low, ffn_saved):
        left, right = grad_low[:, :half], grad_low[:, width - half :]
        hidden = ffn_saved[3]
        return dot_rows(
            both(hidden, swap_cores(hidden)),
            both(pick(on_first, left, right), swap_cores(pick(on_first, right, left))),
        ).astype(BF16)

    def gateup_term(gate_grad, up_grad, ffn_saved):
        normed = ffn_saved[1]
        return dot_rows(
            both(normed, swap_cores(normed)),
            both(
                pick(on_first, gate_grad, up_grad), swap_cores(pick(on_first, up_grad, gate_grad))
            ),
        ).astype(BF16)

    def attn_term(attn_saved, resid_low, query_low, key_low, value_low):
        normed, attended = attn_saved[1].T, attn_saved[5]
        lefts = pick(on_first, normed, attended)
        lefts_other = swap_cores(pick(on_first, attended, normed))
        rights = pick(on_first, query_low.T, resid_low)
        rights_other = swap_cores(pick(on_first, resid_low, query_low.T))
        thin = pick(on_first, key_low, value_low)
        thin_other = swap_cores(pick(on_first, value_low, key_low))
        normed_other = swap_cores(normed)
        return jnp.concatenate(
            [
                dot(jnp.concatenate([lefts, lefts_other], 1), both(rights, rights_other)),
                dot_back(
                    jnp.concatenate([normed, normed_other], 1),
                    jnp.concatenate([thin, thin_other], 1),
                ),
            ],
            axis=1,
        ).astype(BF16)

    grad_low = cotangent_own
    input_grads = [None, None]
    reduced = [None, None]
    gain_grads = [None, None]
    above = None
    for layer in (1, 0):
        w_attn, w_gu, w_dn = weights[layer]
        attn_saved, ffn_saved = saved[layer]
        grad_low = order.wait(grad_low)
        down = Reduce(order, order.wait(down_term(grad_low, ffn_saved)), True)
        resid_grad, gain_ffn_grad, gate_grad, up_grad = backward_ffn(
            grad_low.astype(F32), grad_low, ffn_saved, w_gu, w_dn, layer_gains[layer][1]
        )
        if above:
            above[2].advance()
        gateup = Reduce(
            order, order.wait(gateup_term(gate_grad, up_grad, ffn_saved)), layer == 1
        )
        resid_grad = order.wait(resid_grad)
        down.advance()
        if above:
            above[2].advance()
            above[0].settle()
        resid_low = resid_grad.astype(BF16)
        query_grad, kv_part = backward_scores(resid_low, attn_saved, w_attn, bias)
        kv_part = order.wait(kv_part)
        flows = return_keys(kv_part)
        down.advance()
        gateup.advance()
        if above:
            above[1].settle()
        kv_grad = kv_part[0] + sum(order.wait(flow).astype(F32) for flow in flows)
        input_grad, gain_attn_grad, query_low, key_low, value_low = backward_project(
            resid_grad, query_grad, kv_grad, attn_saved, w_attn, layer_gains[layer][0], tables
        )
        attn = Reduce(
            order,
            order.wait(attn_term(attn_saved, resid_low, query_low, key_low, value_low)),
            layer == 1,
        )
        gateup.advance()
        if layer == 1:
            above = [down, gateup, attn]
        reduced[layer] = [down, gateup, attn]
        grad_low = input_grad.astype(BF16)
        input_grads[layer] = grad_low
        gain_grads[layer] = (gain_attn_grad, gain_ffn_grad)

    gain_total = jnp.stack([*gain_grads[0], *gain_grads[1]])
    gain_total = gain_total + swap_cores(gain_total)
    gain_total = pick(on_first, gain_total[:2], gain_total[2:])
    gain_flight = across(order.hold(gain_total), "ctx", 1)
    above[2].settle()
    attn.advance()
    gain_total = gain_total + order.wait(gain_flight)
    gain_flight = across(order.hold(gain_total), "ctx", 2)
    gateup.advance()
    gain_total = gain_total + order.wait(gain_flight)
    for mask in z_masks()[:-1]:
        gain_total = gain_total + across(order.hold(gain_total), "fsdp", mask)
    attn.advance()
    gain_total = order.wait(gain_total)
    gain_flight = across(gain_total, "fsdp", z_masks()[-1])
    down.settle()
    attn.advance()
    gain_total = gain_total + order.wait(gain_flight)
    reduced = [[f.result.astype(F32) for f in (r[2], r[1], r[0])] for r in reduced]

    def to_layers(first, second):
        own = pick(on_first, first, second)
        other = pick(on_first, one_way(first, 1, 0), one_way(second, 0, 1))
        return pick(on_first, own, other), pick(on_first, other, own)

    section_out = jnp.stack(to_layers(section_outs[0], section_outs[1]))
    section_in_grad = jnp.stack(to_layers(input_grads[0], input_grads[1]))
    attn_first, attn_second = to_layers(reduced[0][0], reduced[1][0])
    gate, up = to_layers(reduced[0][1], reduced[1][1])
    down_left, down_right = to_layers(reduced[0][2], reduced[1][2])
    return (
        section_out[None, :, None],
        section_in_grad[None, :, None],
        attn_first[None, :, :width],
        jnp.concatenate([attn_first[:, width:], attn_second[:, width:]], axis=1)[None],
        attn_second[None, :, :width],
        jnp.concatenate([gate, up], axis=1)[None],
        jnp.concatenate(
            [down_left[:, : width // 2], down_right[:, half - width // 2 :]], axis=1
        )[None],
        gain_total[0][None],
        gain_total[1][None],
    )


def solution(mesh):
    return jax.shard_map(
        shards,
        mesh=mesh,
        in_specs=(
            P(None, "fsdp", "ctx", None),
            P(None, "fsdp", "ctx", None),
            P(None, "fsdp", None),
            P("pipe", "fsdp", None),
            P("pipe", "fsdp", None),
            P("pipe", "fsdp", None),
            P("pipe", "fsdp", None),
            P("pipe", "fsdp", None),
            P("pipe", None),
            P("pipe", None),
        ),
        out_specs=(
            P("pipe", None, "fsdp", "ctx", None),
            P("pipe", None, "fsdp", "ctx", None),
            P("pipe", ("ctx", "fsdp"), None),
            P("pipe", ("ctx", "fsdp"), None),
            P("pipe", ("ctx", "fsdp"), None),
            P("pipe", ("ctx", "fsdp"), None),
            P("pipe", ("ctx", "fsdp"), None),
            P("pipe", None),
            P("pipe", None),
        ),
        check_vma=False,
    )
```

```python
import functools
import math

import jax
import jax.numpy as jnp
from jax import lax
from jax.experimental import pallas as pl
from jax.experimental.pallas import tpu as pltpu
from jax.sharding import PartitionSpec as P

HEADS = 15
KV_HEADS = 5
HEAD = 64
GROUPS = HEADS // KV_HEADS
EPSILON = 1e-05
NEGATIVE = -1e30
SCALE = 1.0 / math.sqrt(HEAD)
F32 = jnp.float32
BF16 = jnp.bfloat16


def swap_cores(array):
    return lax.ppermute(array, "pipe", [(0, 1), (1, 0)])


def one_way(array, source, target):
    return lax.ppermute(array, "pipe", [(source, target)])


def across(array, axis, mask):
    count = lax.axis_size(axis)
    return lax.ppermute(array, axis, [(i, i ^ mask) for i in range(count)])


def pick(flag, first, second):
    return jnp.where(flag, first, second)


def two_ways(first, second):
    on_first = lax.axis_index("pipe") == 0
    return pick(on_first, first, second), pick(on_first, second, first)


class Order:
    def __init__(self):
        self.last = None

    def hold(self, *arrays):
        if self.last is not None:
            *arrays, _ = lax.optimization_barrier((*arrays, self.last))
        return arrays[0] if len(arrays) == 1 else tuple(arrays)

    def wait(self, array):
        array = self.hold(array)
        self.last = array
        return array

    def waits(self, arrays):
        arrays = self.hold(*arrays)
        self.last = arrays[0]
        return arrays


def first_way(array):
    pairs = [(c, c ^ 1) for c in range(4)] + [(4 + c, 4 + (c ^ 2)) for c in range(4)]
    return lax.ppermute(array, ("pipe", "ctx"), pairs)


def second_way(array):
    pairs = [(c, c ^ 2) for c in range(4)] + [(4 + c, 4 + (c ^ 1)) for c in range(4)]
    return lax.ppermute(array, ("pipe", "ctx"), pairs)


def dot(left, right):
    return jnp.dot(left, right, preferred_element_type=F32)


def dot_back(left, right):
    return lax.dot_general(left, right, (((1,), (1,)), ((), ())), preferred_element_type=F32)


def dot_rows(left, right):
    return lax.dot_general(left, right, (((0,), (0,)), ((), ())), preferred_element_type=F32)


def normalize(values, gain):
    return values * lax.rsqrt(jnp.mean(values * values, axis=-1, keepdims=True) + EPSILON) * gain


def normalize_back(values, gain, grad):
    inverse = lax.rsqrt(jnp.mean(values * values, axis=-1, keepdims=True) + EPSILON)
    unit = values * inverse
    gain_grad = jnp.sum(grad * unit, axis=0)
    scaled = grad * gain
    return inverse * (scaled - unit * jnp.mean(scaled * unit, axis=-1, keepdims=True)), gain_grad


def angle_tables(token_pos):
    half_size = HEAD // 2
    freqs = jnp.exp(jnp.arange(half_size, dtype=F32) * (-2.0 * math.log(100000.0) / HEAD))
    angles = freqs[:, None] * token_pos[None, :]
    cosine, sine = jnp.cos(angles), jnp.sin(angles)
    return jnp.concatenate([cosine, cosine], axis=0), jnp.concatenate([sine, sine], axis=0)


def rotate(values, tables):
    rows, cols = values.shape
    heads = values.reshape(rows // HEAD, HEAD, cols)
    half = HEAD // 2
    turned = jnp.concatenate([-heads[:, half:], heads[:, :half]], axis=1)
    return (heads * tables[0] + turned * tables[1]).reshape(rows, cols)


def rotate_back(values, tables):
    rows, cols = values.shape
    heads = values.reshape(rows // HEAD, HEAD, cols)
    half = HEAD // 2
    scaled = heads * tables[1]
    turned = jnp.concatenate([scaled[:, half:], -scaled[:, :half]], axis=1)
    return (heads * tables[0] + turned).reshape(rows, cols)


def z_masks():
    count = lax.axis_size("fsdp")
    masks = []
    while count > 1:
        count //= 2
        masks.append(count)
    return masks


class Spread:
    def __init__(self, order, own):
        self.order = order
        held = order.hold(own)[None]
        self.rank = [0]
        for mask in z_masks()[:-2]:
            held = jnp.concatenate([held, across(held, "fsdp", mask)], axis=0)
            self.rank = self.rank + [place ^ mask for place in self.rank]
        self.held = held
        self.flights = [across(held, "fsdp", mask) for mask in (1, 2, 3)]
        self.step = 0

    @classmethod
    def behind(cls, order, held):
        self = cls.__new__(cls)
        self.order, self.held, self.flights, self.rank = order, held, [], None
        self.step = 0
        return self

    def slot(self, number):
        return number if self.rank is None else lax.axis_index("fsdp") ^ self.rank[number]

    def collect(self):
        self.flights = [self.order.wait(flight) for flight in self.flights]

    def advance(self):
        self.step += 1
        if self.step == 1:
            self.collect()
            held = [self.held, *self.flights]
            if self.rank is not None:
                self.rank = [place ^ mask for mask in range(4) for place in self.rank]
            held = self.order.hold(jnp.concatenate(held, axis=0))
            self.flight = first_way(held)
            self.side = second_way(held)
            self.parts = [(held, swap_cores(held))]
        elif self.step == 2:
            got = self.order.wait(self.flight)
            side = self.order.wait(self.side)
            self.flight = second_way(got)
            self.parts.append((got, swap_cores(got)))
            self.parts.append((side, swap_cores(side)))
        else:
            got = self.order.wait(self.flight)
            self.parts.append((got, swap_cores(got)))

    def arrays(self):
        return [part[side] for side in range(2) for part in self.parts]


def place_attn(group):
    arrays = group.arrays()
    depth, rows, cols = arrays[0].shape
    zcount = lax.axis_size("fsdp")
    ccount = lax.axis_size("ctx")

    def body(*refs):
        out, sems = refs[8], refs[9]
        core, ctx = lax.axis_index("pipe"), lax.axis_index("ctx")
        copies = []
        for number in range(8):
            half = core if number < 4 else 1 - core
            mask = 0
            if number % 2 == 1:
                mask = mask ^ (1 + half)
            if number % 4 >= 2:
                mask = mask ^ (2 - half)
            col = pl.multiple_of((ctx ^ mask) * cols, cols)
            for slot in range(depth):
                copies.append(
                    pltpu.make_async_copy(
                        refs[number].at[slot],
                        out.at[group.slot(slot), half, :, pl.ds(col, cols)],
                        sems.at[len(copies)],
                    )
                )
        for copy in copies:
            copy.start()
        for copy in copies:
            copy.wait()

    out = pl.pallas_call(
        body,
        out_shape=jax.ShapeDtypeStruct((zcount, 2, rows, ccount * cols), BF16),
        in_specs=[pl.BlockSpec(memory_space=pl.ANY)] * 8,
        out_specs=pl.BlockSpec(memory_space=pltpu.VMEM),
        scratch_shapes=[pltpu.SemaphoreType.DMA((8 * depth,))],
        compiler_params=pltpu.CompilerParams(vmem_limit_bytes=40 * 1024 * 1024),
        cost_estimate=pl.CostEstimate(flops=0, bytes_accessed=0, transcendentals=0),
    )(*arrays)
    return out.reshape(-1, out.shape[-1])


def first_side(half, ctx):
    return pick(half == 0, ctx % 2, ctx // 2)


class Down:
    def __init__(self, order, piece):
        self.order = order
        self.flight = lax.all_gather(order.hold(piece), "fsdp", axis=0, tiled=False)

    def start(self):
        self.near = self.order.wait(self.flight)
        self.flight = first_way(self.near)
        self.near_other = swap_cores(self.near)

    def finish(self):
        far = self.order.wait(self.flight)
        return [self.near, far, self.near_other, swap_cores(far)]


class Ffn:
    def __init__(self, group, down):
        self.group = group
        self.arrays = group.arrays() + down
        self.depth, self.rows, self.cols = self.arrays[0].shape

    def scratch(self, rows):
        return [
            pltpu.VMEM((4, 2, self.depth * self.rows, self.cols), BF16),
            pltpu.VMEM((4, 2, 2, *self.arrays[8].shape[1:]), BF16),
            pltpu.SemaphoreType.DMA((4, 2 * self.depth)),
            pltpu.SemaphoreType.DMA((16,)),
            pltpu.VMEM((rows, self.arrays[8].shape[2]), F32),
        ]

    def start(self, refs, held, down, sems, down_sems):
        core, ctx = lax.axis_index("pipe"), lax.axis_index("ctx")
        blocks, quarters = [], []
        for number in range(4):
            copies = []
            other = 4 + (0, 2, 1, 3)[number]
            for side, half in ((number, core), (other, 1 - core)):
                for slot in range(self.depth):
                    row = pl.multiple_of(self.group.slot(slot) * self.rows, 16)
                    copies.append(
                        pltpu.make_async_copy(
                            refs[side].at[slot],
                            held.at[number, half, pl.ds(row, self.rows), :],
                            sems.at[number, len(copies)],
                        )
                    )
            blocks.append(copies)
            mask = (0, 1 + core, 2 - core, 3)[number]
            quarters.append(ctx ^ mask)
        downs = []
        for side, half in ((8, core), (9, core), (10, 1 - core), (11, 1 - core)):
            near = first_side(half, ctx)
            for zed in range(4):
                downs.append(
                    pltpu.make_async_copy(
                        refs[side].at[zed],
                        down.at[zed, half, near if side % 2 == 0 else 1 - near],
                        down_sems.at[len(downs)],
                    )
                )
        for copy in blocks[0] + downs + blocks[1] + blocks[2] + blocks[3]:
            copy.start()
        return blocks, quarters, downs

    def call(self, body, outs, *args):
        return pl.pallas_call(
            body,
            out_shape=outs,
            in_specs=[pl.BlockSpec(memory_space=pltpu.VMEM)] * len(args)
            + [pl.BlockSpec(memory_space=pl.ANY)] * 12,
            out_specs=[pl.BlockSpec(memory_space=pltpu.VMEM)] * len(outs),
            scratch_shapes=self.scratch(args[0].shape[0]),
            compiler_params=pltpu.CompilerParams(vmem_limit_bytes=48 * 1024 * 1024),
            cost_estimate=pl.CostEstimate(flops=0, bytes_accessed=0, transcendentals=0),
        )(*args, *self.arrays)

    def forward(self, resid, gain):
        rows, width = resid.shape
        cols = self.cols
        ffn = 4 * cols

        def body(r_ref, gain_ref, *refs):
            low_ref, normed_ref, gate_ref, up_ref, hidden_ref = refs[12:17]
            held, down, total = refs[17], refs[18], refs[21]
            blocks, quarters, downs = self.start(refs[:12], *refs[17:21])
            resid = r_ref[...]
            normed = normalize(resid, gain_ref[...]).astype(BF16)
            normed_ref[...] = normed.T
            total[...] = resid
            for number in range(4):
                for copy in blocks[number]:
                    copy.wait()
                gate = dot(normed, held[number, 0])
                up = dot(normed, held[number, 1])
                hidden = (gate / (1.0 + jnp.exp(-gate)) * up).astype(BF16)
                place = pl.ds(pl.multiple_of(quarters[number] * cols, cols), cols)
                gate_ref[:, place] = gate
                up_ref[:, place] = up
                hidden_ref[place, :] = hidden.T
                if number == 0:
                    for copy in downs:
                        copy.wait()
                weights = down[quarters[number]].reshape(cols, width)
                total[...] += dot(hidden, weights)
            low_ref[...] = total[...].astype(BF16)

        return self.call(
            body,
            [
                jax.ShapeDtypeStruct((rows, width), BF16),
                jax.ShapeDtypeStruct((width, rows), BF16),
                jax.ShapeDtypeStruct((rows, ffn), F32),
                jax.ShapeDtypeStruct((rows, ffn), F32),
                jax.ShapeDtypeStruct((ffn, rows), BF16),
            ],
            resid,
            gain[None],
        )

    def backward(self, grad_low, resid, gain, gate, up):
        rows, width = resid.shape
        cols = self.cols
        ffn = 4 * cols

        def body(grad_ref, r_ref, gain_ref, gate_ref, up_ref, *refs):
            out_ref, gain_out, gate_out, up_out, total = *refs[12:16], refs[20]
            held, down = refs[16:18]
            blocks, quarters, downs = self.start(refs[:12], *refs[16:20])
            grad = grad_ref[...]
            for number in range(4):
                place = pl.ds(pl.multiple_of(quarters[number] * cols, cols), cols)
                if number == 0:
                    for copy in downs:
                        copy.wait()
                weights = down[quarters[number]].reshape(cols, width)
                hidden_grad = dot_back(grad, weights)
                gate, up = gate_ref[:, place], up_ref[:, place]
                sig = 1.0 / (1.0 + jnp.exp(-gate))
                gate_grad = (hidden_grad * up * (sig * (1.0 + gate * (1.0 - sig)))).astype(BF16)
                up_grad = (hidden_grad * (gate * sig)).astype(BF16)
                own, other = two_ways(gate_grad, up_grad)
                gate_out[:, place] = own
                up_out[:, place] = other
                for copy in blocks[number]:
                    copy.wait()
                part = dot_back(gate_grad, held[number, 0]) + dot_back(up_grad, held[number, 1])
                if number == 0:
                    total[...] = part
                else:
                    total[...] += part
            resid_part, gain_grad = normalize_back(r_ref[...], gain_ref[...], total[...])
            out_ref[...] = grad.astype(F32) + resid_part
            gain_out[...] = gain_grad[None]

        outs = self.call(
            body,
            [
                jax.ShapeDtypeStruct((rows, width), F32),
                jax.ShapeDtypeStruct((1, width), F32),
                jax.ShapeDtypeStruct((rows, ffn), BF16),
                jax.ShapeDtypeStruct((rows, ffn), BF16),
            ],
            grad_low,
            resid,
            gain[None],
            gate,
            up,
        )
        return outs[0], outs[1][0], outs[2], outs[3]


class WholeFfn:
    def __init__(self, w_gateup, w_down, layer):
        core = lax.axis_index("pipe")
        whole = []
        for array in (w_gateup, w_down):
            mine = lax.all_gather(array, "fsdp", axis=0, tiled=True)
            whole.append(pick(core == layer, mine, swap_cores(mine)))
        self.w_gateup, self.w_down = whole

    def forward(self, resid, gain):
        normed = normalize(resid, gain).astype(BF16)
        gated = dot(normed, self.w_gateup)
        ffn = gated.shape[1] // 2
        gate, up = gated[:, :ffn], gated[:, ffn:]
        hidden = (gate / (1.0 + jnp.exp(-gate)) * up).astype(BF16)
        outputs = (resid + dot(hidden, self.w_down)).astype(BF16)
        return outputs, normed.T, gate, up, hidden.T

    def backward(self, grad_low, resid, gain, gate, up):
        ffn = gate.shape[1]
        hidden_grad = dot_back(grad_low, self.w_down)
        sig = 1.0 / (1.0 + jnp.exp(-gate))
        gate_grad = (hidden_grad * up * (sig * (1.0 + gate * (1.0 - sig)))).astype(BF16)
        up_grad = (hidden_grad * (gate * sig)).astype(BF16)
        normed_grad = dot_back(gate_grad, self.w_gateup[:, :ffn]) + dot_back(
            up_grad, self.w_gateup[:, ffn:]
        )
        resid_part, gain_grad = normalize_back(resid, gain, normed_grad)
        own, other = two_ways(gate_grad, up_grad)
        return grad_low.astype(F32) + resid_part, gain_grad, own, other


def own_pieces(w_query, w_keyval, w_out, w_gateup, w_down, core, ctx):
    attn = jnp.concatenate([w_keyval, w_query, w_out], axis=1)
    rows = attn.shape[0] // 2
    cols = attn.shape[1] // 4
    ffn = w_gateup.shape[1] // 2
    depth = w_down.shape[0] // 2

    def parts(half):
        return (
            lax.dynamic_slice(attn, (half * rows, ctx * cols), (rows, cols)),
            lax.dynamic_slice(w_gateup, (0, half * ffn + ctx * cols), (2 * rows, cols)),
            lax.dynamic_slice_in_dim(
                w_down, half * depth + first_side(half, ctx) * (depth // 2), depth // 2, 0
            ),
        )

    kept = parts(core)
    received = [swap_cores(piece) for piece in parts(1 - core)]
    first = [pick(core == 0, a, b) for a, b in zip(kept, received)]
    second = [pick(core == 0, b, a) for a, b in zip(kept, received)]
    return first, second


def add_low(kept, received):
    return (kept.astype(F32) + received.astype(F32)).astype(BF16)


def term(*pairs, gains=None):
    rows = pairs[0][0].shape[0]
    deep = rows // 4
    widths = [pair[2].shape[1] if pair[4] else pair[2].shape[0] for pair in pairs]

    def body(*refs):
        sent_ref, kept_ref = refs[-2:]
        core, ctx = lax.axis_index("pipe"), lax.axis_index("ctx")
        y, x = ctx // 2, ctx % 2
        for out, xx, yy in ((sent_ref, 1 - x, 1 - y), (kept_ref, x, y)):
            for side in range(2):
                block = jnp.where(core == 0, xx + 2 * side, 2 * yy + side)
                place = pl.ds(pl.multiple_of(block * deep, 16), deep)
                offset = 0
                for number, pair in enumerate(pairs):
                    lefts = [ref[place, :] for ref in refs[4 * number : 4 * number + 2]]
                    rights = refs[4 * number + 2 : 4 * number + 4]
                    for start in range(0, widths[number], 640):
                        stop = min(start + 640, widths[number])
                        total = None
                        for left, right in zip(lefts, rights):
                            if pair[4]:
                                part = dot(left, right[:, start:stop])
                            else:
                                part = dot_back(left, right[start:stop, :])
                            total = part if total is None else total + part
                        out[side, :deep, offset + start : offset + stop] = total.astype(BF16)
                    offset += widths[number]
                if gains is not None:
                    out[side, deep:, :] = refs[-3][...]

    extra = []
    if gains is not None:
        low = gains.astype(BF16)
        extra = [jnp.pad(low, ((0, 16 - low.shape[0]), (0, sum(widths) - low.shape[1])))]
    shape = jax.ShapeDtypeStruct((2, deep + 16 * len(extra), sum(widths)), BF16)
    arrays = [array for pair in pairs for array in pair[:4]]
    return local_call(body, [shape, shape], *arrays, *extra)


class Reduce:
    def __init__(self, order, term, offload=False, extra=0):
        self.order = order
        self.extra = extra
        self.offload = offload
        core, ctx, self.zed = lax.axis_index("pipe"), lax.axis_index("ctx"), lax.axis_index("fsdp")
        self.side = pick(core == 0, ctx // 2, ctx % 2)
        self.step = 0
        self.result = None
        sent, self.kept = term
        self.flights = [first_way(sent)]

    def land(self):
        total = self.kept.astype(F32)
        for flight in self.flights:
            total = total + self.order.wait(flight).astype(F32)
        return total

    def advance(self):
        if self.result is not None:
            return
        total = self.land()
        self.step += 1
        if self.step == 3:
            self.result = total
            return
        low = total.astype(BF16)
        index = lax.dynamic_index_in_dim
        if self.step == 1:
            self.kept, sent = self.order.waits(
                (index(low, self.side, 0, False), index(low, 1 - self.side, 0, False))
            )
            self.flights = [second_way(sent)]
            return
        if self.offload:
            count = lax.axis_size("fsdp")
            parts = low.reshape(count, low.shape[0] // count, low.shape[1])
            parts = self.order.wait(parts)
            self.result = lax.psum_scatter(parts, "fsdp", scatter_dimension=0, tiled=False)
            return
        deep = low.shape[0] - self.extra
        body, tail = low[:deep], low[deep:]
        for mask in z_masks()[:-2]:
            half = body.shape[0] // 2
            high = (self.zed & mask) != 0
            self.kept = jnp.concatenate([pick(high, body[half:], body[:half]), tail], axis=0)
            sent = jnp.concatenate([pick(high, body[:half], body[half:]), tail], axis=0)
            self.flights = [across(sent, "fsdp", mask)]
            low = self.land().astype(BF16)
            body, tail = low[:half], low[half:]
        parts = body.reshape(4, body.shape[0] // 4, body.shape[1])
        if self.extra:
            tails = jnp.broadcast_to(tail, (4, *tail.shape))
            parts = jnp.concatenate([parts, tails], axis=1)
        here = self.zed % 4
        self.kept = index(parts, here, 0, False)
        sent = [index(parts, here ^ mask, 0, False) for mask in (3, 2, 1)]
        sent = self.order.waits(sent)
        self.flights = [across(block, "fsdp", mask) for block, mask in zip(sent, (3, 2, 1))]

    def settle(self):
        self.result = self.order.wait(self.result)


def send_keys(keyval):
    flows = []
    for mask in (3, 1, 2):
        flows.append(across(keyval, "ctx", mask))
    return flows[1], flows[2], flows[0]


def return_keys(parts):
    return [across(part, "ctx", mask) for part, mask in zip(parts, (1, 2, 3))]


def local_call(kernel, outs, *args):
    return pl.pallas_call(
        kernel,
        out_shape=outs,
        in_specs=[pl.BlockSpec(memory_space=pltpu.VMEM)] * len(args),
        out_specs=[pl.BlockSpec(memory_space=pltpu.VMEM)] * len(outs),
        compiler_params=pltpu.CompilerParams(vmem_limit_bytes=48 * 1024 * 1024),
        cost_estimate=pl.CostEstimate(flops=0, bytes_accessed=0, transcendentals=0),
    )(*args)


def project(inputs_low, w_attn, gain_attn, tables):
    rows, width = inputs_low.shape
    kv_width = (w_attn.shape[1] - 2 * width) // 2

    def body(x_ref, w_ref, gain_ref, cos_ref, sin_ref, normed_ref, q_ref, kv_ref):
        tables = cos_ref[...], sin_ref[...]
        normed = normalize(x_ref[...].astype(F32), gain_ref[...]).astype(BF16)
        normed_ref[...] = normed.T
        projected = dot(normed, w_ref[:, : 2 * kv_width + width]).T
        kv_ref[:kv_width, :] = rotate(projected[:kv_width], tables).astype(BF16)
        kv_ref[kv_width:, :] = projected[kv_width : 2 * kv_width].astype(BF16)
        queries = rotate(projected[2 * kv_width :], tables).astype(BF16)
        q_ref[...] = (queries.astype(F32) * SCALE).astype(BF16)

    return local_call(
        body,
        [
            jax.ShapeDtypeStruct((width, rows), BF16),
            jax.ShapeDtypeStruct((width, rows), BF16),
            jax.ShapeDtypeStruct((2 * kv_width, rows), BF16),
        ],
        inputs_low,
        w_attn,
        gain_attn[None],
        *tables,
    )


def head_rows(ref, head, offset=0):
    return ref[pl.ds(pl.multiple_of(head * HEAD + offset, HEAD), HEAD), :]


def attend_kernel(
    q_ref, p0, p1, p2, p3, bias_ref, x_ref, w_ref, normed_ref, own_ref, send_ref, lse_ref, r_ref, o_ref
):
    pieces = (p0, p1, p2, p3)
    count = q_ref.shape[1]
    kv_width = p0.shape[0] // 2
    ones = jnp.ones((16, count), BF16)

    def group(kv_head, carry):
        keys = [head_rows(p, kv_head).T for p in pieces]
        values = [
            jnp.concatenate([head_rows(p, kv_head, kv_width), ones], axis=0) for p in pieces
        ]
        for member in range(GROUPS):
            head = kv_head * GROUPS + member
            query = head_rows(q_ref, head)
            scores = [
                dot(keys[r], query) + bias_ref[r * count : (r + 1) * count, :] for r in range(4)
            ]
            top = jnp.maximum(
                jnp.maximum(scores[0], scores[1]), jnp.maximum(scores[2], scores[3])
            )
            top = jnp.max(top, axis=0, keepdims=True)
            total = jnp.zeros((HEAD + 16, count), F32)
            for r in range(4):
                total = total + dot(values[r], jnp.exp(scores[r] - top).astype(BF16))
            summed = total[HEAD : HEAD + 1]
            o_ref[pl.ds(pl.multiple_of(head * HEAD, HEAD), HEAD), :] = (
                total[:HEAD] / summed
            ).astype(BF16)
            lse_ref[head] = top + jnp.log(summed)
        return carry

    lax.fori_loop(0, KV_HEADS, group, 0)
    attended = o_ref[...]
    own_ref[...], send_ref[...] = two_ways(normed_ref[...], attended)
    width = attended.shape[0]
    r_ref[...] = x_ref[...].astype(F32) + dot(
        attended.T, w_ref[:, w_ref.shape[1] - width :]
    )


def scores_back_kernel(
    dr_ref,
    w_ref,
    q_ref,
    p0,
    p1,
    p2,
    p3,
    bias_ref,
    lse_ref,
    left_own_ref,
    left_send_ref,
    cos_ref,
    sin_ref,
    own_ref,
    send_ref,
    kv_own_ref,
    kv_x_ref,
    kv_y_ref,
    kv_xy_ref,
    do_ref,
    o_ref,
    dq_ref,
):
    tables = cos_ref[...], sin_ref[...]
    width = q_ref.shape[0]
    resid_low = dr_ref[...].astype(BF16)
    do_ref[...] = dot_back(w_ref[:, w_ref.shape[1] - width :], resid_low).astype(BF16)
    _, o_ref[...] = two_ways(left_own_ref[...], left_send_ref[...])
    pieces = (p0, p1, p2, p3)
    count = q_ref.shape[1]
    kv_width = p0.shape[0] // 2

    def group(kv_head, carry):
        keys_turned = [head_rows(p, kv_head) for p in pieces]
        keys = [k.T for k in keys_turned]
        values = [head_rows(p, kv_head, kv_width).T for p in pieces]
        key_grads = [jnp.zeros((HEAD, count), F32) for _ in range(4)]
        value_grads = [jnp.zeros((HEAD, count), F32) for _ in range(4)]
        for member in range(GROUPS):
            head = kv_head * GROUPS + member
            query = head_rows(q_ref, head)
            grad = head_rows(do_ref, head)
            delta = jnp.sum(
                grad.astype(F32) * head_rows(o_ref, head).astype(F32), axis=0, keepdims=True
            )
            log_total = lse_ref[head]
            query_grad = jnp.zeros((HEAD, count), F32)
            for r in range(4):
                scores = dot(keys[r], query) + bias_ref[r * count : (r + 1) * count, :]
                probs = jnp.exp(scores - log_total)
                prob_grad = dot(values[r], grad)
                score_low = (probs * (prob_grad - delta)).astype(BF16)
                value_grads[r] = value_grads[r] + dot_back(grad, probs.astype(BF16))
                key_grads[r] = key_grads[r] + dot_back(query, score_low)
                query_grad = query_grad + dot(keys_turned[r], score_low)
            dq_ref[pl.ds(pl.multiple_of(head * HEAD, HEAD), HEAD), :] = rotate_back(
                query_grad * SCALE, tables
            ).astype(BF16)
        start = pl.multiple_of(kv_head * HEAD, HEAD)
        for r, ref in enumerate((kv_own_ref, kv_x_ref, kv_y_ref, kv_xy_ref)):
            ref[pl.ds(start, HEAD), :] = key_grads[r].astype(ref.dtype)
            place = pl.ds(pl.multiple_of(start + kv_width, HEAD), HEAD)
            ref[place, :] = value_grads[r].astype(ref.dtype)
        return carry

    lax.fori_loop(0, KV_HEADS, group, 0)
    own_ref[...], send_ref[...] = two_ways(dq_ref[...], resid_low.T)


def attend(inputs_low, projected, pieces, w_attn, bias):
    normed, queries, _ = projected
    width, rows = queries.shape
    left_own, left_send, log_total, resid, _ = local_call(
        attend_kernel,
        [
            jax.ShapeDtypeStruct((width, rows), BF16),
            jax.ShapeDtypeStruct((width, rows), BF16),
            jax.ShapeDtypeStruct((HEADS, 1, rows), F32),
            jax.ShapeDtypeStruct((rows, width), F32),
            jax.ShapeDtypeStruct((width, rows), BF16),
        ],
        queries,
        *pieces,
        bias,
        inputs_low,
        w_attn,
        normed,
    )
    lefts = (left_own, swap_cores(left_send), normed, swap_cores(normed))
    return resid, (inputs_low, queries, pieces, log_total, left_own, left_send, lefts)


def backward_scores(resid_grad, saved, w_attn, bias, tables):
    _, queries, pieces, log_total, left_own, left_send, _ = saved
    width, rows = queries.shape
    keys = pieces[0].shape
    return local_call(
        scores_back_kernel,
        [
            jax.ShapeDtypeStruct((width, rows), BF16),
            jax.ShapeDtypeStruct((width, rows), BF16),
            jax.ShapeDtypeStruct(keys, F32),
            jax.ShapeDtypeStruct(keys, BF16),
            jax.ShapeDtypeStruct(keys, BF16),
            jax.ShapeDtypeStruct(keys, BF16),
            jax.ShapeDtypeStruct((width, rows), BF16),
            jax.ShapeDtypeStruct((width, rows), BF16),
            jax.ShapeDtypeStruct((width, rows), BF16),
        ],
        resid_grad,
        w_attn,
        queries,
        *pieces,
        bias,
        log_total,
        left_own,
        left_send,
        *tables,
    )[:6]


def backward_project(resid_grad, rights, kv_own, flows, saved, w_attn, gain_attn, tables):
    inputs_low = saved[0]
    rows, width = inputs_low.shape
    kv_width = kv_own.shape[0] // 2

    def body(
        dr_ref, own, send, kv0, kv1, kv2, kv3, x_ref, w_ref, gain_ref, cos_ref, sin_ref,
        low_ref, gain_out, thin_own, thin_send,
    ):
        tables = cos_ref[...], sin_ref[...]
        kv = kv0[...]
        for ref in (kv1, kv2, kv3):
            kv = kv + ref[...].astype(F32)
        keys = rotate_back(kv[:kv_width], tables).astype(BF16)
        values = kv[kv_width:].astype(BF16)
        queries, _ = two_ways(own[...], send[...])
        thin_own[...], thin_send[...] = two_ways(keys, values)
        projected = jnp.concatenate([keys, values, queries], axis=0).T
        normed_grad = dot_back(projected, w_ref[:, : 2 * kv_width + width])
        part, gain_grad = normalize_back(
            x_ref[...].astype(F32), gain_ref[...], normed_grad
        )
        low_ref[...] = (dr_ref[...] + part).astype(BF16)
        gain_out[...] = gain_grad[None]

    low, gain_grad, thin_own, thin_send = local_call(
        body,
        [
            jax.ShapeDtypeStruct((rows, width), BF16),
            jax.ShapeDtypeStruct((1, width), F32),
            jax.ShapeDtypeStruct((kv_width, rows), BF16),
            jax.ShapeDtypeStruct((kv_width, rows), BF16),
        ],
        resid_grad,
        *rights,
        kv_own,
        *flows,
        inputs_low,
        w_attn,
        gain_attn[None],
        *tables,
    )
    return low, gain_grad[0], thin_own, thin_send


def shards(
    tokens, cotangent, doc_ids, w_query, w_keyval, w_out, w_gateup, w_down, gain_attn, gain_ffn
):
    core = lax.axis_index("pipe")
    ctx = lax.axis_index("ctx")
    zed = lax.axis_index("fsdp")
    on_first = core == 0
    rows = tokens.shape[2]
    width = tokens.shape[3]
    length = doc_ids.shape[2]
    kv_width = w_keyval.shape[2] // 2

    pieces = own_pieces(
        w_query[0], w_keyval[0], w_out[0], w_gateup[0], w_down[0], core, ctx
    )
    gains = jnp.concatenate([gain_attn, gain_ffn], axis=0)
    gains_other = swap_cores(gains)
    layer_gains = (pick(on_first, gains, gains_other), pick(on_first, gains_other, gains))

    doc_row = lax.dynamic_index_in_dim(doc_ids[:, 0], core, 0, keepdims=False)
    inputs_low = lax.dynamic_index_in_dim(tokens[:, 0], core, 0, keepdims=False)
    cotangent_own = lax.dynamic_index_in_dim(cotangent[:, 0], core, 0, keepdims=False)
    earlier = jnp.sum((doc_row[None, :] < doc_row[:, None]).astype(jnp.int32), axis=1)
    positions = jnp.arange(length, dtype=jnp.int32) - earlier
    token_pos = lax.dynamic_slice_in_dim(positions, ctx * rows, rows, 0)
    tables = angle_tables(token_pos.astype(F32))
    own_docs = lax.dynamic_slice_in_dim(doc_row, ctx * rows, rows, 0)
    query_index = ctx * rows + jnp.arange(rows, dtype=jnp.int32)
    key_docs = []
    key_index = []
    for mask in range(4):
        key_docs.append(lax.dynamic_slice_in_dim(doc_row, (ctx ^ mask) * rows, rows, 0))
        key_index.append((ctx ^ mask) * rows + jnp.arange(rows, dtype=jnp.int32))
    key_docs = jnp.concatenate(key_docs)
    key_index = jnp.concatenate(key_index)
    seen = (own_docs[None, :] == key_docs[:, None]) & (
        key_index[:, None] <= query_index[None, :]
    )
    bias = jnp.where(seen, 0.0, NEGATIVE).astype(F32)

    order = Order()
    (attn_first, ffn_first, down_first), (attn_second, ffn_second, down_second) = pieces
    tiles = w_gateup.shape[1] % 16 == 0
    split = attn_first.shape[0]
    attn0 = Spread(order, attn_first)
    ffn_first, down_first = order.waits((ffn_first, down_first))
    if tiles:
        down0 = Down(order, down_first)
    attn0.flights[0] = order.wait(attn0.flights[0])
    if tiles:
        ffn0 = Spread(order, ffn_first)
    attn0.advance()
    attn0.advance()
    if tiles:
        ffn0.advance()
    second = order.hold(jnp.concatenate([attn_second, ffn_second], axis=0))
    second = lax.all_gather(second, "fsdp", axis=0, tiled=False)
    attn0.advance()
    w_attn0 = order.wait(place_attn(attn0))
    own0 = project(inputs_low, w_attn0, layer_gains[0][0], tables)
    keys0 = send_keys(own0[2])
    keyval0 = (own0[2], *[order.wait(flow) for flow in keys0])
    if tiles:
        ffn0.advance()
        down0.start()
    resid0, attn_saved0 = attend(inputs_low, own0, keyval0, w_attn0, bias)
    resid0 = order.wait(resid0)
    second = order.wait(second)
    attn1 = Spread.behind(order, second[:, :split])
    attn1.advance()
    if tiles:
        down1 = Down(order, down_second)
        ffn0.advance()
        weights0 = Ffn(ffn0, down0.finish())
    else:
        weights0 = WholeFfn(w_gateup[0], w_down[0], 0)
        weights1 = WholeFfn(w_gateup[0], w_down[0], 1)
    middle, *ffn_saved0 = weights0.forward(resid0, layer_gains[0][1])
    middle = order.wait(middle)
    attn1.advance()
    if tiles:
        ffn1 = Spread.behind(order, second[:, split:])
        ffn1.advance()
    attn1.advance()
    w_attn1 = order.wait(place_attn(attn1))
    own1 = project(middle, w_attn1, layer_gains[1][0], tables)
    keys1 = send_keys(own1[2])
    keyval1 = (own1[2], *[order.wait(flow) for flow in keys1])
    if tiles:
        ffn1.advance()
        down1.start()
    resid1, attn_saved1 = attend(middle, own1, keyval1, w_attn1, bias)
    resid1 = order.wait(resid1)
    turned0 = [(array, order.wait(swap_cores(array))) for array in (ffn_saved0[0], ffn_saved0[3])]
    if tiles:
        ffn1.advance()
        weights1 = Ffn(ffn1, down1.finish())
    outputs1, *ffn_saved1 = weights1.forward(resid1, layer_gains[1][1])
    section_outs = [middle, outputs1]

    weights = [(w_attn0, weights0), (w_attn1, weights1)]
    saved = [(attn_saved0, (resid0, *ffn_saved0)), (attn_saved1, (resid1, *ffn_saved1))]
    half = -(-width // 256) * 128
    turned = [
        turned0,
        [(array, swap_cores(array)) for array in (ffn_saved1[0], ffn_saved1[3])],
    ]

    grad_low = cotangent_own
    input_grads = [None, None]
    reduced = [None, None]
    gain_grads = [None, None]
    above = None
    for layer in (1, 0):
        w_attn, w_ffn = weights[layer]
        attn_saved, ffn_saved = saved[layer]
        normed, hidden = turned[layer]
        grad_low = order.wait(grad_low)
        own, send = two_ways(grad_low[:, :half], grad_low[:, width - half :])
        down = Reduce(order, order.waits(term((*hidden, own, swap_cores(send), True))), True)
        resid_grad, gain_ffn_grad, own, send = w_ffn.backward(
            order.hold(grad_low), ffn_saved[0], layer_gains[layer][1], ffn_saved[2], ffn_saved[3]
        )
        resid_grad = order.wait(resid_grad)
        if above:
            above[1].advance()
            above[2].advance()
            above[0].settle()
        down.advance()
        gateup = Reduce(order, order.waits(term((*normed, own, swap_cores(send), True))), True)
        *rights, kv_own, kv_x, kv_y, kv_xy = backward_scores(
            resid_grad, attn_saved, w_attn, bias, tables
        )
        kv_own = order.wait(kv_own)
        if above:
            above[2].advance()
            above[1].settle()
        down.advance()
        flows = return_keys(order.hold(kv_x, kv_y, kv_xy))
        gateup.advance()
        flows = [order.wait(flow) for flow in flows]
        if above:
            above[2].settle()
        grad_low, gain_attn_grad, own, send = backward_project(
            resid_grad, rights, kv_own, flows, attn_saved, w_attn, layer_gains[layer][0], tables
        )
        gain_grads[layer] = (gain_attn_grad, gain_ffn_grad)
        gains = None
        if layer == 0:
            gains = jnp.stack([*gain_grads[0], *gain_grads[1]])
            gains = gains + swap_cores(gains)
            gains = pick(on_first, gains[:2], gains[2:])
        lefts = attn_saved[6]
        attn = Reduce(
            order,
            order.waits(
                term(
                    (*lefts[:2], rights[0], swap_cores(rights[1]), False),
                    (*lefts[2:], own, swap_cores(send), False),
                    gains=gains,
                )
            ),
            layer == 1,
            0 if gains is None else 16,
        )
        if layer == 1:
            above = [down, gateup, attn]
        reduced[layer] = [down, gateup, attn]
        input_grads[layer] = grad_low

    gateup.advance()

    def to_layers(first, second):
        own, other = two_ways(first, second)
        other = swap_cores(other)
        return two_ways(own, other)

    section_out = order.wait(jnp.stack(to_layers(section_outs[0], section_outs[1])))
    attn.advance()
    down.settle()
    section_in_grad = order.wait(jnp.stack(to_layers(input_grads[0], input_grads[1])))
    attn.advance()
    down_left, down_right = order.waits(to_layers(down.result, above[0].result))
    attn.advance()
    gain_total = attn.result[-16:-14, :width]
    attn_first, attn_second = to_layers(attn.result[:-16].astype(BF16), above[2].result)
    gateup.settle()
    gate, up = to_layers(gateup.result, above[1].result)
    attn_first, attn_second, gate, up, down_left, down_right = [
        array.astype(F32) for array in (attn_first, attn_second, gate, up, down_left, down_right)
    ]
    return (
        section_out[None, :, None],
        section_in_grad[None, :, None],
        attn_first[None, :, :width],
        jnp.concatenate([attn_first[:, width:], attn_second[:, width:]], axis=1)[None],
        attn_second[None, :, :width],
        jnp.concatenate([gate, up], axis=1)[None],
        jnp.concatenate(
            [down_left[:, : width // 2], down_right[:, half - width // 2 :]], axis=1
        )[None],
        gain_total[0][None],
        gain_total[1][None],
    )


def solution(mesh):
    return jax.shard_map(
        shards,
        mesh=mesh,
        in_specs=(
            P(None, "fsdp", "ctx", None),
            P(None, "fsdp", "ctx", None),
            P(None, "fsdp", None),
            P("pipe", "fsdp", None),
            P("pipe", "fsdp", None),
            P("pipe", "fsdp", None),
            P("pipe", "fsdp", None),
            P("pipe", "fsdp", None),
            P("pipe", None),
            P("pipe", None),
        ),
        out_specs=(
            P("pipe", None, "fsdp", "ctx", None),
            P("pipe", None, "fsdp", "ctx", None),
            P("pipe", ("ctx", "fsdp"), None),
            P("pipe", ("ctx", "fsdp"), None),
            P("pipe", ("ctx", "fsdp"), None),
            P("pipe", ("ctx", "fsdp"), None),
            P("pipe", ("ctx", "fsdp"), None),
            P("pipe", None),
            P("pipe", None),
        ),
        check_vma=False,
    )
```

```python
import functools
import math

import jax
import jax.numpy as jnp
from jax import lax
from jax.experimental import pallas as pl
from jax.experimental.pallas import tpu as pltpu
from jax.sharding import PartitionSpec as P

HEADS = 15
KV_HEADS = 5
HEAD = 64
GROUPS = HEADS // KV_HEADS
EPSILON = 1e-05
NEGATIVE = -1e30
SCALE = 1.0 / math.sqrt(HEAD)
F32 = jnp.float32
BF16 = jnp.bfloat16


def swap_cores(array):
    return lax.ppermute(array, "pipe", [(0, 1), (1, 0)])


def one_way(array, source, target):
    return lax.ppermute(array, "pipe", [(source, target)])


def across(array, axis, mask):
    count = lax.axis_size(axis)
    return lax.ppermute(array, axis, [(i, i ^ mask) for i in range(count)])


def pick(flag, first, second):
    return jnp.where(flag, first, second)


def two_ways(first, second):
    on_first = lax.axis_index("pipe") == 0
    return pick(on_first, first, second), pick(on_first, second, first)


class Order:
    def __init__(self):
        self.last = None

    def hold(self, *arrays):
        if self.last is not None:
            *arrays, _ = lax.optimization_barrier((*arrays, self.last))
        return arrays[0] if len(arrays) == 1 else tuple(arrays)

    def wait(self, array):
        array = self.hold(array)
        self.last = array
        return array

    def waits(self, arrays):
        arrays = self.hold(*arrays)
        self.last = arrays[0]
        return arrays


def first_way(array):
    pairs = [(c, c ^ 1) for c in range(4)] + [(4 + c, 4 + (c ^ 2)) for c in range(4)]
    return lax.ppermute(array, ("pipe", "ctx"), pairs)


def second_way(array):
    pairs = [(c, c ^ 2) for c in range(4)] + [(4 + c, 4 + (c ^ 1)) for c in range(4)]
    return lax.ppermute(array, ("pipe", "ctx"), pairs)


def dot(left, right):
    return jnp.dot(left, right, preferred_element_type=F32)


def dot_back(left, right):
    return lax.dot_general(left, right, (((1,), (1,)), ((), ())), preferred_element_type=F32)


def dot_rows(left, right):
    return lax.dot_general(left, right, (((0,), (0,)), ((), ())), preferred_element_type=F32)


def normalize(values, gain):
    return values * lax.rsqrt(jnp.mean(values * values, axis=-1, keepdims=True) + EPSILON) * gain


def normalize_back(values, gain, grad):
    inverse = lax.rsqrt(jnp.mean(values * values, axis=-1, keepdims=True) + EPSILON)
    unit = values * inverse
    gain_grad = jnp.sum(grad * unit, axis=0)
    scaled = grad * gain
    return inverse * (scaled - unit * jnp.mean(scaled * unit, axis=-1, keepdims=True)), gain_grad


def angle_tables(token_pos):
    half_size = HEAD // 2
    freqs = jnp.exp(jnp.arange(half_size, dtype=F32) * (-2.0 * math.log(100000.0) / HEAD))
    angles = freqs[:, None] * token_pos[None, :]
    cosine, sine = jnp.cos(angles), jnp.sin(angles)
    return jnp.concatenate([cosine, cosine], axis=0), jnp.concatenate([sine, sine], axis=0)


def rotate(values, tables):
    rows, cols = values.shape
    heads = values.reshape(rows // HEAD, HEAD, cols)
    half = HEAD // 2
    turned = jnp.concatenate([-heads[:, half:], heads[:, :half]], axis=1)
    return (heads * tables[0] + turned * tables[1]).reshape(rows, cols)


def rotate_back(values, tables):
    rows, cols = values.shape
    heads = values.reshape(rows // HEAD, HEAD, cols)
    half = HEAD // 2
    scaled = heads * tables[1]
    turned = jnp.concatenate([scaled[:, half:], -scaled[:, :half]], axis=1)
    return (heads * tables[0] + turned).reshape(rows, cols)


def z_masks():
    count = lax.axis_size("fsdp")
    masks = []
    while count > 1:
        count //= 2
        masks.append(count)
    return masks


class Spread:
    def __init__(self, order, own):
        self.order = order
        held = order.hold(own)[None]
        self.rank = [0]
        for mask in z_masks()[:-2]:
            held = jnp.concatenate([held, across(held, "fsdp", mask)], axis=0)
            self.rank = self.rank + [place ^ mask for place in self.rank]
        self.held = held
        self.flights = [across(held, "fsdp", mask) for mask in (1, 2, 3)]
        self.step = 0

    @classmethod
    def behind(cls, order, held):
        self = cls.__new__(cls)
        self.order, self.held, self.flights, self.rank = order, held, [], None
        self.step = 0
        return self

    def slot(self, number):
        return number if self.rank is None else lax.axis_index("fsdp") ^ self.rank[number]

    def collect(self):
        self.flights = [self.order.wait(flight) for flight in self.flights]

    def advance(self):
        self.step += 1
        if self.step == 1:
            self.collect()
            held = [self.held, *self.flights]
            if self.rank is not None:
                self.rank = [place ^ mask for mask in range(4) for place in self.rank]
            held = self.order.hold(jnp.concatenate(held, axis=0))
            self.flight = first_way(held)
            self.side = second_way(held)
            self.parts = [(held, swap_cores(held))]
        elif self.step == 2:
            got = self.order.wait(self.flight)
            side = self.order.wait(self.side)
            self.flight = second_way(got)
            self.parts.append((got, swap_cores(got)))
            self.parts.append((side, swap_cores(side)))
        else:
            got = self.order.wait(self.flight)
            self.parts.append((got, swap_cores(got)))

    def arrays(self):
        return [part[side] for side in range(2) for part in self.parts]


def place_attn(group):
    arrays = group.arrays()
    depth, rows, cols = arrays[0].shape
    zcount = lax.axis_size("fsdp")
    ccount = lax.axis_size("ctx")

    def body(*refs):
        out, sems = refs[8], refs[9]
        core, ctx = lax.axis_index("pipe"), lax.axis_index("ctx")
        copies = []
        for number in range(8):
            half = core if number < 4 else 1 - core
            mask = 0
            if number % 2 == 1:
                mask = mask ^ (1 + half)
            if number % 4 >= 2:
                mask = mask ^ (2 - half)
            col = pl.multiple_of((ctx ^ mask) * cols, cols)
            for slot in range(depth):
                copies.append(
                    pltpu.make_async_copy(
                        refs[number].at[slot],
                        out.at[group.slot(slot), half, :, pl.ds(col, cols)],
                        sems.at[len(copies)],
                    )
                )
        for copy in copies:
            copy.start()
        for copy in copies:
            copy.wait()

    out = pl.pallas_call(
        body,
        out_shape=jax.ShapeDtypeStruct((zcount, 2, rows, ccount * cols), BF16),
        in_specs=[pl.BlockSpec(memory_space=pl.ANY)] * 8,
        out_specs=pl.BlockSpec(memory_space=pltpu.VMEM),
        scratch_shapes=[pltpu.SemaphoreType.DMA((8 * depth,))],
        compiler_params=pltpu.CompilerParams(vmem_limit_bytes=40 * 1024 * 1024),
        cost_estimate=pl.CostEstimate(flops=0, bytes_accessed=0, transcendentals=0),
    )(*arrays)
    return out.reshape(-1, out.shape[-1])


def first_side(half, ctx):
    return pick(half == 0, ctx % 2, ctx // 2)


class Down:
    def __init__(self, order, piece):
        self.order = order
        self.flight = lax.all_gather(order.hold(piece), "fsdp", axis=0, tiled=False)

    def start(self):
        self.near = self.order.wait(self.flight)
        self.flight = first_way(self.near)
        self.near_other = swap_cores(self.near)

    def finish(self):
        far = self.order.wait(self.flight)
        return [self.near, far, self.near_other, swap_cores(far)]


class Ffn:
    def __init__(self, group, down):
        self.group = group
        self.arrays = group.arrays() + down
        self.depth, self.rows, self.cols = self.arrays[0].shape

    def scratch(self, rows):
        return [
            pltpu.VMEM((4, 2, self.depth * self.rows, self.cols), BF16),
            pltpu.VMEM((4, 2, 2, *self.arrays[8].shape[1:]), BF16),
            pltpu.SemaphoreType.DMA((4, 2 * self.depth)),
            pltpu.SemaphoreType.DMA((16,)),
            pltpu.VMEM((rows, self.arrays[8].shape[2]), F32),
        ]

    def start(self, refs, held, down, sems, down_sems):
        core, ctx = lax.axis_index("pipe"), lax.axis_index("ctx")
        blocks, quarters = [], []
        for number in range(4):
            copies = []
            other = 4 + (0, 2, 1, 3)[number]
            for side, half in ((number, core), (other, 1 - core)):
                for slot in range(self.depth):
                    row = pl.multiple_of(self.group.slot(slot) * self.rows, 16)
                    copies.append(
                        pltpu.make_async_copy(
                            refs[side].at[slot],
                            held.at[number, half, pl.ds(row, self.rows), :],
                            sems.at[number, len(copies)],
                        )
                    )
            blocks.append(copies)
            mask = (0, 1 + core, 2 - core, 3)[number]
            quarters.append(ctx ^ mask)
        downs = []
        for side, half in ((8, core), (9, core), (10, 1 - core), (11, 1 - core)):
            near = first_side(half, ctx)
            for zed in range(4):
                downs.append(
                    pltpu.make_async_copy(
                        refs[side].at[zed],
                        down.at[zed, half, near if side % 2 == 0 else 1 - near],
                        down_sems.at[len(downs)],
                    )
                )
        for copy in blocks[0] + downs + blocks[1] + blocks[2] + blocks[3]:
            copy.start()
        return blocks, quarters, downs

    def call(self, body, outs, *args):
        return pl.pallas_call(
            body,
            out_shape=outs,
            in_specs=[pl.BlockSpec(memory_space=pltpu.VMEM)] * len(args)
            + [pl.BlockSpec(memory_space=pl.ANY)] * 12,
            out_specs=[pl.BlockSpec(memory_space=pltpu.VMEM)] * len(outs),
            scratch_shapes=self.scratch(args[0].shape[0]),
            compiler_params=pltpu.CompilerParams(vmem_limit_bytes=48 * 1024 * 1024),
            cost_estimate=pl.CostEstimate(flops=0, bytes_accessed=0, transcendentals=0),
        )(*args, *self.arrays)

    def forward(self, resid, gain):
        rows, width = resid.shape
        cols = self.cols
        ffn = 4 * cols

        def body(r_ref, gain_ref, *refs):
            low_ref, normed_ref, gate_ref, up_ref, hidden_ref = refs[12:17]
            held, down, total = refs[17], refs[18], refs[21]
            blocks, quarters, downs = self.start(refs[:12], *refs[17:21])
            resid = r_ref[...]
            normed = normalize(resid, gain_ref[...]).astype(BF16)
            normed_ref[...] = normed.T
            total[...] = resid
            for number in range(4):
                for copy in blocks[number]:
                    copy.wait()
                gate = dot(normed, held[number, 0])
                up = dot(normed, held[number, 1])
                hidden = (gate / (1.0 + jnp.exp(-gate)) * up).astype(BF16)
                place = pl.ds(pl.multiple_of(quarters[number] * cols, cols), cols)
                gate_ref[:, place] = gate
                up_ref[:, place] = up
                hidden_ref[place, :] = hidden.T
                if number == 0:
                    for copy in downs:
                        copy.wait()
                weights = down[quarters[number]].reshape(cols, width)
                total[...] += dot(hidden, weights)
            low_ref[...] = total[...].astype(BF16)

        return self.call(
            body,
            [
                jax.ShapeDtypeStruct((rows, width), BF16),
                jax.ShapeDtypeStruct((width, rows), BF16),
                jax.ShapeDtypeStruct((rows, ffn), F32),
                jax.ShapeDtypeStruct((rows, ffn), F32),
                jax.ShapeDtypeStruct((ffn, rows), BF16),
            ],
            resid,
            gain[None],
        )

    def backward(self, grad_low, resid, gain, gate, up):
        rows, width = resid.shape
        cols = self.cols
        ffn = 4 * cols

        def body(grad_ref, r_ref, gain_ref, gate_ref, up_ref, *refs):
            out_ref, gain_out, gate_out, up_out, total = *refs[12:16], refs[20]
            held, down = refs[16:18]
            blocks, quarters, downs = self.start(refs[:12], *refs[16:20])
            grad = grad_ref[...]
            for number in range(4):
                place = pl.ds(pl.multiple_of(quarters[number] * cols, cols), cols)
                if number == 0:
                    for copy in downs:
                        copy.wait()
                weights = down[quarters[number]].reshape(cols, width)
                hidden_grad = dot_back(grad, weights)
                gate, up = gate_ref[:, place], up_ref[:, place]
                sig = 1.0 / (1.0 + jnp.exp(-gate))
                gate_grad = (hidden_grad * up * (sig * (1.0 + gate * (1.0 - sig)))).astype(BF16)
                up_grad = (hidden_grad * (gate * sig)).astype(BF16)
                own, other = two_ways(gate_grad, up_grad)
                gate_out[:, place] = own
                up_out[:, place] = other
                for copy in blocks[number]:
                    copy.wait()
                part = dot_back(gate_grad, held[number, 0]) + dot_back(up_grad, held[number, 1])
                if number == 0:
                    total[...] = part
                else:
                    total[...] += part
            resid_part, gain_grad = normalize_back(r_ref[...], gain_ref[...], total[...])
            out_ref[...] = grad.astype(F32) + resid_part
            gain_out[...] = gain_grad[None]

        outs = self.call(
            body,
            [
                jax.ShapeDtypeStruct((rows, width), F32),
                jax.ShapeDtypeStruct((1, width), F32),
                jax.ShapeDtypeStruct((rows, ffn), BF16),
                jax.ShapeDtypeStruct((rows, ffn), BF16),
            ],
            grad_low,
            resid,
            gain[None],
            gate,
            up,
        )
        return outs[0], outs[1][0], outs[2], outs[3]

    def both(self, resid, gain, grad_low):
        rows, width = resid.shape
        cols = self.cols
        ffn = 4 * cols

        def body(r_ref, gain_ref, grad_ref, *refs):
            low_ref, normed_ref, hidden_ref, out_ref, gain_out, own_ref, send_ref = refs[12:19]
            held, down, total = refs[19], refs[20], refs[23]
            blocks, quarters, downs = self.start(refs[:12], *refs[19:23])
            resid = r_ref[...]
            grad = grad_ref[...]
            normed = normalize(resid, gain_ref[...]).astype(BF16)
            normed_ref[...] = normed.T
            total[...] = resid
            normed_grad = jnp.zeros((rows, width), F32)
            for number in range(4):
                for copy in blocks[number]:
                    copy.wait()
                gate = dot(normed, held[number, 0])
                up = dot(normed, held[number, 1])
                sig = 1.0 / (1.0 + jnp.exp(-gate))
                act = gate / (1.0 + jnp.exp(-gate))
                hidden = (act * up).astype(BF16)
                place = pl.ds(pl.multiple_of(quarters[number] * cols, cols), cols)
                hidden_ref[place, :] = hidden.T
                if number == 0:
                    for copy in downs:
                        copy.wait()
                weights = down[quarters[number]].reshape(cols, width)
                total[...] += dot(hidden, weights)
                hidden_grad = dot_back(grad, weights)
                gate_grad = (hidden_grad * up * (sig * (1.0 + gate * (1.0 - sig)))).astype(BF16)
                up_grad = (hidden_grad * act).astype(BF16)
                own_ref[:, place], send_ref[:, place] = two_ways(gate_grad, up_grad)
                part = dot_back(gate_grad, held[number, 0]) + dot_back(up_grad, held[number, 1])
                normed_grad = normed_grad + part
            low_ref[...] = total[...].astype(BF16)
            resid_part, gain_grad = normalize_back(r_ref[...], gain_ref[...], normed_grad)
            out_ref[...] = grad.astype(F32) + resid_part
            gain_out[...] = gain_grad[None]

        outs = self.call(
            body,
            [
                jax.ShapeDtypeStruct((rows, width), BF16),
                jax.ShapeDtypeStruct((width, rows), BF16),
                jax.ShapeDtypeStruct((ffn, rows), BF16),
                jax.ShapeDtypeStruct((rows, width), F32),
                jax.ShapeDtypeStruct((1, width), F32),
                jax.ShapeDtypeStruct((rows, ffn), BF16),
                jax.ShapeDtypeStruct((rows, ffn), BF16),
            ],
            resid,
            gain[None],
            grad_low,
        )
        return outs[:3], (outs[3], outs[4][0], outs[5], outs[6])


class WholeFfn:
    def __init__(self, w_gateup, w_down, layer):
        core = lax.axis_index("pipe")
        whole = []
        for array in (w_gateup, w_down):
            mine = lax.all_gather(array, "fsdp", axis=0, tiled=True)
            whole.append(pick(core == layer, mine, swap_cores(mine)))
        self.w_gateup, self.w_down = whole

    def forward(self, resid, gain):
        normed = normalize(resid, gain).astype(BF16)
        gated = dot(normed, self.w_gateup)
        ffn = gated.shape[1] // 2
        gate, up = gated[:, :ffn], gated[:, ffn:]
        hidden = (gate / (1.0 + jnp.exp(-gate)) * up).astype(BF16)
        outputs = (resid + dot(hidden, self.w_down)).astype(BF16)
        return outputs, normed.T, gate, up, hidden.T

    def both(self, resid, gain, grad_low):
        outputs, normed, gate, up, hidden = self.forward(resid, gain)
        return (outputs, normed, hidden), self.backward(grad_low, resid, gain, gate, up)

    def backward(self, grad_low, resid, gain, gate, up):
        ffn = gate.shape[1]
        hidden_grad = dot_back(grad_low, self.w_down)
        sig = 1.0 / (1.0 + jnp.exp(-gate))
        gate_grad = (hidden_grad * up * (sig * (1.0 + gate * (1.0 - sig)))).astype(BF16)
        up_grad = (hidden_grad * (gate * sig)).astype(BF16)
        normed_grad = dot_back(gate_grad, self.w_gateup[:, :ffn]) + dot_back(
            up_grad, self.w_gateup[:, ffn:]
        )
        resid_part, gain_grad = normalize_back(resid, gain, normed_grad)
        own, other = two_ways(gate_grad, up_grad)
        return grad_low.astype(F32) + resid_part, gain_grad, own, other


def own_pieces(w_query, w_keyval, w_out, w_gateup, w_down, core, ctx):
    sources = (w_keyval, w_query, w_out)
    rows = w_query.shape[0] // 2
    cols = sum(source.shape[1] for source in sources) // 4
    ffn = w_gateup.shape[1] // 2
    depth = w_down.shape[0] // 2

    def quarter(number):
        found, place = [], 0
        for source in sources:
            start = max(number * cols - place, 0)
            stop = min((number + 1) * cols - place, source.shape[1])
            if start < stop:
                found.append(source[:, start:stop])
            place += source.shape[1]
        return found[0] if len(found) == 1 else jnp.concatenate(found, axis=1)

    attn = pick(
        ctx < 2, pick(ctx == 0, quarter(0), quarter(1)), pick(ctx == 2, quarter(2), quarter(3))
    )
    attn_parts = two_ways(attn[:rows], attn[rows:])

    def parts(half, attn_part):
        return (
            attn_part,
            lax.dynamic_slice(w_gateup, (0, half * ffn + ctx * cols), (2 * rows, cols)),
            lax.dynamic_slice_in_dim(
                w_down, half * depth + first_side(half, ctx) * (depth // 2), depth // 2, 0
            ),
        )

    kept = parts(core, attn_parts[0])
    received = [swap_cores(piece) for piece in parts(1 - core, attn_parts[1])]
    first = [pick(core == 0, a, b) for a, b in zip(kept, received)]
    second = [pick(core == 0, b, a) for a, b in zip(kept, received)]
    return first, second


def add_low(kept, received):
    return (kept.astype(F32) + received.astype(F32)).astype(BF16)


def term(*pairs, gains=None):
    rows = pairs[0][0].shape[0]
    deep = rows // 4
    widths = [pair[2].shape[1] if pair[4] else pair[2].shape[0] for pair in pairs]

    def body(*refs):
        sent_ref, kept_ref = refs[-2:]
        core, ctx = lax.axis_index("pipe"), lax.axis_index("ctx")
        y, x = ctx // 2, ctx % 2
        for out, xx, yy in ((sent_ref, 1 - x, 1 - y), (kept_ref, x, y)):
            for side in range(2):
                block = jnp.where(core == 0, xx + 2 * side, 2 * yy + side)
                place = pl.ds(pl.multiple_of(block * deep, 16), deep)
                offset = 0
                for number, pair in enumerate(pairs):
                    lefts = [ref[place, :] for ref in refs[4 * number : 4 * number + 2]]
                    rights = refs[4 * number + 2 : 4 * number + 4]
                    for start in range(0, widths[number], 640):
                        stop = min(start + 640, widths[number])
                        total = None
                        for left, right in zip(lefts, rights):
                            if pair[4]:
                                part = dot(left, right[:, start:stop])
                            else:
                                part = dot_back(left, right[start:stop, :])
                            total = part if total is None else total + part
                        out[side, :deep, offset + start : offset + stop] = total.astype(BF16)
                    offset += widths[number]
                if gains is not None:
                    out[side, deep:, :] = refs[-3][...]

    extra = []
    if gains is not None:
        low = gains.astype(BF16)
        extra = [jnp.pad(low, ((0, 16 - low.shape[0]), (0, sum(widths) - low.shape[1])))]
    shape = jax.ShapeDtypeStruct((2, deep + 16 * len(extra), sum(widths)), BF16)
    arrays = [array for pair in pairs for array in pair[:4]]
    return local_call(body, [shape, shape], *arrays, *extra)


class Reduce:
    def __init__(self, order, term, offload=False, extra=0):
        self.order = order
        self.extra = extra
        self.offload = offload
        core, ctx, self.zed = lax.axis_index("pipe"), lax.axis_index("ctx"), lax.axis_index("fsdp")
        self.side = pick(core == 0, ctx // 2, ctx % 2)
        self.step = 0
        self.result = None
        sent, kept = term
        self.kept = [kept]
        self.flights = [first_way(sent)]

    def land(self):
        parts = self.kept + [self.order.wait(flight) for flight in self.flights]
        return sum(part.astype(F32) for part in parts)

    def advance(self):
        if self.result is not None:
            return
        index = lax.dynamic_index_in_dim
        self.step += 1
        if self.step == 1:
            parts = self.kept + [self.order.wait(flight) for flight in self.flights]
            sent = sum(index(part, 1 - self.side, 0, False).astype(F32) for part in parts)
            self.kept = [index(part, self.side, 0, False) for part in parts]
            self.flights = [second_way(self.order.wait(sent.astype(BF16)))]
            return
        total = self.land()
        if self.step == 3:
            self.result = total
            return
        low = total.astype(BF16)
        if self.offload:
            count = lax.axis_size("fsdp")
            parts = low.reshape(count, low.shape[0] // count, low.shape[1])
            parts = self.order.wait(parts)
            self.result = lax.psum_scatter(parts, "fsdp", scatter_dimension=0, tiled=False)
            return
        deep = low.shape[0] - self.extra
        body, tail = low[:deep], low[deep:]
        for mask in z_masks()[:-2]:
            half = body.shape[0] // 2
            high = (self.zed & mask) != 0
            self.kept = [jnp.concatenate([pick(high, body[half:], body[:half]), tail], axis=0)]
            sent = jnp.concatenate([pick(high, body[:half], body[half:]), tail], axis=0)
            self.flights = [across(sent, "fsdp", mask)]
            low = self.land().astype(BF16)
            body, tail = low[:half], low[half:]
        parts = body.reshape(4, body.shape[0] // 4, body.shape[1])
        if self.extra:
            tails = jnp.broadcast_to(tail, (4, *tail.shape))
            parts = jnp.concatenate([parts, tails], axis=1)
        here = self.zed % 4
        self.kept = [index(parts, here, 0, False)]
        sent = [index(parts, here ^ mask, 0, False) for mask in (3, 2, 1)]
        sent = self.order.waits(sent)
        self.flights = [across(block, "fsdp", mask) for block, mask in zip(sent, (3, 2, 1))]

    def settle(self):
        self.result = self.order.wait(self.result)


def send_keys(keyval):
    flows = []
    for mask in (3, 1, 2):
        flows.append(across(keyval, "ctx", mask))
    return flows[1], flows[2], flows[0]


def return_keys(parts):
    return [across(part, "ctx", mask) for part, mask in zip(parts, (1, 2, 3))]


def local_call(kernel, outs, *args):
    return pl.pallas_call(
        kernel,
        out_shape=outs,
        in_specs=[pl.BlockSpec(memory_space=pltpu.VMEM)] * len(args),
        out_specs=[pl.BlockSpec(memory_space=pltpu.VMEM)] * len(outs),
        compiler_params=pltpu.CompilerParams(vmem_limit_bytes=48 * 1024 * 1024),
        cost_estimate=pl.CostEstimate(flops=0, bytes_accessed=0, transcendentals=0),
    )(*args)


def project(inputs_low, w_attn, gain_attn, tables):
    rows, width = inputs_low.shape
    kv_width = (w_attn.shape[1] - 2 * width) // 2

    def body(x_ref, w_ref, gain_ref, cos_ref, sin_ref, normed_ref, q_ref, kv_ref):
        tables = cos_ref[...], sin_ref[...]
        normed = normalize(x_ref[...].astype(F32), gain_ref[...]).astype(BF16)
        normed_ref[...] = normed.T
        projected = dot(normed, w_ref[:, : 2 * kv_width + width]).T
        kv_ref[:kv_width, :] = rotate(projected[:kv_width], tables).astype(BF16)
        kv_ref[kv_width:, :] = projected[kv_width : 2 * kv_width].astype(BF16)
        queries = rotate(projected[2 * kv_width :], tables).astype(BF16)
        q_ref[...] = (queries.astype(F32) * SCALE).astype(BF16)

    return local_call(
        body,
        [
            jax.ShapeDtypeStruct((width, rows), BF16),
            jax.ShapeDtypeStruct((width, rows), BF16),
            jax.ShapeDtypeStruct((2 * kv_width, rows), BF16),
        ],
        inputs_low,
        w_attn,
        gain_attn[None],
        *tables,
    )


def head_rows(ref, head, offset=0):
    return ref[pl.ds(pl.multiple_of(head * HEAD + offset, HEAD), HEAD), :]


def attend_kernel(
    q_ref, p0, p1, p2, p3, bias_ref, x_ref, w_ref, normed_ref, own_ref, send_ref, lse_ref, r_ref, o_ref
):
    pieces = (p0, p1, p2, p3)
    count = q_ref.shape[1]
    kv_width = p0.shape[0] // 2
    ones = jnp.ones((16, count), BF16)

    def group(kv_head, carry):
        keys = [head_rows(p, kv_head).T for p in pieces]
        values = [
            jnp.concatenate([head_rows(p, kv_head, kv_width), ones], axis=0) for p in pieces
        ]
        for member in range(GROUPS):
            head = kv_head * GROUPS + member
            query = head_rows(q_ref, head)
            scores = [
                dot(keys[r], query) + bias_ref[r * count : (r + 1) * count, :] for r in range(4)
            ]
            top = jnp.maximum(
                jnp.maximum(scores[0], scores[1]), jnp.maximum(scores[2], scores[3])
            )
            top = jnp.max(top, axis=0, keepdims=True)
            total = jnp.zeros((HEAD + 16, count), F32)
            for r in range(4):
                total = total + dot(values[r], jnp.exp(scores[r] - top).astype(BF16))
            summed = total[HEAD : HEAD + 1]
            o_ref[pl.ds(pl.multiple_of(head * HEAD, HEAD), HEAD), :] = (
                total[:HEAD] / summed
            ).astype(BF16)
            lse_ref[head] = top + jnp.log(summed)
        return carry

    lax.fori_loop(0, KV_HEADS, group, 0)
    attended = o_ref[...]
    own_ref[...], send_ref[...] = two_ways(normed_ref[...], attended)
    width = attended.shape[0]
    r_ref[...] = x_ref[...].astype(F32) + dot(
        attended.T, w_ref[:, w_ref.shape[1] - width :]
    )


def scores_back_kernel(
    dr_ref,
    w_ref,
    q_ref,
    p0,
    p1,
    p2,
    p3,
    bias_ref,
    lse_ref,
    left_own_ref,
    left_send_ref,
    cos_ref,
    sin_ref,
    own_ref,
    send_ref,
    kv_own_ref,
    kv_x_ref,
    kv_y_ref,
    kv_xy_ref,
    do_ref,
    o_ref,
    dq_ref,
):
    tables = cos_ref[...], sin_ref[...]
    width = q_ref.shape[0]
    resid_low = dr_ref[...].astype(BF16)
    do_ref[...] = dot_back(w_ref[:, w_ref.shape[1] - width :], resid_low).astype(BF16)
    _, o_ref[...] = two_ways(left_own_ref[...], left_send_ref[...])
    pieces = (p0, p1, p2, p3)
    count = q_ref.shape[1]
    kv_width = p0.shape[0] // 2

    def group(kv_head, carry):
        keys_turned = [head_rows(p, kv_head) for p in pieces]
        keys = [k.T for k in keys_turned]
        values = [head_rows(p, kv_head, kv_width).T for p in pieces]
        key_grads = [jnp.zeros((HEAD, count), F32) for _ in range(4)]
        value_grads = [jnp.zeros((HEAD, count), F32) for _ in range(4)]
        for member in range(GROUPS):
            head = kv_head * GROUPS + member
            query = head_rows(q_ref, head)
            grad = head_rows(do_ref, head)
            delta = jnp.sum(
                grad.astype(F32) * head_rows(o_ref, head).astype(F32), axis=0, keepdims=True
            )
            log_total = lse_ref[head]
            query_grad = jnp.zeros((HEAD, count), F32)
            for r in range(4):
                scores = dot(keys[r], query) + bias_ref[r * count : (r + 1) * count, :]
                probs = jnp.exp(scores - log_total)
                prob_grad = dot(values[r], grad)
                score_low = (probs * (prob_grad - delta)).astype(BF16)
                value_grads[r] = value_grads[r] + dot_back(grad, probs.astype(BF16))
                key_grads[r] = key_grads[r] + dot_back(query, score_low)
                query_grad = query_grad + dot(keys_turned[r], score_low)
            dq_ref[pl.ds(pl.multiple_of(head * HEAD, HEAD), HEAD), :] = rotate_back(
                query_grad * SCALE, tables
            ).astype(BF16)
        start = pl.multiple_of(kv_head * HEAD, HEAD)
        for r, ref in enumerate((kv_own_ref, kv_x_ref, kv_y_ref, kv_xy_ref)):
            ref[pl.ds(start, HEAD), :] = key_grads[r].astype(ref.dtype)
            place = pl.ds(pl.multiple_of(start + kv_width, HEAD), HEAD)
            ref[place, :] = value_grads[r].astype(ref.dtype)
        return carry

    lax.fori_loop(0, KV_HEADS, group, 0)
    own_ref[...], send_ref[...] = two_ways(dq_ref[...], resid_low.T)


def attend(inputs_low, projected, pieces, w_attn, bias):
    normed, queries, _ = projected
    width, rows = queries.shape
    left_own, left_send, log_total, resid, _ = local_call(
        attend_kernel,
        [
            jax.ShapeDtypeStruct((width, rows), BF16),
            jax.ShapeDtypeStruct((width, rows), BF16),
            jax.ShapeDtypeStruct((HEADS, 1, rows), F32),
            jax.ShapeDtypeStruct((rows, width), F32),
            jax.ShapeDtypeStruct((width, rows), BF16),
        ],
        queries,
        *pieces,
        bias,
        inputs_low,
        w_attn,
        normed,
    )
    lefts = (left_own, swap_cores(left_send), normed, swap_cores(normed))
    return resid, (inputs_low, queries, pieces, log_total, left_own, left_send, lefts)


def backward_scores(resid_grad, saved, w_attn, bias, tables):
    _, queries, pieces, log_total, left_own, left_send, _ = saved
    width, rows = queries.shape
    keys = pieces[0].shape
    return local_call(
        scores_back_kernel,
        [
            jax.ShapeDtypeStruct((width, rows), BF16),
            jax.ShapeDtypeStruct((width, rows), BF16),
            jax.ShapeDtypeStruct(keys, F32),
            jax.ShapeDtypeStruct(keys, BF16),
            jax.ShapeDtypeStruct(keys, BF16),
            jax.ShapeDtypeStruct(keys, BF16),
            jax.ShapeDtypeStruct((width, rows), BF16),
            jax.ShapeDtypeStruct((width, rows), BF16),
            jax.ShapeDtypeStruct((width, rows), BF16),
        ],
        resid_grad,
        w_attn,
        queries,
        *pieces,
        bias,
        log_total,
        left_own,
        left_send,
        *tables,
    )[:6]


def backward_project(resid_grad, rights, kv_own, flows, saved, w_attn, gain_attn, tables):
    inputs_low = saved[0]
    rows, width = inputs_low.shape
    kv_width = kv_own.shape[0] // 2

    def body(
        dr_ref, own, send, kv0, kv1, kv2, kv3, x_ref, w_ref, gain_ref, cos_ref, sin_ref,
        low_ref, gain_out, thin_own, thin_send,
    ):
        tables = cos_ref[...], sin_ref[...]
        kv = kv0[...]
        for ref in (kv1, kv2, kv3):
            kv = kv + ref[...].astype(F32)
        keys = rotate_back(kv[:kv_width], tables).astype(BF16)
        values = kv[kv_width:].astype(BF16)
        queries, _ = two_ways(own[...], send[...])
        thin_own[...], thin_send[...] = two_ways(keys, values)
        projected = jnp.concatenate([keys, values, queries], axis=0).T
        normed_grad = dot_back(projected, w_ref[:, : 2 * kv_width + width])
        part, gain_grad = normalize_back(
            x_ref[...].astype(F32), gain_ref[...], normed_grad
        )
        low_ref[...] = (dr_ref[...] + part).astype(BF16)
        gain_out[...] = gain_grad[None]

    low, gain_grad, thin_own, thin_send = local_call(
        body,
        [
            jax.ShapeDtypeStruct((rows, width), BF16),
            jax.ShapeDtypeStruct((1, width), F32),
            jax.ShapeDtypeStruct((kv_width, rows), BF16),
            jax.ShapeDtypeStruct((kv_width, rows), BF16),
        ],
        resid_grad,
        *rights,
        kv_own,
        *flows,
        inputs_low,
        w_attn,
        gain_attn[None],
        *tables,
    )
    return low, gain_grad[0], thin_own, thin_send


def shards(
    tokens, cotangent, doc_ids, w_query, w_keyval, w_out, w_gateup, w_down, gain_attn, gain_ffn
):
    core = lax.axis_index("pipe")
    ctx = lax.axis_index("ctx")
    zed = lax.axis_index("fsdp")
    on_first = core == 0
    rows = tokens.shape[2]
    width = tokens.shape[3]
    length = doc_ids.shape[2]
    kv_width = w_keyval.shape[2] // 2

    pieces = own_pieces(
        w_query[0], w_keyval[0], w_out[0], w_gateup[0], w_down[0], core, ctx
    )
    gains = jnp.concatenate([gain_attn, gain_ffn], axis=0)
    gains_other = swap_cores(gains)
    layer_gains = (pick(on_first, gains, gains_other), pick(on_first, gains_other, gains))

    doc_row = lax.dynamic_index_in_dim(doc_ids[:, 0], core, 0, keepdims=False)
    inputs_low = lax.dynamic_index_in_dim(tokens[:, 0], core, 0, keepdims=False)
    cotangent_own = lax.dynamic_index_in_dim(cotangent[:, 0], core, 0, keepdims=False)
    earlier = jnp.sum((doc_row[None, :] < doc_row[:, None]).astype(jnp.int32), axis=1)
    positions = jnp.arange(length, dtype=jnp.int32) - earlier
    token_pos = lax.dynamic_slice_in_dim(positions, ctx * rows, rows, 0)
    tables = angle_tables(token_pos.astype(F32))
    own_docs = lax.dynamic_slice_in_dim(doc_row, ctx * rows, rows, 0)
    query_index = ctx * rows + jnp.arange(rows, dtype=jnp.int32)
    key_docs = []
    key_index = []
    for mask in range(4):
        key_docs.append(lax.dynamic_slice_in_dim(doc_row, (ctx ^ mask) * rows, rows, 0))
        key_index.append((ctx ^ mask) * rows + jnp.arange(rows, dtype=jnp.int32))
    key_docs = jnp.concatenate(key_docs)
    key_index = jnp.concatenate(key_index)
    seen = (own_docs[None, :] == key_docs[:, None]) & (
        key_index[:, None] <= query_index[None, :]
    )
    bias = jnp.where(seen, 0.0, NEGATIVE).astype(F32)

    order = Order()
    (attn_first, ffn_first, down_first), (attn_second, ffn_second, down_second) = pieces
    tiles = w_gateup.shape[1] % 16 == 0
    split = attn_first.shape[0]
    attn0 = Spread(order, attn_first)
    ffn_first, down_first = order.waits((ffn_first, down_first))
    if tiles:
        down0 = Down(order, down_first)
    attn0.flights[0] = order.wait(attn0.flights[0])
    if tiles:
        ffn0 = Spread(order, ffn_first)
    attn0.advance()
    attn0.advance()
    if tiles:
        ffn0.advance()
    second = order.hold(jnp.concatenate([attn_second, ffn_second], axis=0))
    second = lax.all_gather(second, "fsdp", axis=0, tiled=False)
    attn0.advance()
    w_attn0 = order.wait(place_attn(attn0))
    own0 = project(inputs_low, w_attn0, layer_gains[0][0], tables)
    keys0 = send_keys(own0[2])
    keyval0 = (own0[2], *[order.wait(flow) for flow in keys0])
    if tiles:
        ffn0.advance()
        down0.start()
    resid0, attn_saved0 = attend(inputs_low, own0, keyval0, w_attn0, bias)
    resid0 = order.wait(resid0)
    second = order.wait(second)
    attn1 = Spread.behind(order, second[:, :split])
    attn1.advance()
    if tiles:
        down1 = Down(order, down_second)
        ffn0.advance()
        weights0 = Ffn(ffn0, down0.finish())
    else:
        weights0 = WholeFfn(w_gateup[0], w_down[0], 0)
        weights1 = WholeFfn(w_gateup[0], w_down[0], 1)
    middle, *ffn_saved0 = weights0.forward(resid0, layer_gains[0][1])
    middle = order.wait(middle)
    attn1.advance()
    if tiles:
        ffn1 = Spread.behind(order, second[:, split:])
        ffn1.advance()
    attn1.advance()
    w_attn1 = order.wait(place_attn(attn1))
    own1 = project(middle, w_attn1, layer_gains[1][0], tables)
    keys1 = send_keys(own1[2])
    keyval1 = (own1[2], *[order.wait(flow) for flow in keys1])
    if tiles:
        ffn1.advance()
        down1.start()
    resid1, attn_saved1 = attend(middle, own1, keyval1, w_attn1, bias)
    resid1 = order.wait(resid1)
    turned0 = [(array, order.wait(swap_cores(array))) for array in (ffn_saved0[0], ffn_saved0[3])]
    if tiles:
        ffn1.advance()
        weights1 = Ffn(ffn1, down1.finish())
    (outputs1, normed1, hidden1), back1 = weights1.both(
        resid1, layer_gains[1][1], cotangent_own
    )
    section_outs = [middle, outputs1]

    weights = [(w_attn0, weights0), (w_attn1, weights1)]
    saved = [(attn_saved0, (resid0, *ffn_saved0)), (attn_saved1, None)]
    half = -(-width // 256) * 128
    turned = [
        turned0,
        [(array, swap_cores(array)) for array in (normed1, hidden1)],
    ]

    grad_low = cotangent_own
    input_grads = [None, None]
    reduced = [None, None]
    gain_grads = [None, None]
    above = None
    for layer in (1, 0):
        w_attn, w_ffn = weights[layer]
        attn_saved, ffn_saved = saved[layer]
        normed, hidden = turned[layer]
        grad_low = order.wait(grad_low)
        own, send = two_ways(grad_low[:, :half], grad_low[:, width - half :])
        down = Reduce(order, order.waits(term((*hidden, own, swap_cores(send), True))), True)
        if layer == 1:
            resid_grad, gain_ffn_grad, own, send = back1
        else:
            resid_grad, gain_ffn_grad, own, send = w_ffn.backward(
                order.hold(grad_low),
                ffn_saved[0],
                layer_gains[layer][1],
                ffn_saved[2],
                ffn_saved[3],
            )
        resid_grad = order.wait(resid_grad)
        if layer == 0:
            above[1].advance()
            above[2].advance()
            above[0].settle()
            down.advance()
            gateup = Reduce(order, order.waits(term((*normed, own, swap_cores(send), True))), True)
        *rights, kv_own, kv_x, kv_y, kv_xy = backward_scores(
            resid_grad, attn_saved, w_attn, bias, tables
        )
        kv_own = order.wait(kv_own)
        if layer == 0:
            above[1].advance()
            above[2].advance()
            down.advance()
        flows = return_keys(order.hold(kv_x, kv_y, kv_xy))
        if layer == 1:
            gateup_term = order.waits(term((*normed, own, swap_cores(send), True)))
            flows = [order.wait(flow) for flow in flows]
            gateup = Reduce(order, order.hold(*gateup_term), True)
            down.advance()
        else:
            gateup.advance()
            flows = [order.wait(flow) for flow in flows]
            above[1].settle()
        grad_low, gain_attn_grad, own, send = backward_project(
            resid_grad, rights, kv_own, flows, attn_saved, w_attn, layer_gains[layer][0], tables
        )
        gain_grads[layer] = (gain_attn_grad, gain_ffn_grad)
        gains = None
        if layer == 0:
            grad_low = order.wait(grad_low)
            above[2].settle()
            gains = jnp.stack([*gain_grads[0], *gain_grads[1]])
            gains = gains + swap_cores(gains)
            gains = pick(on_first, gains[:2], gains[2:])
        lefts = attn_saved[6]
        attn = Reduce(
            order,
            order.waits(
                term(
                    (*lefts[:2], rights[0], swap_cores(rights[1]), False),
                    (*lefts[2:], own, swap_cores(send), False),
                    gains=gains,
                )
            ),
            layer == 1,
            0 if gains is None else 16,
        )
        if layer == 1:
            down.advance()
            above = [down, gateup, attn]
        reduced[layer] = [down, gateup, attn]
        input_grads[layer] = grad_low

    down.settle()
    gateup.advance()

    def to_layers(first, second):
        own, other = two_ways(first, second)
        other = swap_cores(other)
        return two_ways(own, other)

    section_out = order.wait(jnp.stack(to_layers(section_outs[0], section_outs[1])))
    attn.advance()
    section_in_grad = order.wait(jnp.stack(to_layers(input_grads[0], input_grads[1])))
    attn.advance()
    down_left, down_right = order.waits(to_layers(down.result, above[0].result))
    attn.advance()
    gain_total = attn.result[-16:-14, :width]
    attn_first, attn_second = to_layers(attn.result[:-16].astype(BF16), above[2].result)
    gateup.settle()
    gate, up = to_layers(gateup.result, above[1].result)
    attn_first, attn_second, gate, up, down_left, down_right = [
        array.astype(F32) for array in (attn_first, attn_second, gate, up, down_left, down_right)
    ]
    return (
        section_out[None, :, None],
        section_in_grad[None, :, None],
        attn_first[None, :, :width],
        jnp.concatenate([attn_first[:, width:], attn_second[:, width:]], axis=1)[None],
        attn_second[None, :, :width],
        jnp.concatenate([gate, up], axis=1)[None],
        jnp.concatenate(
            [down_left[:, : width // 2], down_right[:, half - width // 2 :]], axis=1
        )[None],
        gain_total[0][None],
        gain_total[1][None],
    )


def solution(mesh):
    return jax.shard_map(
        shards,
        mesh=mesh,
        in_specs=(
            P(None, "fsdp", "ctx", None),
            P(None, "fsdp", "ctx", None),
            P(None, "fsdp", None),
            P("pipe", "fsdp", None),
            P("pipe", "fsdp", None),
            P("pipe", "fsdp", None),
            P("pipe", "fsdp", None),
            P("pipe", "fsdp", None),
            P("pipe", None),
            P("pipe", None),
        ),
        out_specs=(
            P("pipe", None, "fsdp", "ctx", None),
            P("pipe", None, "fsdp", "ctx", None),
            P("pipe", ("ctx", "fsdp"), None),
            P("pipe", ("ctx", "fsdp"), None),
            P("pipe", ("ctx", "fsdp"), None),
            P("pipe", ("ctx", "fsdp"), None),
            P("pipe", ("ctx", "fsdp"), None),
            P("pipe", None),
            P("pipe", None),
        ),
        check_vma=False,
    )
```

```python
import functools
import math

import jax
import jax.numpy as jnp
from jax import lax
from jax.experimental import pallas as pl
from jax.experimental.pallas import tpu as pltpu
from jax.sharding import PartitionSpec as P

HEADS = 15
KV_HEADS = 5
HEAD = 64
GROUPS = HEADS // KV_HEADS
EPSILON = 1e-05
NEGATIVE = -1e30
SCALE = 1.0 / math.sqrt(HEAD)
F32 = jnp.float32
BF16 = jnp.bfloat16


def swap_cores(array):
    return lax.ppermute(array, "pipe", [(0, 1), (1, 0)])


def one_way(array, source, target):
    return lax.ppermute(array, "pipe", [(source, target)])


def across(array, axis, mask):
    count = lax.axis_size(axis)
    return lax.ppermute(array, axis, [(i, i ^ mask) for i in range(count)])


def pick(flag, first, second):
    return jnp.where(flag, first, second)


def two_ways(first, second):
    on_first = lax.axis_index("pipe") == 0
    return pick(on_first, first, second), pick(on_first, second, first)


class Order:
    def __init__(self):
        self.last = None

    def hold(self, *arrays):
        if self.last is not None:
            *arrays, _ = lax.optimization_barrier((*arrays, self.last))
        return arrays[0] if len(arrays) == 1 else tuple(arrays)

    def wait(self, array):
        array = self.hold(array)
        self.last = array
        return array

    def waits(self, arrays):
        arrays = self.hold(*arrays)
        self.last = arrays[0]
        return arrays


def first_way(array):
    pairs = [(c, c ^ 1) for c in range(4)] + [(4 + c, 4 + (c ^ 2)) for c in range(4)]
    return lax.ppermute(array, ("pipe", "ctx"), pairs)


def second_way(array):
    pairs = [(c, c ^ 2) for c in range(4)] + [(4 + c, 4 + (c ^ 1)) for c in range(4)]
    return lax.ppermute(array, ("pipe", "ctx"), pairs)


def dot(left, right):
    return jnp.dot(left, right, preferred_element_type=F32)


def dot_back(left, right):
    return lax.dot_general(left, right, (((1,), (1,)), ((), ())), preferred_element_type=F32)


def dot_rows(left, right):
    return lax.dot_general(left, right, (((0,), (0,)), ((), ())), preferred_element_type=F32)


def normalize(values, gain):
    return values * lax.rsqrt(jnp.mean(values * values, axis=-1, keepdims=True) + EPSILON) * gain


def normalize_back(values, gain, grad):
    inverse = lax.rsqrt(jnp.mean(values * values, axis=-1, keepdims=True) + EPSILON)
    unit = values * inverse
    gain_grad = jnp.sum(grad * unit, axis=0)
    scaled = grad * gain
    return inverse * (scaled - unit * jnp.mean(scaled * unit, axis=-1, keepdims=True)), gain_grad


def angle_tables(token_pos):
    half_size = HEAD // 2
    freqs = jnp.exp(jnp.arange(half_size, dtype=F32) * (-2.0 * math.log(100000.0) / HEAD))
    angles = freqs[:, None] * token_pos[None, :]
    cosine, sine = jnp.cos(angles), jnp.sin(angles)
    return jnp.concatenate([cosine, cosine], axis=0), jnp.concatenate([sine, sine], axis=0)


def rotate(values, tables):
    rows, cols = values.shape
    heads = values.reshape(rows // HEAD, HEAD, cols)
    half = HEAD // 2
    turned = jnp.concatenate([-heads[:, half:], heads[:, :half]], axis=1)
    return (heads * tables[0] + turned * tables[1]).reshape(rows, cols)


def rotate_back(values, tables):
    rows, cols = values.shape
    heads = values.reshape(rows // HEAD, HEAD, cols)
    half = HEAD // 2
    scaled = heads * tables[1]
    turned = jnp.concatenate([scaled[:, half:], -scaled[:, :half]], axis=1)
    return (heads * tables[0] + turned).reshape(rows, cols)


def z_masks():
    count = lax.axis_size("fsdp")
    masks = []
    while count > 1:
        count //= 2
        masks.append(count)
    return masks


class Spread:
    def __init__(self, order, own):
        self.order = order
        held = order.hold(own)[None]
        self.rank = [0]
        for mask in z_masks()[:-2]:
            held = jnp.concatenate([held, across(held, "fsdp", mask)], axis=0)
            self.rank = self.rank + [place ^ mask for place in self.rank]
        self.held = held
        self.flights = [across(held, "fsdp", mask) for mask in (1, 2, 3)]
        self.step = 0

    @classmethod
    def behind(cls, order, held):
        self = cls.__new__(cls)
        self.order, self.held, self.flights, self.rank = order, held, [], None
        self.step = 0
        return self

    def slot(self, number):
        return number if self.rank is None else lax.axis_index("fsdp") ^ self.rank[number]

    def collect(self):
        self.flights = [self.order.wait(flight) for flight in self.flights]

    def advance(self):
        self.step += 1
        if self.step == 1:
            self.collect()
            held = [self.held, *self.flights]
            if self.rank is not None:
                self.rank = [place ^ mask for mask in range(4) for place in self.rank]
            held = self.order.hold(jnp.concatenate(held, axis=0))
            self.flight = first_way(held)
            self.side = second_way(held)
            self.parts = [(held, swap_cores(held))]
        elif self.step == 2:
            got = self.order.wait(self.flight)
            side = self.order.wait(self.side)
            self.flight = second_way(got)
            self.parts.append((got, swap_cores(got)))
            self.parts.append((side, swap_cores(side)))
        else:
            got = self.order.wait(self.flight)
            self.parts.append((got, swap_cores(got)))

    def arrays(self):
        return [part[side] for side in range(2) for part in self.parts]


def place_attn(group):
    arrays = group.arrays()
    depth, rows, cols = arrays[0].shape
    zcount = lax.axis_size("fsdp")
    ccount = lax.axis_size("ctx")

    def body(*refs):
        out, sems = refs[8], refs[9]
        core, ctx = lax.axis_index("pipe"), lax.axis_index("ctx")
        copies = []
        for number in range(8):
            half = core if number < 4 else 1 - core
            mask = 0
            if number % 2 == 1:
                mask = mask ^ (1 + half)
            if number % 4 >= 2:
                mask = mask ^ (2 - half)
            col = pl.multiple_of((ctx ^ mask) * cols, cols)
            for slot in range(depth):
                copies.append(
                    pltpu.make_async_copy(
                        refs[number].at[slot],
                        out.at[group.slot(slot), half, :, pl.ds(col, cols)],
                        sems.at[len(copies)],
                    )
                )
        for copy in copies:
            copy.start()
        for copy in copies:
            copy.wait()

    out = pl.pallas_call(
        body,
        out_shape=jax.ShapeDtypeStruct((zcount, 2, rows, ccount * cols), BF16),
        in_specs=[pl.BlockSpec(memory_space=pl.ANY)] * 8,
        out_specs=pl.BlockSpec(memory_space=pltpu.VMEM),
        scratch_shapes=[pltpu.SemaphoreType.DMA((8 * depth,))],
        compiler_params=pltpu.CompilerParams(vmem_limit_bytes=40 * 1024 * 1024),
        cost_estimate=pl.CostEstimate(flops=0, bytes_accessed=0, transcendentals=0),
    )(*arrays)
    return out.reshape(-1, out.shape[-1])


def first_side(half, ctx):
    return pick(half == 0, ctx % 2, ctx // 2)


class Down:
    def __init__(self, order, piece):
        self.order = order
        self.flight = lax.all_gather(order.hold(piece), "fsdp", axis=0, tiled=False)

    def start(self):
        self.near = self.order.wait(self.flight)
        self.flight = first_way(self.near)
        self.near_other = swap_cores(self.near)

    def finish(self):
        far = self.order.wait(self.flight)
        return [self.near, far, self.near_other, swap_cores(far)]


class Ffn:
    def __init__(self, group, down):
        self.group = group
        self.arrays = group.arrays() + down
        self.depth, self.rows, self.cols = self.arrays[0].shape

    def scratch(self, rows):
        return [
            pltpu.VMEM((4, 2, self.depth * self.rows, self.cols), BF16),
            pltpu.VMEM((4, 2, 2, *self.arrays[8].shape[1:]), BF16),
            pltpu.SemaphoreType.DMA((4, 2 * self.depth)),
            pltpu.SemaphoreType.DMA((16,)),
            pltpu.VMEM((rows, self.arrays[8].shape[2]), F32),
        ]

    def start(self, refs, held, down, sems, down_sems):
        core, ctx = lax.axis_index("pipe"), lax.axis_index("ctx")
        blocks, quarters = [], []
        for number in range(4):
            copies = []
            other = 4 + (0, 2, 1, 3)[number]
            for side, half in ((number, core), (other, 1 - core)):
                for slot in range(self.depth):
                    row = pl.multiple_of(self.group.slot(slot) * self.rows, 16)
                    copies.append(
                        pltpu.make_async_copy(
                            refs[side].at[slot],
                            held.at[number, half, pl.ds(row, self.rows), :],
                            sems.at[number, len(copies)],
                        )
                    )
            blocks.append(copies)
            mask = (0, 1 + core, 2 - core, 3)[number]
            quarters.append(ctx ^ mask)
        downs = []
        for side, half in ((8, core), (9, core), (10, 1 - core), (11, 1 - core)):
            near = first_side(half, ctx)
            for zed in range(4):
                downs.append(
                    pltpu.make_async_copy(
                        refs[side].at[zed],
                        down.at[zed, half, near if side % 2 == 0 else 1 - near],
                        down_sems.at[len(downs)],
                    )
                )
        for copy in blocks[0] + downs + blocks[1] + blocks[2] + blocks[3]:
            copy.start()
        return blocks, quarters, downs

    def call(self, body, outs, *args):
        return pl.pallas_call(
            body,
            out_shape=outs,
            in_specs=[pl.BlockSpec(memory_space=pltpu.VMEM)] * len(args)
            + [pl.BlockSpec(memory_space=pl.ANY)] * 12,
            out_specs=[pl.BlockSpec(memory_space=pltpu.VMEM)] * len(outs),
            scratch_shapes=self.scratch(args[0].shape[0]),
            compiler_params=pltpu.CompilerParams(vmem_limit_bytes=48 * 1024 * 1024),
            cost_estimate=pl.CostEstimate(flops=0, bytes_accessed=0, transcendentals=0),
        )(*args, *self.arrays)

    def forward(self, resid, gain):
        rows, width = resid.shape
        cols = self.cols
        ffn = 4 * cols

        def body(r_ref, gain_ref, *refs):
            low_ref, normed_ref, gate_ref, up_ref, hidden_ref = refs[12:17]
            held, down, total = refs[17], refs[18], refs[21]
            blocks, quarters, downs = self.start(refs[:12], *refs[17:21])
            resid = r_ref[...]
            normed = normalize(resid, gain_ref[...]).astype(BF16)
            normed_ref[...] = normed.T
            total[...] = resid
            for number in range(4):
                for copy in blocks[number]:
                    copy.wait()
                gate = dot(normed, held[number, 0])
                up = dot(normed, held[number, 1])
                hidden = (gate / (1.0 + jnp.exp(-gate)) * up).astype(BF16)
                place = pl.ds(pl.multiple_of(quarters[number] * cols, cols), cols)
                gate_ref[:, place] = gate
                up_ref[:, place] = up
                hidden_ref[place, :] = hidden.T
                if number == 0:
                    for copy in downs:
                        copy.wait()
                weights = down[quarters[number]].reshape(cols, width)
                total[...] += dot(hidden, weights)
            low_ref[...] = total[...].astype(BF16)

        return self.call(
            body,
            [
                jax.ShapeDtypeStruct((rows, width), BF16),
                jax.ShapeDtypeStruct((width, rows), BF16),
                jax.ShapeDtypeStruct((rows, ffn), F32),
                jax.ShapeDtypeStruct((rows, ffn), F32),
                jax.ShapeDtypeStruct((ffn, rows), BF16),
            ],
            resid,
            gain[None],
        )

    def backward(self, grad_low, resid, gain, gate, up):
        rows, width = resid.shape
        cols = self.cols
        ffn = 4 * cols

        def body(grad_ref, r_ref, gain_ref, gate_ref, up_ref, *refs):
            out_ref, gain_out, gate_out, up_out, total = *refs[12:16], refs[20]
            held, down = refs[16:18]
            blocks, quarters, downs = self.start(refs[:12], *refs[16:20])
            grad = grad_ref[...]
            for number in range(4):
                place = pl.ds(pl.multiple_of(quarters[number] * cols, cols), cols)
                if number == 0:
                    for copy in downs:
                        copy.wait()
                weights = down[quarters[number]].reshape(cols, width)
                hidden_grad = dot_back(grad, weights)
                gate, up = gate_ref[:, place], up_ref[:, place]
                sig = 1.0 / (1.0 + jnp.exp(-gate))
                gate_grad = (hidden_grad * up * (sig * (1.0 + gate * (1.0 - sig)))).astype(BF16)
                up_grad = (hidden_grad * (gate * sig)).astype(BF16)
                own, other = two_ways(gate_grad, up_grad)
                gate_out[:, place] = own
                up_out[:, place] = other
                for copy in blocks[number]:
                    copy.wait()
                part = dot_back(gate_grad, held[number, 0]) + dot_back(up_grad, held[number, 1])
                if number == 0:
                    total[...] = part
                else:
                    total[...] += part
            resid_part, gain_grad = normalize_back(r_ref[...], gain_ref[...], total[...])
            out_ref[...] = grad.astype(F32) + resid_part
            gain_out[...] = gain_grad[None]

        outs = self.call(
            body,
            [
                jax.ShapeDtypeStruct((rows, width), F32),
                jax.ShapeDtypeStruct((1, width), F32),
                jax.ShapeDtypeStruct((rows, ffn), BF16),
                jax.ShapeDtypeStruct((rows, ffn), BF16),
            ],
            grad_low,
            resid,
            gain[None],
            gate,
            up,
        )
        return outs[0], outs[1][0], outs[2], outs[3]

    def both(self, resid, gain, grad_low):
        rows, width = resid.shape
        cols = self.cols
        ffn = 4 * cols

        def body(r_ref, gain_ref, grad_ref, *refs):
            low_ref, normed_ref, hidden_ref, out_ref, gain_out, own_ref, send_ref = refs[12:19]
            held, down, total = refs[19], refs[20], refs[23]
            blocks, quarters, downs = self.start(refs[:12], *refs[19:23])
            resid = r_ref[...]
            grad = grad_ref[...]
            normed = normalize(resid, gain_ref[...]).astype(BF16)
            normed_ref[...] = normed.T
            total[...] = resid
            normed_grad = jnp.zeros((rows, width), F32)
            for number in range(4):
                for copy in blocks[number]:
                    copy.wait()
                gate = dot(normed, held[number, 0])
                up = dot(normed, held[number, 1])
                sig = 1.0 / (1.0 + jnp.exp(-gate))
                act = gate / (1.0 + jnp.exp(-gate))
                hidden = (act * up).astype(BF16)
                place = pl.ds(pl.multiple_of(quarters[number] * cols, cols), cols)
                hidden_ref[place, :] = hidden.T
                if number == 0:
                    for copy in downs:
                        copy.wait()
                weights = down[quarters[number]].reshape(cols, width)
                total[...] += dot(hidden, weights)
                hidden_grad = dot_back(grad, weights)
                gate_grad = (hidden_grad * up * (sig * (1.0 + gate * (1.0 - sig)))).astype(BF16)
                up_grad = (hidden_grad * act).astype(BF16)
                own_ref[:, place], send_ref[:, place] = two_ways(gate_grad, up_grad)
                part = dot_back(gate_grad, held[number, 0]) + dot_back(up_grad, held[number, 1])
                normed_grad = normed_grad + part
            low_ref[...] = total[...].astype(BF16)
            resid_part, gain_grad = normalize_back(r_ref[...], gain_ref[...], normed_grad)
            out_ref[...] = grad.astype(F32) + resid_part
            gain_out[...] = gain_grad[None]

        outs = self.call(
            body,
            [
                jax.ShapeDtypeStruct((rows, width), BF16),
                jax.ShapeDtypeStruct((width, rows), BF16),
                jax.ShapeDtypeStruct((ffn, rows), BF16),
                jax.ShapeDtypeStruct((rows, width), F32),
                jax.ShapeDtypeStruct((1, width), F32),
                jax.ShapeDtypeStruct((rows, ffn), BF16),
                jax.ShapeDtypeStruct((rows, ffn), BF16),
            ],
            resid,
            gain[None],
            grad_low,
        )
        return outs[:3], (outs[3], outs[4][0], outs[5], outs[6])


class WholeFfn:
    def __init__(self, w_gateup, w_down, layer):
        core = lax.axis_index("pipe")
        whole = []
        for array in (w_gateup, w_down):
            mine = lax.all_gather(array, "fsdp", axis=0, tiled=True)
            whole.append(pick(core == layer, mine, swap_cores(mine)))
        self.w_gateup, self.w_down = whole

    def forward(self, resid, gain):
        normed = normalize(resid, gain).astype(BF16)
        gated = dot(normed, self.w_gateup)
        ffn = gated.shape[1] // 2
        gate, up = gated[:, :ffn], gated[:, ffn:]
        hidden = (gate / (1.0 + jnp.exp(-gate)) * up).astype(BF16)
        outputs = (resid + dot(hidden, self.w_down)).astype(BF16)
        return outputs, normed.T, gate, up, hidden.T

    def both(self, resid, gain, grad_low):
        outputs, normed, gate, up, hidden = self.forward(resid, gain)
        return (outputs, normed, hidden), self.backward(grad_low, resid, gain, gate, up)

    def backward(self, grad_low, resid, gain, gate, up):
        ffn = gate.shape[1]
        hidden_grad = dot_back(grad_low, self.w_down)
        sig = 1.0 / (1.0 + jnp.exp(-gate))
        gate_grad = (hidden_grad * up * (sig * (1.0 + gate * (1.0 - sig)))).astype(BF16)
        up_grad = (hidden_grad * (gate * sig)).astype(BF16)
        normed_grad = dot_back(gate_grad, self.w_gateup[:, :ffn]) + dot_back(
            up_grad, self.w_gateup[:, ffn:]
        )
        resid_part, gain_grad = normalize_back(resid, gain, normed_grad)
        own, other = two_ways(gate_grad, up_grad)
        return grad_low.astype(F32) + resid_part, gain_grad, own, other


def own_pieces(w_query, w_keyval, w_out, w_gateup, w_down, core, ctx):
    sources = (w_keyval, w_query, w_out)
    rows = w_query.shape[0] // 2
    cols = sum(source.shape[1] for source in sources) // 4
    ffn = w_gateup.shape[1] // 2
    depth = w_down.shape[0] // 2

    def quarter(number):
        found, place = [], 0
        for source in sources:
            start = max(number * cols - place, 0)
            stop = min((number + 1) * cols - place, source.shape[1])
            if start < stop:
                found.append(source[:, start:stop])
            place += source.shape[1]
        return found[0] if len(found) == 1 else jnp.concatenate(found, axis=1)

    attn = pick(
        ctx < 2, pick(ctx == 0, quarter(0), quarter(1)), pick(ctx == 2, quarter(2), quarter(3))
    )
    attn_parts = two_ways(attn[:rows], attn[rows:])

    def parts(half, attn_part):
        return (
            attn_part,
            lax.dynamic_slice(w_gateup, (0, half * ffn + ctx * cols), (2 * rows, cols)),
            lax.dynamic_slice_in_dim(
                w_down, half * depth + first_side(half, ctx) * (depth // 2), depth // 2, 0
            ),
        )

    kept = parts(core, attn_parts[0])
    received = [swap_cores(piece) for piece in parts(1 - core, attn_parts[1])]
    first = [pick(core == 0, a, b) for a, b in zip(kept, received)]
    second = [pick(core == 0, b, a) for a, b in zip(kept, received)]
    return first, second


def add_low(kept, received):
    return (kept.astype(F32) + received.astype(F32)).astype(BF16)


def term(*pairs, gains=None):
    rows = pairs[0][0].shape[0]
    deep = rows // 4
    widths = [pair[2].shape[1] if pair[4] else pair[2].shape[0] for pair in pairs]

    def body(*refs):
        sent_ref, kept_ref = refs[-2:]
        core, ctx = lax.axis_index("pipe"), lax.axis_index("ctx")
        y, x = ctx // 2, ctx % 2
        for out, xx, yy in ((sent_ref, 1 - x, 1 - y), (kept_ref, x, y)):
            for side in range(2):
                block = jnp.where(core == 0, xx + 2 * side, 2 * yy + side)
                place = pl.ds(pl.multiple_of(block * deep, 16), deep)
                offset = 0
                for number, pair in enumerate(pairs):
                    lefts = [ref[place, :] for ref in refs[4 * number : 4 * number + 2]]
                    rights = refs[4 * number + 2 : 4 * number + 4]
                    for start in range(0, widths[number], 640):
                        stop = min(start + 640, widths[number])
                        total = None
                        for left, right in zip(lefts, rights):
                            if pair[4]:
                                part = dot(left, right[:, start:stop])
                            else:
                                part = dot_back(left, right[start:stop, :])
                            total = part if total is None else total + part
                        out[side, :deep, offset + start : offset + stop] = total.astype(BF16)
                    offset += widths[number]
                if gains is not None:
                    out[side, deep:, :] = refs[-3][...]

    extra = []
    if gains is not None:
        low = gains.astype(BF16)
        extra = [jnp.pad(low, ((0, 16 - low.shape[0]), (0, sum(widths) - low.shape[1])))]
    shape = jax.ShapeDtypeStruct((2, deep + 16 * len(extra), sum(widths)), BF16)
    arrays = [array for pair in pairs for array in pair[:4]]
    return local_call(body, [shape, shape], *arrays, *extra)


class Reduce:
    def __init__(self, order, term, offload=False, extra=0):
        self.order = order
        self.extra = extra
        self.offload = offload
        core, ctx, self.zed = lax.axis_index("pipe"), lax.axis_index("ctx"), lax.axis_index("fsdp")
        self.side = pick(core == 0, ctx // 2, ctx % 2)
        self.step = 0
        self.result = None
        sent, kept = term
        self.kept = [kept]
        self.flights = [first_way(sent)]

    def land(self):
        parts = self.kept + [self.order.wait(flight) for flight in self.flights]
        return sum(part.astype(F32) for part in parts)

    def advance(self):
        if self.result is not None:
            return
        index = lax.dynamic_index_in_dim
        self.step += 1
        if self.step == 1:
            parts = self.kept + [self.order.wait(flight) for flight in self.flights]
            sent = sum(index(part, 1 - self.side, 0, False).astype(F32) for part in parts)
            self.kept = [index(part, self.side, 0, False) for part in parts]
            self.flights = [second_way(self.order.wait(sent.astype(BF16)))]
            return
        total = self.land()
        if self.step == 3:
            self.result = total
            return
        low = total.astype(BF16)
        if self.offload:
            count = lax.axis_size("fsdp")
            parts = low.reshape(count, low.shape[0] // count, low.shape[1])
            parts = self.order.wait(parts)
            self.result = lax.psum_scatter(parts, "fsdp", scatter_dimension=0, tiled=False)
            return
        deep = low.shape[0] - self.extra
        body, tail = low[:deep], low[deep:]
        for mask in z_masks()[:-2]:
            half = body.shape[0] // 2
            high = (self.zed & mask) != 0
            self.kept = [jnp.concatenate([pick(high, body[half:], body[:half]), tail], axis=0)]
            sent = jnp.concatenate([pick(high, body[:half], body[half:]), tail], axis=0)
            self.flights = [across(sent, "fsdp", mask)]
            low = self.land().astype(BF16)
            body, tail = low[:half], low[half:]
        parts = body.reshape(4, body.shape[0] // 4, body.shape[1])
        if self.extra:
            tails = jnp.broadcast_to(tail, (4, *tail.shape))
            parts = jnp.concatenate([parts, tails], axis=1)
        here = self.zed % 4
        self.kept = [index(parts, here, 0, False)]
        sent = [index(parts, here ^ mask, 0, False) for mask in (3, 2, 1)]
        sent = self.order.waits(sent)
        self.flights = [across(block, "fsdp", mask) for block, mask in zip(sent, (3, 2, 1))]

    def settle(self):
        self.result = self.order.wait(self.result)


def send_keys(keyval):
    flows = []
    for mask in (3, 1, 2):
        flows.append(across(keyval, "ctx", mask))
    return flows[1], flows[2], flows[0]


def return_keys(parts):
    return [across(part, "ctx", mask) for part, mask in zip(parts, (1, 2, 3))]


def local_call(kernel, outs, *args):
    return pl.pallas_call(
        kernel,
        out_shape=outs,
        in_specs=[pl.BlockSpec(memory_space=pltpu.VMEM)] * len(args),
        out_specs=[pl.BlockSpec(memory_space=pltpu.VMEM)] * len(outs),
        compiler_params=pltpu.CompilerParams(vmem_limit_bytes=48 * 1024 * 1024),
        cost_estimate=pl.CostEstimate(flops=0, bytes_accessed=0, transcendentals=0),
    )(*args)


def project(inputs_low, w_attn, gain_attn, tables):
    rows, width = inputs_low.shape
    kv_width = (w_attn.shape[1] - 2 * width) // 2

    def body(x_ref, w_ref, gain_ref, cos_ref, sin_ref, normed_ref, q_ref, kv_ref):
        tables = cos_ref[...], sin_ref[...]
        normed = normalize(x_ref[...].astype(F32), gain_ref[...]).astype(BF16)
        normed_ref[...] = normed.T
        projected = dot(normed, w_ref[:, : 2 * kv_width + width]).T
        kv_ref[:kv_width, :] = rotate(projected[:kv_width], tables).astype(BF16)
        kv_ref[kv_width:, :] = projected[kv_width : 2 * kv_width].astype(BF16)
        queries = rotate(projected[2 * kv_width :], tables).astype(BF16)
        q_ref[...] = (queries.astype(F32) * SCALE).astype(BF16)

    return local_call(
        body,
        [
            jax.ShapeDtypeStruct((width, rows), BF16),
            jax.ShapeDtypeStruct((width, rows), BF16),
            jax.ShapeDtypeStruct((2 * kv_width, rows), BF16),
        ],
        inputs_low,
        w_attn,
        gain_attn[None],
        *tables,
    )


def head_rows(ref, head, offset=0):
    return ref[pl.ds(pl.multiple_of(head * HEAD + offset, HEAD), HEAD), :]


def attend_kernel(
    q_ref, p0, p1, p2, p3, bias_ref, x_ref, w_ref, normed_ref, own_ref, send_ref, lse_ref, r_ref, o_ref
):
    pieces = (p0, p1, p2, p3)
    count = q_ref.shape[1]
    kv_width = p0.shape[0] // 2
    ones = jnp.ones((16, count), BF16)

    def group(kv_head, carry):
        keys = [head_rows(p, kv_head).T for p in pieces]
        values = [
            jnp.concatenate([head_rows(p, kv_head, kv_width), ones], axis=0) for p in pieces
        ]
        for member in range(GROUPS):
            head = kv_head * GROUPS + member
            query = head_rows(q_ref, head)
            scores = [
                dot(keys[r], query) + bias_ref[r * count : (r + 1) * count, :] for r in range(4)
            ]
            top = jnp.maximum(
                jnp.maximum(scores[0], scores[1]), jnp.maximum(scores[2], scores[3])
            )
            top = jnp.max(top, axis=0, keepdims=True)
            total = jnp.zeros((HEAD + 16, count), F32)
            for r in range(4):
                total = total + dot(values[r], jnp.exp(scores[r] - top).astype(BF16))
            summed = total[HEAD : HEAD + 1]
            o_ref[pl.ds(pl.multiple_of(head * HEAD, HEAD), HEAD), :] = (
                total[:HEAD] / summed
            ).astype(BF16)
            lse_ref[head] = top + jnp.log(summed)
        return carry

    lax.fori_loop(0, KV_HEADS, group, 0)
    attended = o_ref[...]
    own_ref[...], send_ref[...] = two_ways(normed_ref[...], attended)
    width = attended.shape[0]
    r_ref[...] = x_ref[...].astype(F32) + dot(
        attended.T, w_ref[:, w_ref.shape[1] - width :]
    )


def scores_back_kernel(
    dr_ref,
    w_ref,
    q_ref,
    p0,
    p1,
    p2,
    p3,
    bias_ref,
    lse_ref,
    left_own_ref,
    left_send_ref,
    cos_ref,
    sin_ref,
    own_ref,
    send_ref,
    kv_own_ref,
    kv_x_ref,
    kv_y_ref,
    kv_xy_ref,
    do_ref,
    o_ref,
    dq_ref,
):
    tables = cos_ref[...], sin_ref[...]
    width = q_ref.shape[0]
    resid_low = dr_ref[...].astype(BF16)
    do_ref[...] = dot_back(w_ref[:, w_ref.shape[1] - width :], resid_low).astype(BF16)
    _, o_ref[...] = two_ways(left_own_ref[...], left_send_ref[...])
    pieces = (p0, p1, p2, p3)
    count = q_ref.shape[1]
    kv_width = p0.shape[0] // 2

    def group(kv_head, carry):
        keys_turned = [head_rows(p, kv_head) for p in pieces]
        keys = [k.T for k in keys_turned]
        values = [head_rows(p, kv_head, kv_width).T for p in pieces]
        key_grads = [jnp.zeros((HEAD, count), F32) for _ in range(4)]
        value_grads = [jnp.zeros((HEAD, count), F32) for _ in range(4)]
        for member in range(GROUPS):
            head = kv_head * GROUPS + member
            query = head_rows(q_ref, head)
            grad = head_rows(do_ref, head)
            delta = jnp.sum(
                grad.astype(F32) * head_rows(o_ref, head).astype(F32), axis=0, keepdims=True
            )
            log_total = lse_ref[head]
            query_grad = jnp.zeros((HEAD, count), F32)
            for r in range(4):
                scores = dot(keys[r], query) + bias_ref[r * count : (r + 1) * count, :]
                probs = jnp.exp(scores - log_total)
                prob_grad = dot(values[r], grad)
                score_low = (probs * (prob_grad - delta)).astype(BF16)
                value_grads[r] = value_grads[r] + dot_back(grad, probs.astype(BF16))
                key_grads[r] = key_grads[r] + dot_back(query, score_low)
                query_grad = query_grad + dot(keys_turned[r], score_low)
            dq_ref[pl.ds(pl.multiple_of(head * HEAD, HEAD), HEAD), :] = rotate_back(
                query_grad * SCALE, tables
            ).astype(BF16)
        start = pl.multiple_of(kv_head * HEAD, HEAD)
        for r, ref in enumerate((kv_own_ref, kv_x_ref, kv_y_ref, kv_xy_ref)):
            ref[pl.ds(start, HEAD), :] = key_grads[r].astype(ref.dtype)
            place = pl.ds(pl.multiple_of(start + kv_width, HEAD), HEAD)
            ref[place, :] = value_grads[r].astype(ref.dtype)
        return carry

    lax.fori_loop(0, KV_HEADS, group, 0)
    own_ref[...], send_ref[...] = two_ways(dq_ref[...], resid_low.T)


def attend(inputs_low, projected, pieces, w_attn, bias):
    normed, queries, _ = projected
    width, rows = queries.shape
    left_own, left_send, log_total, resid, _ = local_call(
        attend_kernel,
        [
            jax.ShapeDtypeStruct((width, rows), BF16),
            jax.ShapeDtypeStruct((width, rows), BF16),
            jax.ShapeDtypeStruct((HEADS, 1, rows), F32),
            jax.ShapeDtypeStruct((rows, width), F32),
            jax.ShapeDtypeStruct((width, rows), BF16),
        ],
        queries,
        *pieces,
        bias,
        inputs_low,
        w_attn,
        normed,
    )
    lefts = (left_own, swap_cores(left_send), normed, swap_cores(normed))
    return resid, (inputs_low, queries, pieces, log_total, left_own, left_send, lefts)


def backward_scores(resid_grad, saved, w_attn, bias, tables):
    _, queries, pieces, log_total, left_own, left_send, _ = saved
    width, rows = queries.shape
    keys = pieces[0].shape
    return local_call(
        scores_back_kernel,
        [
            jax.ShapeDtypeStruct((width, rows), BF16),
            jax.ShapeDtypeStruct((width, rows), BF16),
            jax.ShapeDtypeStruct(keys, F32),
            jax.ShapeDtypeStruct(keys, BF16),
            jax.ShapeDtypeStruct(keys, BF16),
            jax.ShapeDtypeStruct(keys, BF16),
            jax.ShapeDtypeStruct((width, rows), BF16),
            jax.ShapeDtypeStruct((width, rows), BF16),
            jax.ShapeDtypeStruct((width, rows), BF16),
        ],
        resid_grad,
        w_attn,
        queries,
        *pieces,
        bias,
        log_total,
        left_own,
        left_send,
        *tables,
    )[:6]


def backward_project(resid_grad, rights, kv_own, flows, saved, w_attn, gain_attn, tables):
    inputs_low = saved[0]
    rows, width = inputs_low.shape
    kv_width = kv_own.shape[0] // 2

    def body(
        dr_ref, own, send, kv0, kv1, kv2, kv3, x_ref, w_ref, gain_ref, cos_ref, sin_ref,
        low_ref, gain_out, thin_own, thin_send,
    ):
        tables = cos_ref[...], sin_ref[...]
        kv = kv0[...]
        for ref in (kv1, kv2, kv3):
            kv = kv + ref[...].astype(F32)
        keys = rotate_back(kv[:kv_width], tables).astype(BF16)
        values = kv[kv_width:].astype(BF16)
        queries, _ = two_ways(own[...], send[...])
        thin_own[...], thin_send[...] = two_ways(keys, values)
        projected = jnp.concatenate([keys, values, queries], axis=0).T
        normed_grad = dot_back(projected, w_ref[:, : 2 * kv_width + width])
        part, gain_grad = normalize_back(
            x_ref[...].astype(F32), gain_ref[...], normed_grad
        )
        low_ref[...] = (dr_ref[...] + part).astype(BF16)
        gain_out[...] = gain_grad[None]

    low, gain_grad, thin_own, thin_send = local_call(
        body,
        [
            jax.ShapeDtypeStruct((rows, width), BF16),
            jax.ShapeDtypeStruct((1, width), F32),
            jax.ShapeDtypeStruct((kv_width, rows), BF16),
            jax.ShapeDtypeStruct((kv_width, rows), BF16),
        ],
        resid_grad,
        *rights,
        kv_own,
        *flows,
        inputs_low,
        w_attn,
        gain_attn[None],
        *tables,
    )
    return low, gain_grad[0], thin_own, thin_send


def shards(
    tokens, cotangent, doc_ids, w_query, w_keyval, w_out, w_gateup, w_down, gain_attn, gain_ffn
):
    core = lax.axis_index("pipe")
    ctx = lax.axis_index("ctx")
    zed = lax.axis_index("fsdp")
    on_first = core == 0
    rows = tokens.shape[2]
    width = tokens.shape[3]
    length = doc_ids.shape[2]
    kv_width = w_keyval.shape[2] // 2

    pieces = own_pieces(
        w_query[0], w_keyval[0], w_out[0], w_gateup[0], w_down[0], core, ctx
    )
    gains = jnp.concatenate([gain_attn, gain_ffn], axis=0)
    gains_other = swap_cores(gains)
    layer_gains = (pick(on_first, gains, gains_other), pick(on_first, gains_other, gains))

    doc_row = lax.dynamic_index_in_dim(doc_ids[:, 0], core, 0, keepdims=False)
    inputs_low = lax.dynamic_index_in_dim(tokens[:, 0], core, 0, keepdims=False)
    cotangent_own = lax.dynamic_index_in_dim(cotangent[:, 0], core, 0, keepdims=False)
    earlier = jnp.sum((doc_row[None, :] < doc_row[:, None]).astype(jnp.int32), axis=1)
    positions = jnp.arange(length, dtype=jnp.int32) - earlier
    token_pos = lax.dynamic_slice_in_dim(positions, ctx * rows, rows, 0)
    tables = angle_tables(token_pos.astype(F32))
    own_docs = lax.dynamic_slice_in_dim(doc_row, ctx * rows, rows, 0)
    query_index = ctx * rows + jnp.arange(rows, dtype=jnp.int32)
    key_docs = []
    key_index = []
    for mask in range(4):
        key_docs.append(lax.dynamic_slice_in_dim(doc_row, (ctx ^ mask) * rows, rows, 0))
        key_index.append((ctx ^ mask) * rows + jnp.arange(rows, dtype=jnp.int32))
    key_docs = jnp.concatenate(key_docs)
    key_index = jnp.concatenate(key_index)
    seen = (own_docs[None, :] == key_docs[:, None]) & (
        key_index[:, None] <= query_index[None, :]
    )
    bias = jnp.where(seen, 0.0, NEGATIVE).astype(F32)

    order = Order()
    (attn_first, ffn_first, down_first), (attn_second, ffn_second, down_second) = pieces
    tiles = w_gateup.shape[1] % 16 == 0
    split = attn_first.shape[0]
    attn0 = Spread(order, attn_first)
    ffn_first, down_first = order.waits((ffn_first, down_first))
    if tiles:
        down0 = Down(order, down_first)
    attn0.flights[0] = order.wait(attn0.flights[0])
    if tiles:
        ffn0 = Spread(order, ffn_first)
    attn0.advance()
    attn0.advance()
    if tiles:
        ffn0.advance()
    second = order.hold(jnp.concatenate([attn_second, ffn_second], axis=0))
    second = lax.all_gather(second, "fsdp", axis=0, tiled=False)
    attn0.advance()
    w_attn0 = order.wait(place_attn(attn0))
    own0 = project(inputs_low, w_attn0, layer_gains[0][0], tables)
    keys0 = send_keys(own0[2])
    keyval0 = (own0[2], *[order.wait(flow) for flow in keys0])
    if tiles:
        ffn0.advance()
        down0.start()
    resid0, attn_saved0 = attend(inputs_low, own0, keyval0, w_attn0, bias)
    resid0 = order.wait(resid0)
    second = order.wait(second)
    attn1 = Spread.behind(order, second[:, :split])
    attn1.advance()
    if tiles:
        down1 = Down(order, down_second)
        ffn0.advance()
        weights0 = Ffn(ffn0, down0.finish())
    else:
        weights0 = WholeFfn(w_gateup[0], w_down[0], 0)
        weights1 = WholeFfn(w_gateup[0], w_down[0], 1)
    middle, *ffn_saved0 = weights0.forward(resid0, layer_gains[0][1])
    middle = order.wait(middle)
    attn1.advance()
    if tiles:
        ffn1 = Spread.behind(order, second[:, split:])
        ffn1.advance()
    attn1.advance()
    w_attn1 = order.wait(place_attn(attn1))
    own1 = project(middle, w_attn1, layer_gains[1][0], tables)
    keys1 = send_keys(own1[2])
    if tiles:
        ffn1.advance()
    keyval1 = (own1[2], *[order.wait(flow) for flow in keys1])
    if tiles:
        down1.start()
    resid1, attn_saved1 = attend(middle, own1, keyval1, w_attn1, bias)
    resid1 = order.wait(resid1)
    turned0 = [(array, order.wait(swap_cores(array))) for array in (ffn_saved0[0], ffn_saved0[3])]
    if tiles:
        ffn1.advance()
        weights1 = Ffn(ffn1, down1.finish())
    (outputs1, normed1, hidden1), back1 = weights1.both(
        resid1, layer_gains[1][1], cotangent_own
    )
    section_outs = [middle, outputs1]

    weights = [(w_attn0, weights0), (w_attn1, weights1)]
    saved = [(attn_saved0, (resid0, *ffn_saved0)), (attn_saved1, None)]
    half = -(-width // 256) * 128
    turned = [
        turned0,
        [(array, swap_cores(array)) for array in (normed1, hidden1)],
    ]

    grad_low = cotangent_own
    input_grads = [None, None]
    reduced = [None, None]
    gain_grads = [None, None]
    above = None
    for layer in (1, 0):
        w_attn, w_ffn = weights[layer]
        attn_saved, ffn_saved = saved[layer]
        normed, hidden = turned[layer]
        grad_low = order.wait(grad_low)
        own, send = two_ways(grad_low[:, :half], grad_low[:, width - half :])
        down = Reduce(order, order.waits(term((*hidden, own, swap_cores(send), True))), True)
        if layer == 1:
            resid_grad, gain_ffn_grad, own, send = back1
        else:
            resid_grad, gain_ffn_grad, own, send = w_ffn.backward(
                order.hold(grad_low),
                ffn_saved[0],
                layer_gains[layer][1],
                ffn_saved[2],
                ffn_saved[3],
            )
        resid_grad = order.wait(resid_grad)
        if layer == 0:
            above[1].advance()
            above[2].advance()
            above[0].settle()
            down.advance()
        *rights, kv_own, kv_x, kv_y, kv_xy = backward_scores(
            resid_grad, attn_saved, w_attn, bias, tables
        )
        kv_own = order.wait(kv_own)
        flows = return_keys(order.hold(kv_x, kv_y, kv_xy))
        gateup_term = order.waits(term((*normed, own, swap_cores(send), True)))
        if layer == 0:
            above[1].advance()
        flows = [order.wait(flow) for flow in flows]
        gateup = Reduce(order, order.hold(*gateup_term), True)
        if layer == 1:
            down.advance()
        grad_low, gain_attn_grad, own, send = backward_project(
            resid_grad, rights, kv_own, flows, attn_saved, w_attn, layer_gains[layer][0], tables
        )
        gain_grads[layer] = (gain_attn_grad, gain_ffn_grad)
        gains = None
        if layer == 0:
            grad_low = order.wait(grad_low)
            gains = jnp.stack([*gain_grads[0], *gain_grads[1]])
            gains = gains + swap_cores(gains)
            gains = pick(on_first, gains[:2], gains[2:])
        lefts = attn_saved[6]
        attn = Reduce(
            order,
            order.waits(
                term(
                    (*lefts[:2], rights[0], swap_cores(rights[1]), False),
                    (*lefts[2:], own, swap_cores(send), False),
                    gains=gains,
                )
            ),
            layer == 1,
            0 if gains is None else 16,
        )
        if layer == 1:
            down.advance()
            above = [down, gateup, attn]
        reduced[layer] = [down, gateup, attn]
        input_grads[layer] = grad_low

    above[2].advance()
    down.advance()
    above[1].settle()
    gateup.advance()

    def to_layers(first, second):
        own, other = two_ways(first, second)
        other = swap_cores(other)
        return two_ways(own, other)

    section_out = order.wait(jnp.stack(to_layers(section_outs[0], section_outs[1])))
    attn.advance()
    above[2].settle()
    gateup.advance()
    section_in_grad = order.wait(jnp.stack(to_layers(input_grads[0], input_grads[1])))
    attn.advance()
    down.settle()
    down_left, down_right = order.waits(to_layers(down.result, above[0].result))
    attn.advance()
    gain_total = attn.result[-16:-14, :width]
    attn_first, attn_second = to_layers(attn.result[:-16].astype(BF16), above[2].result)
    gateup.settle()
    gate, up = to_layers(gateup.result, above[1].result)
    attn_first, attn_second, gate, up, down_left, down_right = [
        array.astype(F32) for array in (attn_first, attn_second, gate, up, down_left, down_right)
    ]
    return (
        section_out[None, :, None],
        section_in_grad[None, :, None],
        attn_first[None, :, :width],
        jnp.concatenate([attn_first[:, width:], attn_second[:, width:]], axis=1)[None],
        attn_second[None, :, :width],
        jnp.concatenate([gate, up], axis=1)[None],
        jnp.concatenate(
            [down_left[:, : width // 2], down_right[:, half - width // 2 :]], axis=1
        )[None],
        gain_total[0][None],
        gain_total[1][None],
    )


def solution(mesh):
    return jax.shard_map(
        shards,
        mesh=mesh,
        in_specs=(
            P(None, "fsdp", "ctx", None),
            P(None, "fsdp", "ctx", None),
            P(None, "fsdp", None),
            P("pipe", "fsdp", None),
            P("pipe", "fsdp", None),
            P("pipe", "fsdp", None),
            P("pipe", "fsdp", None),
            P("pipe", "fsdp", None),
            P("pipe", None),
            P("pipe", None),
        ),
        out_specs=(
            P("pipe", None, "fsdp", "ctx", None),
            P("pipe", None, "fsdp", "ctx", None),
            P("pipe", ("ctx", "fsdp"), None),
            P("pipe", ("ctx", "fsdp"), None),
            P("pipe", ("ctx", "fsdp"), None),
            P("pipe", ("ctx", "fsdp"), None),
            P("pipe", ("ctx", "fsdp"), None),
            P("pipe", None),
            P("pipe", None),
        ),
        check_vma=False,
    )
```

```python
import functools
import math

import jax
import jax.numpy as jnp
from jax import lax
from jax.experimental import pallas as pl
from jax.experimental.pallas import tpu as pltpu
from jax.sharding import PartitionSpec as P

HEADS = 15
KV_HEADS = 5
HEAD = 64
GROUPS = HEADS // KV_HEADS
EPSILON = 1e-05
NEGATIVE = -1e30
SCALE = 1.0 / math.sqrt(HEAD)
F32 = jnp.float32
BF16 = jnp.bfloat16


def swap_cores(array):
    return lax.ppermute(array, "pipe", [(0, 1), (1, 0)])


def one_way(array, source, target):
    return lax.ppermute(array, "pipe", [(source, target)])


def across(array, axis, mask):
    count = lax.axis_size(axis)
    return lax.ppermute(array, axis, [(i, i ^ mask) for i in range(count)])


def pick(flag, first, second):
    return jnp.where(flag, first, second)


def two_ways(first, second):
    on_first = lax.axis_index("pipe") == 0
    return pick(on_first, first, second), pick(on_first, second, first)


class Order:
    def __init__(self):
        self.last = None

    def hold(self, *arrays):
        if self.last is not None:
            *arrays, _ = lax.optimization_barrier((*arrays, self.last))
        return arrays[0] if len(arrays) == 1 else tuple(arrays)

    def wait(self, array):
        array = self.hold(array)
        self.last = array
        return array

    def waits(self, arrays):
        arrays = self.hold(*arrays)
        self.last = arrays[0]
        return arrays


def first_way(array):
    pairs = [(c, c ^ 1) for c in range(4)] + [(4 + c, 4 + (c ^ 2)) for c in range(4)]
    return lax.ppermute(array, ("pipe", "ctx"), pairs)


def second_way(array):
    pairs = [(c, c ^ 2) for c in range(4)] + [(4 + c, 4 + (c ^ 1)) for c in range(4)]
    return lax.ppermute(array, ("pipe", "ctx"), pairs)


def dot(left, right):
    return jnp.dot(left, right, preferred_element_type=F32)


def dot_back(left, right):
    return lax.dot_general(left, right, (((1,), (1,)), ((), ())), preferred_element_type=F32)


def dot_rows(left, right):
    return lax.dot_general(left, right, (((0,), (0,)), ((), ())), preferred_element_type=F32)


def normalize(values, gain):
    return values * lax.rsqrt(jnp.mean(values * values, axis=-1, keepdims=True) + EPSILON) * gain


def normalize_back(values, gain, grad):
    inverse = lax.rsqrt(jnp.mean(values * values, axis=-1, keepdims=True) + EPSILON)
    unit = values * inverse
    gain_grad = jnp.sum(grad * unit, axis=0)
    scaled = grad * gain
    return inverse * (scaled - unit * jnp.mean(scaled * unit, axis=-1, keepdims=True)), gain_grad


def angle_tables(token_pos):
    half_size = HEAD // 2
    freqs = jnp.exp(jnp.arange(half_size, dtype=F32) * (-2.0 * math.log(100000.0) / HEAD))
    angles = freqs[:, None] * token_pos[None, :]
    cosine, sine = jnp.cos(angles), jnp.sin(angles)
    return jnp.concatenate([cosine, cosine], axis=0), jnp.concatenate([sine, sine], axis=0)


def rotate(values, tables):
    rows, cols = values.shape
    heads = values.reshape(rows // HEAD, HEAD, cols)
    half = HEAD // 2
    turned = jnp.concatenate([-heads[:, half:], heads[:, :half]], axis=1)
    return (heads * tables[0] + turned * tables[1]).reshape(rows, cols)


def rotate_back(values, tables):
    rows, cols = values.shape
    heads = values.reshape(rows // HEAD, HEAD, cols)
    half = HEAD // 2
    scaled = heads * tables[1]
    turned = jnp.concatenate([scaled[:, half:], -scaled[:, :half]], axis=1)
    return (heads * tables[0] + turned).reshape(rows, cols)


def z_masks():
    count = lax.axis_size("fsdp")
    masks = []
    while count > 1:
        count //= 2
        masks.append(count)
    return masks


class Spread:
    def __init__(self, order, own):
        self.order = order
        held = order.hold(own)[None]
        self.rank = [0]
        for mask in z_masks()[:-2]:
            held = jnp.concatenate([held, across(held, "fsdp", mask)], axis=0)
            self.rank = self.rank + [place ^ mask for place in self.rank]
        self.held = held
        self.flights = [across(held, "fsdp", mask) for mask in (1, 2, 3)]
        self.step = 0

    @classmethod
    def behind(cls, order, held):
        self = cls.__new__(cls)
        self.order, self.held, self.flights, self.rank = order, held, [], None
        self.step = 0
        return self

    def slot(self, number):
        return number if self.rank is None else lax.axis_index("fsdp") ^ self.rank[number]

    def collect(self):
        self.flights = [self.order.wait(flight) for flight in self.flights]

    def advance(self):
        self.step += 1
        if self.step == 1:
            self.collect()
            held = [self.held, *self.flights]
            if self.rank is not None:
                self.rank = [place ^ mask for mask in range(4) for place in self.rank]
            held = self.order.hold(jnp.concatenate(held, axis=0))
            self.flight = first_way(held)
            self.side = second_way(held)
            self.parts = [(held, swap_cores(held))]
        elif self.step == 2:
            got = self.order.wait(self.flight)
            side = self.order.wait(self.side)
            self.flight = second_way(got)
            self.parts.append((got, swap_cores(got)))
            self.parts.append((side, swap_cores(side)))
        else:
            got = self.order.wait(self.flight)
            self.parts.append((got, swap_cores(got)))

    def arrays(self):
        return [part[side] for side in range(2) for part in self.parts]


def place_attn(group):
    arrays = group.arrays()
    depth, rows, cols = arrays[0].shape
    zcount = lax.axis_size("fsdp")
    ccount = lax.axis_size("ctx")

    def body(*refs):
        out, sems = refs[8], refs[9]
        core, ctx = lax.axis_index("pipe"), lax.axis_index("ctx")
        copies = []
        for number in range(8):
            half = core if number < 4 else 1 - core
            mask = 0
            if number % 2 == 1:
                mask = mask ^ (1 + half)
            if number % 4 >= 2:
                mask = mask ^ (2 - half)
            col = pl.multiple_of((ctx ^ mask) * cols, cols)
            for slot in range(depth):
                copies.append(
                    pltpu.make_async_copy(
                        refs[number].at[slot],
                        out.at[group.slot(slot), half, :, pl.ds(col, cols)],
                        sems.at[len(copies)],
                    )
                )
        for copy in copies:
            copy.start()
        for copy in copies:
            copy.wait()

    out = pl.pallas_call(
        body,
        out_shape=jax.ShapeDtypeStruct((zcount, 2, rows, ccount * cols), BF16),
        in_specs=[pl.BlockSpec(memory_space=pl.ANY)] * 8,
        out_specs=pl.BlockSpec(memory_space=pltpu.VMEM),
        scratch_shapes=[pltpu.SemaphoreType.DMA((8 * depth,))],
        compiler_params=pltpu.CompilerParams(vmem_limit_bytes=40 * 1024 * 1024),
        cost_estimate=pl.CostEstimate(flops=0, bytes_accessed=0, transcendentals=0),
    )(*arrays)
    return out.reshape(-1, out.shape[-1])


def first_side(half, ctx):
    return pick(half == 0, ctx % 2, ctx // 2)


class Down:
    def __init__(self, order, piece):
        self.order = order
        self.flight = lax.all_gather(order.hold(piece), "fsdp", axis=0, tiled=False)

    def start(self):
        self.near = self.order.wait(self.flight)
        self.flight = first_way(self.near)
        self.near_other = swap_cores(self.near)

    def finish(self):
        far = self.order.wait(self.flight)
        return [self.near, far, self.near_other, swap_cores(far)]


class Ffn:
    def __init__(self, group, down):
        self.group = group
        self.arrays = group.arrays() + down
        self.depth, self.rows, self.cols = self.arrays[0].shape

    def scratch(self, rows):
        return [
            pltpu.VMEM((4, 2, self.depth * self.rows, self.cols), BF16),
            pltpu.VMEM((4, 2, 2, *self.arrays[8].shape[1:]), BF16),
            pltpu.SemaphoreType.DMA((4, 2 * self.depth)),
            pltpu.SemaphoreType.DMA((16,)),
            pltpu.VMEM((rows, self.arrays[8].shape[2]), F32),
        ]

    def start(self, refs, held, down, sems, down_sems):
        core, ctx = lax.axis_index("pipe"), lax.axis_index("ctx")
        blocks, quarters = [], []
        for number in range(4):
            copies = []
            other = 4 + (0, 2, 1, 3)[number]
            for side, half in ((number, core), (other, 1 - core)):
                for slot in range(self.depth):
                    row = pl.multiple_of(self.group.slot(slot) * self.rows, 16)
                    copies.append(
                        pltpu.make_async_copy(
                            refs[side].at[slot],
                            held.at[number, half, pl.ds(row, self.rows), :],
                            sems.at[number, len(copies)],
                        )
                    )
            blocks.append(copies)
            mask = (0, 1 + core, 2 - core, 3)[number]
            quarters.append(ctx ^ mask)
        downs = []
        for side, half in ((8, core), (9, core), (10, 1 - core), (11, 1 - core)):
            near = first_side(half, ctx)
            for zed in range(4):
                downs.append(
                    pltpu.make_async_copy(
                        refs[side].at[zed],
                        down.at[zed, half, near if side % 2 == 0 else 1 - near],
                        down_sems.at[len(downs)],
                    )
                )
        for copy in blocks[0] + downs + blocks[1] + blocks[2] + blocks[3]:
            copy.start()
        return blocks, quarters, downs

    def call(self, body, outs, *args):
        return pl.pallas_call(
            body,
            out_shape=outs,
            in_specs=[pl.BlockSpec(memory_space=pltpu.VMEM)] * len(args)
            + [pl.BlockSpec(memory_space=pl.ANY)] * 12,
            out_specs=[pl.BlockSpec(memory_space=pltpu.VMEM)] * len(outs),
            scratch_shapes=self.scratch(args[0].shape[0]),
            compiler_params=pltpu.CompilerParams(vmem_limit_bytes=48 * 1024 * 1024),
            cost_estimate=pl.CostEstimate(flops=0, bytes_accessed=0, transcendentals=0),
        )(*args, *self.arrays)

    def forward(self, resid, gain):
        rows, width = resid.shape
        cols = self.cols
        ffn = 4 * cols

        def body(r_ref, gain_ref, *refs):
            low_ref, normed_ref, gate_ref, up_ref, hidden_ref = refs[12:17]
            held, down, total = refs[17], refs[18], refs[21]
            blocks, quarters, downs = self.start(refs[:12], *refs[17:21])
            resid = r_ref[...]
            normed = normalize(resid, gain_ref[...]).astype(BF16)
            normed_ref[...] = normed.T
            total[...] = resid
            for number in range(4):
                for copy in blocks[number]:
                    copy.wait()
                gate = dot(normed, held[number, 0])
                up = dot(normed, held[number, 1])
                hidden = (gate / (1.0 + jnp.exp(-gate)) * up).astype(BF16)
                place = pl.ds(pl.multiple_of(quarters[number] * cols, cols), cols)
                gate_ref[:, place] = gate
                up_ref[:, place] = up
                hidden_ref[place, :] = hidden.T
                if number == 0:
                    for copy in downs:
                        copy.wait()
                weights = down[quarters[number]].reshape(cols, width)
                total[...] += dot(hidden, weights)
            low_ref[...] = total[...].astype(BF16)

        return self.call(
            body,
            [
                jax.ShapeDtypeStruct((rows, width), BF16),
                jax.ShapeDtypeStruct((width, rows), BF16),
                jax.ShapeDtypeStruct((rows, ffn), F32),
                jax.ShapeDtypeStruct((rows, ffn), F32),
                jax.ShapeDtypeStruct((ffn, rows), BF16),
            ],
            resid,
            gain[None],
        )

    def backward(self, grad_low, resid, gain, gate, up):
        rows, width = resid.shape
        cols = self.cols
        ffn = 4 * cols

        def body(grad_ref, r_ref, gain_ref, gate_ref, up_ref, *refs):
            out_ref, gain_out, gate_out, up_out, total = *refs[12:16], refs[20]
            held, down = refs[16:18]
            blocks, quarters, downs = self.start(refs[:12], *refs[16:20])
            grad = grad_ref[...]
            for number in range(4):
                place = pl.ds(pl.multiple_of(quarters[number] * cols, cols), cols)
                if number == 0:
                    for copy in downs:
                        copy.wait()
                weights = down[quarters[number]].reshape(cols, width)
                hidden_grad = dot_back(grad, weights)
                gate, up = gate_ref[:, place], up_ref[:, place]
                sig = 1.0 / (1.0 + jnp.exp(-gate))
                gate_grad = (hidden_grad * up * (sig * (1.0 + gate * (1.0 - sig)))).astype(BF16)
                up_grad = (hidden_grad * (gate * sig)).astype(BF16)
                own, other = two_ways(gate_grad, up_grad)
                gate_out[:, place] = own
                up_out[:, place] = other
                for copy in blocks[number]:
                    copy.wait()
                part = dot_back(gate_grad, held[number, 0]) + dot_back(up_grad, held[number, 1])
                if number == 0:
                    total[...] = part
                else:
                    total[...] += part
            resid_part, gain_grad = normalize_back(r_ref[...], gain_ref[...], total[...])
            out_ref[...] = grad.astype(F32) + resid_part
            gain_out[...] = gain_grad[None]

        outs = self.call(
            body,
            [
                jax.ShapeDtypeStruct((rows, width), F32),
                jax.ShapeDtypeStruct((1, width), F32),
                jax.ShapeDtypeStruct((rows, ffn), BF16),
                jax.ShapeDtypeStruct((rows, ffn), BF16),
            ],
            grad_low,
            resid,
            gain[None],
            gate,
            up,
        )
        return outs[0], outs[1][0], outs[2], outs[3]

    def both(self, resid, gain, grad_low):
        rows, width = resid.shape
        cols = self.cols
        ffn = 4 * cols

        def body(r_ref, gain_ref, grad_ref, *refs):
            low_ref, normed_ref, hidden_ref, out_ref, gain_out, own_ref, send_ref = refs[12:19]
            held, down, total = refs[19], refs[20], refs[23]
            blocks, quarters, downs = self.start(refs[:12], *refs[19:23])
            resid = r_ref[...]
            grad = grad_ref[...]
            normed = normalize(resid, gain_ref[...]).astype(BF16)
            normed_ref[...] = normed.T
            total[...] = resid
            normed_grad = jnp.zeros((rows, width), F32)
            for number in range(4):
                for copy in blocks[number]:
                    copy.wait()
                gate = dot(normed, held[number, 0])
                up = dot(normed, held[number, 1])
                sig = 1.0 / (1.0 + jnp.exp(-gate))
                act = gate / (1.0 + jnp.exp(-gate))
                hidden = (act * up).astype(BF16)
                place = pl.ds(pl.multiple_of(quarters[number] * cols, cols), cols)
                hidden_ref[place, :] = hidden.T
                if number == 0:
                    for copy in downs:
                        copy.wait()
                weights = down[quarters[number]].reshape(cols, width)
                total[...] += dot(hidden, weights)
                hidden_grad = dot_back(grad, weights)
                gate_grad = (hidden_grad * up * (sig * (1.0 + gate * (1.0 - sig)))).astype(BF16)
                up_grad = (hidden_grad * act).astype(BF16)
                own_ref[:, place], send_ref[:, place] = two_ways(gate_grad, up_grad)
                part = dot_back(gate_grad, held[number, 0]) + dot_back(up_grad, held[number, 1])
                normed_grad = normed_grad + part
            low_ref[...] = total[...].astype(BF16)
            resid_part, gain_grad = normalize_back(r_ref[...], gain_ref[...], normed_grad)
            out_ref[...] = grad.astype(F32) + resid_part
            gain_out[...] = gain_grad[None]

        outs = self.call(
            body,
            [
                jax.ShapeDtypeStruct((rows, width), BF16),
                jax.ShapeDtypeStruct((width, rows), BF16),
                jax.ShapeDtypeStruct((ffn, rows), BF16),
                jax.ShapeDtypeStruct((rows, width), F32),
                jax.ShapeDtypeStruct((1, width), F32),
                jax.ShapeDtypeStruct((rows, ffn), BF16),
                jax.ShapeDtypeStruct((rows, ffn), BF16),
            ],
            resid,
            gain[None],
            grad_low,
        )
        return outs[:3], (outs[3], outs[4][0], outs[5], outs[6])


class WholeFfn:
    def __init__(self, w_gateup, w_down, layer):
        core = lax.axis_index("pipe")
        whole = []
        for array in (w_gateup, w_down):
            mine = lax.all_gather(array, "fsdp", axis=0, tiled=True)
            whole.append(pick(core == layer, mine, swap_cores(mine)))
        self.w_gateup, self.w_down = whole

    def forward(self, resid, gain):
        normed = normalize(resid, gain).astype(BF16)
        gated = dot(normed, self.w_gateup)
        ffn = gated.shape[1] // 2
        gate, up = gated[:, :ffn], gated[:, ffn:]
        hidden = (gate / (1.0 + jnp.exp(-gate)) * up).astype(BF16)
        outputs = (resid + dot(hidden, self.w_down)).astype(BF16)
        return outputs, normed.T, gate, up, hidden.T

    def both(self, resid, gain, grad_low):
        outputs, normed, gate, up, hidden = self.forward(resid, gain)
        return (outputs, normed, hidden), self.backward(grad_low, resid, gain, gate, up)

    def backward(self, grad_low, resid, gain, gate, up):
        ffn = gate.shape[1]
        hidden_grad = dot_back(grad_low, self.w_down)
        sig = 1.0 / (1.0 + jnp.exp(-gate))
        gate_grad = (hidden_grad * up * (sig * (1.0 + gate * (1.0 - sig)))).astype(BF16)
        up_grad = (hidden_grad * (gate * sig)).astype(BF16)
        normed_grad = dot_back(gate_grad, self.w_gateup[:, :ffn]) + dot_back(
            up_grad, self.w_gateup[:, ffn:]
        )
        resid_part, gain_grad = normalize_back(resid, gain, normed_grad)
        own, other = two_ways(gate_grad, up_grad)
        return grad_low.astype(F32) + resid_part, gain_grad, own, other


def own_pieces(w_query, w_keyval, w_out, w_gateup, w_down, core, ctx):
    sources = (w_keyval, w_query, w_out)
    rows = w_query.shape[0] // 2
    cols = sum(source.shape[1] for source in sources) // 4
    ffn = w_gateup.shape[1] // 2
    depth = w_down.shape[0] // 2

    def quarter(number):
        found, place = [], 0
        for source in sources:
            start = max(number * cols - place, 0)
            stop = min((number + 1) * cols - place, source.shape[1])
            if start < stop:
                found.append(source[:, start:stop])
            place += source.shape[1]
        return found[0] if len(found) == 1 else jnp.concatenate(found, axis=1)

    attn = pick(
        ctx < 2, pick(ctx == 0, quarter(0), quarter(1)), pick(ctx == 2, quarter(2), quarter(3))
    )
    attn_parts = two_ways(attn[:rows], attn[rows:])

    def parts(half, attn_part):
        return (
            attn_part,
            lax.dynamic_slice(w_gateup, (0, half * ffn + ctx * cols), (2 * rows, cols)),
            lax.dynamic_slice_in_dim(
                w_down, half * depth + first_side(half, ctx) * (depth // 2), depth // 2, 0
            ),
        )

    kept = parts(core, attn_parts[0])
    received = [swap_cores(piece) for piece in parts(1 - core, attn_parts[1])]
    first = [pick(core == 0, a, b) for a, b in zip(kept, received)]
    second = [pick(core == 0, b, a) for a, b in zip(kept, received)]
    return first, second


def add_low(kept, received):
    return (kept.astype(F32) + received.astype(F32)).astype(BF16)


def term(*pairs, gains=None):
    rows = pairs[0][0].shape[0]
    deep = rows // 4
    widths = [pair[2].shape[1] if pair[4] else pair[2].shape[0] for pair in pairs]

    def body(*refs):
        sent_ref, kept_ref = refs[-2:]
        core, ctx = lax.axis_index("pipe"), lax.axis_index("ctx")
        y, x = ctx // 2, ctx % 2
        for out, xx, yy in ((sent_ref, 1 - x, 1 - y), (kept_ref, x, y)):
            for side in range(2):
                block = jnp.where(core == 0, xx + 2 * side, 2 * yy + side)
                place = pl.ds(pl.multiple_of(block * deep, 16), deep)
                offset = 0
                for number, pair in enumerate(pairs):
                    lefts = [ref[place, :] for ref in refs[4 * number : 4 * number + 2]]
                    rights = refs[4 * number + 2 : 4 * number + 4]
                    for start in range(0, widths[number], 640):
                        stop = min(start + 640, widths[number])
                        total = None
                        for left, right in zip(lefts, rights):
                            if pair[4]:
                                part = dot(left, right[:, start:stop])
                            else:
                                part = dot_back(left, right[start:stop, :])
                            total = part if total is None else total + part
                        out[side, :deep, offset + start : offset + stop] = total.astype(BF16)
                    offset += widths[number]
                if gains is not None:
                    out[side, deep:, :] = refs[-3][...]

    extra = []
    if gains is not None:
        low = gains.astype(BF16)
        extra = [jnp.pad(low, ((0, 16 - low.shape[0]), (0, sum(widths) - low.shape[1])))]
    shape = jax.ShapeDtypeStruct((2, deep + 16 * len(extra), sum(widths)), BF16)
    arrays = [array for pair in pairs for array in pair[:4]]
    return local_call(body, [shape, shape], *arrays, *extra)


class Reduce:
    def __init__(self, order, term, offload=False, extra=0):
        self.order = order
        self.extra = extra
        self.offload = offload
        core, ctx, self.zed = lax.axis_index("pipe"), lax.axis_index("ctx"), lax.axis_index("fsdp")
        self.side = pick(core == 0, ctx // 2, ctx % 2)
        self.step = 0
        self.result = None
        sent, kept = term
        self.kept = [kept]
        self.flights = [first_way(sent)]

    def land(self):
        parts = self.kept + [self.order.wait(flight) for flight in self.flights]
        return sum(part.astype(F32) for part in parts)

    def advance(self):
        if self.result is not None:
            return
        index = lax.dynamic_index_in_dim
        self.step += 1
        if self.step == 1:
            parts = self.kept + [self.order.wait(flight) for flight in self.flights]
            sent = sum(index(part, 1 - self.side, 0, False).astype(F32) for part in parts)
            self.kept = [index(part, self.side, 0, False) for part in parts]
            self.flights = [second_way(self.order.wait(sent.astype(BF16)))]
            return
        total = self.land()
        if self.step == 4:
            self.result = total
            return
        low = total.astype(BF16)
        if self.step == 3:
            sent = self.order.wait(index(low, 1 - self.high_bit, 0, False))
            self.kept = [index(low, self.high_bit, 0, False)]
            self.flights = [across(sent, "fsdp", 2)]
            return
        if self.offload:
            count = lax.axis_size("fsdp")
            parts = low.reshape(count, low.shape[0] // count, low.shape[1])
            parts = self.order.wait(parts)
            self.result = lax.psum_scatter(parts, "fsdp", scatter_dimension=0, tiled=False)
            return
        deep = low.shape[0] - self.extra
        body, tail = low[:deep], low[deep:]
        for mask in z_masks()[:-2]:
            half = body.shape[0] // 2
            high = (self.zed & mask) != 0
            self.kept = [jnp.concatenate([pick(high, body[half:], body[:half]), tail], axis=0)]
            sent = jnp.concatenate([pick(high, body[:half], body[half:]), tail], axis=0)
            self.flights = [across(sent, "fsdp", mask)]
            low = self.land().astype(BF16)
            body, tail = low[:half], low[half:]
        parts = body.reshape(4, body.shape[0] // 4, body.shape[1])
        if self.extra:
            tails = jnp.broadcast_to(tail, (4, *tail.shape))
            parts = jnp.concatenate([parts, tails], axis=1)
        low_bit, self.high_bit = self.zed % 2, self.zed % 4 // 2
        pairs = parts.reshape(2, 2, *parts.shape[1:])
        sent = self.order.wait(index(pairs, 1 - low_bit, 1, False))
        self.kept = [index(pairs, low_bit, 1, False)]
        self.flights = [across(sent, "fsdp", 1)]

    def settle(self):
        self.result = self.order.wait(self.result)


def send_keys(keyval):
    flows = []
    for mask in (3, 1, 2):
        flows.append(across(keyval, "ctx", mask))
    return flows[1], flows[2], flows[0]


def return_keys(parts):
    return [across(part, "ctx", mask) for part, mask in zip(parts, (1, 2, 3))]


def local_call(kernel, outs, *args):
    return pl.pallas_call(
        kernel,
        out_shape=outs,
        in_specs=[pl.BlockSpec(memory_space=pltpu.VMEM)] * len(args),
        out_specs=[pl.BlockSpec(memory_space=pltpu.VMEM)] * len(outs),
        compiler_params=pltpu.CompilerParams(vmem_limit_bytes=48 * 1024 * 1024),
        cost_estimate=pl.CostEstimate(flops=0, bytes_accessed=0, transcendentals=0),
    )(*args)


def project(inputs_low, w_attn, gain_attn, tables):
    rows, width = inputs_low.shape
    kv_width = (w_attn.shape[1] - 2 * width) // 2

    def body(x_ref, w_ref, gain_ref, cos_ref, sin_ref, normed_ref, q_ref, kv_ref):
        tables = cos_ref[...], sin_ref[...]
        normed = normalize(x_ref[...].astype(F32), gain_ref[...]).astype(BF16)
        normed_ref[...] = normed.T
        projected = dot(normed, w_ref[:, : 2 * kv_width + width]).T
        kv_ref[:kv_width, :] = rotate(projected[:kv_width], tables).astype(BF16)
        kv_ref[kv_width:, :] = projected[kv_width : 2 * kv_width].astype(BF16)
        queries = rotate(projected[2 * kv_width :], tables).astype(BF16)
        q_ref[...] = (queries.astype(F32) * SCALE).astype(BF16)

    return local_call(
        body,
        [
            jax.ShapeDtypeStruct((width, rows), BF16),
            jax.ShapeDtypeStruct((width, rows), BF16),
            jax.ShapeDtypeStruct((2 * kv_width, rows), BF16),
        ],
        inputs_low,
        w_attn,
        gain_attn[None],
        *tables,
    )


def head_rows(ref, head, offset=0):
    return ref[pl.ds(pl.multiple_of(head * HEAD + offset, HEAD), HEAD), :]


def attend_kernel(
    q_ref, p0, p1, p2, p3, bias_ref, x_ref, w_ref, normed_ref, own_ref, send_ref, lse_ref, r_ref, o_ref
):
    pieces = (p0, p1, p2, p3)
    count = q_ref.shape[1]
    kv_width = p0.shape[0] // 2
    ones = jnp.ones((16, count), BF16)

    def group(kv_head, carry):
        keys = [head_rows(p, kv_head).T for p in pieces]
        values = [
            jnp.concatenate([head_rows(p, kv_head, kv_width), ones], axis=0) for p in pieces
        ]
        for member in range(GROUPS):
            head = kv_head * GROUPS + member
            query = head_rows(q_ref, head)
            scores = [
                dot(keys[r], query) + bias_ref[r * count : (r + 1) * count, :] for r in range(4)
            ]
            top = jnp.maximum(
                jnp.maximum(scores[0], scores[1]), jnp.maximum(scores[2], scores[3])
            )
            top = jnp.max(top, axis=0, keepdims=True)
            total = jnp.zeros((HEAD + 16, count), F32)
            for r in range(4):
                total = total + dot(values[r], jnp.exp(scores[r] - top).astype(BF16))
            summed = total[HEAD : HEAD + 1]
            o_ref[pl.ds(pl.multiple_of(head * HEAD, HEAD), HEAD), :] = (
                total[:HEAD] / summed
            ).astype(BF16)
            lse_ref[head] = top + jnp.log(summed)
        return carry

    lax.fori_loop(0, KV_HEADS, group, 0)
    attended = o_ref[...]
    own_ref[...], send_ref[...] = two_ways(normed_ref[...], attended)
    width = attended.shape[0]
    r_ref[...] = x_ref[...].astype(F32) + dot(
        attended.T, w_ref[:, w_ref.shape[1] - width :]
    )


def scores_back_kernel(
    dr_ref,
    w_ref,
    q_ref,
    p0,
    p1,
    p2,
    p3,
    bias_ref,
    lse_ref,
    left_own_ref,
    left_send_ref,
    cos_ref,
    sin_ref,
    own_ref,
    send_ref,
    kv_own_ref,
    kv_x_ref,
    kv_y_ref,
    kv_xy_ref,
    do_ref,
    o_ref,
    dq_ref,
):
    tables = cos_ref[...], sin_ref[...]
    width = q_ref.shape[0]
    resid_low = dr_ref[...].astype(BF16)
    do_ref[...] = dot_back(w_ref[:, w_ref.shape[1] - width :], resid_low).astype(BF16)
    _, o_ref[...] = two_ways(left_own_ref[...], left_send_ref[...])
    pieces = (p0, p1, p2, p3)
    count = q_ref.shape[1]
    kv_width = p0.shape[0] // 2

    def group(kv_head, carry):
        keys_turned = [head_rows(p, kv_head) for p in pieces]
        keys = [k.T for k in keys_turned]
        values = [head_rows(p, kv_head, kv_width).T for p in pieces]
        key_grads = [jnp.zeros((HEAD, count), F32) for _ in range(4)]
        value_grads = [jnp.zeros((HEAD, count), F32) for _ in range(4)]
        for member in range(GROUPS):
            head = kv_head * GROUPS + member
            query = head_rows(q_ref, head)
            grad = head_rows(do_ref, head)
            delta = jnp.sum(
                grad.astype(F32) * head_rows(o_ref, head).astype(F32), axis=0, keepdims=True
            )
            log_total = lse_ref[head]
            query_grad = jnp.zeros((HEAD, count), F32)
            for r in range(4):
                scores = dot(keys[r], query) + bias_ref[r * count : (r + 1) * count, :]
                probs = jnp.exp(scores - log_total)
                prob_grad = dot(values[r], grad)
                score_low = (probs * (prob_grad - delta)).astype(BF16)
                value_grads[r] = value_grads[r] + dot_back(grad, probs.astype(BF16))
                key_grads[r] = key_grads[r] + dot_back(query, score_low)
                query_grad = query_grad + dot(keys_turned[r], score_low)
            dq_ref[pl.ds(pl.multiple_of(head * HEAD, HEAD), HEAD), :] = rotate_back(
                query_grad * SCALE, tables
            ).astype(BF16)
        start = pl.multiple_of(kv_head * HEAD, HEAD)
        for r, ref in enumerate((kv_own_ref, kv_x_ref, kv_y_ref, kv_xy_ref)):
            ref[pl.ds(start, HEAD), :] = key_grads[r].astype(ref.dtype)
            place = pl.ds(pl.multiple_of(start + kv_width, HEAD), HEAD)
            ref[place, :] = value_grads[r].astype(ref.dtype)
        return carry

    lax.fori_loop(0, KV_HEADS, group, 0)
    own_ref[...], send_ref[...] = two_ways(dq_ref[...], resid_low.T)


def attend(inputs_low, projected, pieces, w_attn, bias):
    normed, queries, _ = projected
    width, rows = queries.shape
    left_own, left_send, log_total, resid, _ = local_call(
        attend_kernel,
        [
            jax.ShapeDtypeStruct((width, rows), BF16),
            jax.ShapeDtypeStruct((width, rows), BF16),
            jax.ShapeDtypeStruct((HEADS, 1, rows), F32),
            jax.ShapeDtypeStruct((rows, width), F32),
            jax.ShapeDtypeStruct((width, rows), BF16),
        ],
        queries,
        *pieces,
        bias,
        inputs_low,
        w_attn,
        normed,
    )
    lefts = (left_own, swap_cores(left_send), normed, swap_cores(normed))
    return resid, (inputs_low, queries, pieces, log_total, left_own, left_send, lefts)


def backward_scores(resid_grad, saved, w_attn, bias, tables):
    _, queries, pieces, log_total, left_own, left_send, _ = saved
    width, rows = queries.shape
    keys = pieces[0].shape
    return local_call(
        scores_back_kernel,
        [
            jax.ShapeDtypeStruct((width, rows), BF16),
            jax.ShapeDtypeStruct((width, rows), BF16),
            jax.ShapeDtypeStruct(keys, F32),
            jax.ShapeDtypeStruct(keys, BF16),
            jax.ShapeDtypeStruct(keys, BF16),
            jax.ShapeDtypeStruct(keys, BF16),
            jax.ShapeDtypeStruct((width, rows), BF16),
            jax.ShapeDtypeStruct((width, rows), BF16),
            jax.ShapeDtypeStruct((width, rows), BF16),
        ],
        resid_grad,
        w_attn,
        queries,
        *pieces,
        bias,
        log_total,
        left_own,
        left_send,
        *tables,
    )[:6]


def backward_project(resid_grad, rights, kv_own, flows, saved, w_attn, gain_attn, tables):
    inputs_low = saved[0]
    rows, width = inputs_low.shape
    kv_width = kv_own.shape[0] // 2

    def body(
        dr_ref, own, send, kv0, kv1, kv2, kv3, x_ref, w_ref, gain_ref, cos_ref, sin_ref,
        low_ref, gain_out, thin_own, thin_send,
    ):
        tables = cos_ref[...], sin_ref[...]
        kv = kv0[...]
        for ref in (kv1, kv2, kv3):
            kv = kv + ref[...].astype(F32)
        keys = rotate_back(kv[:kv_width], tables).astype(BF16)
        values = kv[kv_width:].astype(BF16)
        queries, _ = two_ways(own[...], send[...])
        thin_own[...], thin_send[...] = two_ways(keys, values)
        projected = jnp.concatenate([keys, values, queries], axis=0).T
        normed_grad = dot_back(projected, w_ref[:, : 2 * kv_width + width])
        part, gain_grad = normalize_back(
            x_ref[...].astype(F32), gain_ref[...], normed_grad
        )
        low_ref[...] = (dr_ref[...] + part).astype(BF16)
        gain_out[...] = gain_grad[None]

    low, gain_grad, thin_own, thin_send = local_call(
        body,
        [
            jax.ShapeDtypeStruct((rows, width), BF16),
            jax.ShapeDtypeStruct((1, width), F32),
            jax.ShapeDtypeStruct((kv_width, rows), BF16),
            jax.ShapeDtypeStruct((kv_width, rows), BF16),
        ],
        resid_grad,
        *rights,
        kv_own,
        *flows,
        inputs_low,
        w_attn,
        gain_attn[None],
        *tables,
    )
    return low, gain_grad[0], thin_own, thin_send


def shards(
    tokens, cotangent, doc_ids, w_query, w_keyval, w_out, w_gateup, w_down, gain_attn, gain_ffn
):
    core = lax.axis_index("pipe")
    ctx = lax.axis_index("ctx")
    zed = lax.axis_index("fsdp")
    on_first = core == 0
    rows = tokens.shape[2]
    width = tokens.shape[3]
    length = doc_ids.shape[2]
    kv_width = w_keyval.shape[2] // 2

    pieces = own_pieces(
        w_query[0], w_keyval[0], w_out[0], w_gateup[0], w_down[0], core, ctx
    )
    gains = jnp.concatenate([gain_attn, gain_ffn], axis=0)
    gains_other = swap_cores(gains)
    layer_gains = (pick(on_first, gains, gains_other), pick(on_first, gains_other, gains))

    doc_row = lax.dynamic_index_in_dim(doc_ids[:, 0], core, 0, keepdims=False)
    inputs_low = lax.dynamic_index_in_dim(tokens[:, 0], core, 0, keepdims=False)
    cotangent_own = lax.dynamic_index_in_dim(cotangent[:, 0], core, 0, keepdims=False)
    earlier = jnp.sum((doc_row[None, :] < doc_row[:, None]).astype(jnp.int32), axis=1)
    positions = jnp.arange(length, dtype=jnp.int32) - earlier
    token_pos = lax.dynamic_slice_in_dim(positions, ctx * rows, rows, 0)
    tables = angle_tables(token_pos.astype(F32))
    own_docs = lax.dynamic_slice_in_dim(doc_row, ctx * rows, rows, 0)
    query_index = ctx * rows + jnp.arange(rows, dtype=jnp.int32)
    key_docs = []
    key_index = []
    for mask in range(4):
        key_docs.append(lax.dynamic_slice_in_dim(doc_row, (ctx ^ mask) * rows, rows, 0))
        key_index.append((ctx ^ mask) * rows + jnp.arange(rows, dtype=jnp.int32))
    key_docs = jnp.concatenate(key_docs)
    key_index = jnp.concatenate(key_index)
    seen = (own_docs[None, :] == key_docs[:, None]) & (
        key_index[:, None] <= query_index[None, :]
    )
    bias = jnp.where(seen, 0.0, NEGATIVE).astype(F32)

    order = Order()
    (attn_first, ffn_first, down_first), (attn_second, ffn_second, down_second) = pieces
    tiles = w_gateup.shape[1] % 16 == 0
    split = attn_first.shape[0]
    attn0 = Spread(order, attn_first)
    ffn_first, down_first = order.waits((ffn_first, down_first))
    if tiles:
        down0 = Down(order, down_first)
    attn0.flights[0] = order.wait(attn0.flights[0])
    if tiles:
        ffn0 = Spread(order, ffn_first)
    attn0.advance()
    attn0.advance()
    if tiles:
        ffn0.advance()
    second = order.hold(jnp.concatenate([attn_second, ffn_second], axis=0))
    second = lax.all_gather(second, "fsdp", axis=0, tiled=False)
    attn0.advance()
    w_attn0 = order.wait(place_attn(attn0))
    own0 = project(inputs_low, w_attn0, layer_gains[0][0], tables)
    keys0 = send_keys(own0[2])
    keyval0 = (own0[2], *[order.wait(flow) for flow in keys0])
    if tiles:
        ffn0.advance()
        down0.start()
    resid0, attn_saved0 = attend(inputs_low, own0, keyval0, w_attn0, bias)
    resid0 = order.wait(resid0)
    second = order.wait(second)
    attn1 = Spread.behind(order, second[:, :split])
    attn1.advance()
    if tiles:
        down1 = Down(order, down_second)
        ffn0.advance()
        weights0 = Ffn(ffn0, down0.finish())
    else:
        weights0 = WholeFfn(w_gateup[0], w_down[0], 0)
        weights1 = WholeFfn(w_gateup[0], w_down[0], 1)
    middle, *ffn_saved0 = weights0.forward(resid0, layer_gains[0][1])
    middle = order.wait(middle)
    attn1.advance()
    if tiles:
        ffn1 = Spread.behind(order, second[:, split:])
        ffn1.advance()
    attn1.advance()
    w_attn1 = order.wait(place_attn(attn1))
    own1 = project(middle, w_attn1, layer_gains[1][0], tables)
    keys1 = send_keys(own1[2])
    if tiles:
        ffn1.advance()
    keyval1 = (own1[2], *[order.wait(flow) for flow in keys1])
    if tiles:
        down1.start()
    resid1, attn_saved1 = attend(middle, own1, keyval1, w_attn1, bias)
    resid1 = order.wait(resid1)
    turned0 = [(array, order.wait(swap_cores(array))) for array in (ffn_saved0[0], ffn_saved0[3])]
    if tiles:
        ffn1.advance()
        weights1 = Ffn(ffn1, down1.finish())
    (outputs1, normed1, hidden1), back1 = weights1.both(
        resid1, layer_gains[1][1], cotangent_own
    )
    section_outs = [middle, outputs1]

    weights = [(w_attn0, weights0), (w_attn1, weights1)]
    saved = [(attn_saved0, (resid0, *ffn_saved0)), (attn_saved1, None)]
    half = -(-width // 256) * 128
    turned = [
        turned0,
        [(array, swap_cores(array)) for array in (normed1, hidden1)],
    ]

    grad_low = cotangent_own
    input_grads = [None, None]
    reduced = [None, None]
    gain_grads = [None, None]
    above = None
    for layer in (1, 0):
        w_attn, w_ffn = weights[layer]
        attn_saved, ffn_saved = saved[layer]
        normed, hidden = turned[layer]
        grad_low = order.wait(grad_low)
        own, send = two_ways(grad_low[:, :half], grad_low[:, width - half :])
        down = Reduce(order, order.waits(term((*hidden, own, swap_cores(send), True))), True)
        if layer == 1:
            resid_grad, gain_ffn_grad, own, send = back1
        else:
            resid_grad, gain_ffn_grad, own, send = w_ffn.backward(
                order.hold(grad_low),
                ffn_saved[0],
                layer_gains[layer][1],
                ffn_saved[2],
                ffn_saved[3],
            )
        resid_grad = order.wait(resid_grad)
        if layer == 0:
            above[1].advance()
            above[2].advance()
            above[0].settle()
            down.advance()
        *rights, kv_own, kv_x, kv_y, kv_xy = backward_scores(
            resid_grad, attn_saved, w_attn, bias, tables
        )
        kv_own = order.wait(kv_own)
        flows = return_keys(order.hold(kv_x, kv_y, kv_xy))
        gateup_term = order.waits(term((*normed, own, swap_cores(send), True)))
        if layer == 0:
            above[1].advance()
        flows = [order.wait(flow) for flow in flows]
        gateup = Reduce(order, order.hold(*gateup_term), True)
        if layer == 1:
            down.advance()
        grad_low, gain_attn_grad, own, send = backward_project(
            resid_grad, rights, kv_own, flows, attn_saved, w_attn, layer_gains[layer][0], tables
        )
        gain_grads[layer] = (gain_attn_grad, gain_ffn_grad)
        gains = None
        if layer == 0:
            grad_low = order.wait(grad_low)
            gains = jnp.stack([*gain_grads[0], *gain_grads[1]])
            gains = gains + swap_cores(gains)
            gains = pick(on_first, gains[:2], gains[2:])
        lefts = attn_saved[6]
        attn = Reduce(
            order,
            order.waits(
                term(
                    (*lefts[:2], rights[0], swap_cores(rights[1]), False),
                    (*lefts[2:], own, swap_cores(send), False),
                    gains=gains,
                )
            ),
            layer == 1,
            0 if gains is None else 16,
        )
        if layer == 1:
            down.advance()
            above = [down, gateup, attn]
        reduced[layer] = [down, gateup, attn]
        input_grads[layer] = grad_low

    above[2].advance()
    down.advance()
    above[1].settle()
    gateup.advance()

    def to_layers(first, second):
        own, other = two_ways(first, second)
        other = swap_cores(other)
        return two_ways(own, other)

    section_out = order.wait(jnp.stack(to_layers(section_outs[0], section_outs[1])))
    attn.advance()
    above[2].settle()
    gateup.advance()
    section_in_grad = order.wait(jnp.stack(to_layers(input_grads[0], input_grads[1])))
    attn.advance()
    attn.advance()
    down.settle()
    down_left, down_right = order.waits(to_layers(down.result, above[0].result))
    attn.advance()
    gain_total = attn.result[-16:-14, :width]
    attn_first, attn_second = to_layers(attn.result[:-16].astype(BF16), above[2].result)
    gateup.settle()
    gate, up = to_layers(gateup.result, above[1].result)
    attn_first, attn_second, gate, up, down_left, down_right = [
        array.astype(F32) for array in (attn_first, attn_second, gate, up, down_left, down_right)
    ]
    return (
        section_out[None, :, None],
        section_in_grad[None, :, None],
        attn_first[None, :, :width],
        jnp.concatenate([attn_first[:, width:], attn_second[:, width:]], axis=1)[None],
        attn_second[None, :, :width],
        jnp.concatenate([gate, up], axis=1)[None],
        jnp.concatenate(
            [down_left[:, : width // 2], down_right[:, half - width // 2 :]], axis=1
        )[None],
        gain_total[0][None],
        gain_total[1][None],
    )


def solution(mesh):
    return jax.shard_map(
        shards,
        mesh=mesh,
        in_specs=(
            P(None, "fsdp", "ctx", None),
            P(None, "fsdp", "ctx", None),
            P(None, "fsdp", None),
            P("pipe", "fsdp", None),
            P("pipe", "fsdp", None),
            P("pipe", "fsdp", None),
            P("pipe", "fsdp", None),
            P("pipe", "fsdp", None),
            P("pipe", None),
            P("pipe", None),
        ),
        out_specs=(
            P("pipe", None, "fsdp", "ctx", None),
            P("pipe", None, "fsdp", "ctx", None),
            P("pipe", ("ctx", "fsdp"), None),
            P("pipe", ("ctx", "fsdp"), None),
            P("pipe", ("ctx", "fsdp"), None),
            P("pipe", ("ctx", "fsdp"), None),
            P("pipe", ("ctx", "fsdp"), None),
            P("pipe", None),
            P("pipe", None),
        ),
        check_vma=False,
    )
```
